32 devices in a mesh: rep: 8 (over y, x, core), shard: 4 (over z).
Axes of the slice: x: 2, y: 2, z: 4, core: 2. Of those that a mesh axis runs over, the one named last changes fastest.
Arguments:
- tokens: bfloat16 [8192, 2048], P(('rep', 'shard')), may hold values from -6 to 6
- cotangent: bfloat16 [8192, 2048], P(('rep', 'shard')), may hold values from -6 to 6
- live_counts: int32 [8, 4], P('rep'), may hold values from 128 to 256, as said below
- routes: int32 [8192, 2], P(('rep', 'shard')), may hold values from 0 to 3, all different within a row
- norm_in: bfloat16 [2048], P('shard'), may hold values from 0.5 to 1.5
- w_query: bfloat16 [2048, 2048], P('shard'), may hold values from -0.125 to 0.125
- w_key: bfloat16 [2048, 2048], P('shard'), may hold values from -0.125 to 0.125
- w_value: bfloat16 [2048, 2048], P('shard'), may hold values from -0.125 to 0.125
- norm_query: bfloat16 [2048], P('shard'), may hold values from 0.5 to 1.5
- norm_key: bfloat16 [2048], P('shard'), may hold values from 0.5 to 1.5
- w_out: bfloat16 [2048, 2048], P('shard'), may hold values from -1 to 1
- norm_mid: bfloat16 [2048], P('shard'), may hold values from 0.5 to 1.5
- w_router: bfloat16 [2048, 4], P('shard'), may hold values from -0.09375 to 0.09375
- w_gate: bfloat16 [4, 2048, 1024], P(None, 'shard'), may hold values from -0.125 to 0.125
- w_up: bfloat16 [4, 2048, 1024], P(None, 'shard'), may hold values from -0.125 to 0.125
- w_down: bfloat16 [4, 1024, 2048], P(None, 'shard'), may hold values from -0.5 to 0.5
Outputs:
- output: bfloat16 [8192, 2048], P(('rep', 'shard'))
- input_grad: bfloat16 [8192, 2048], P(('rep', 'shard'))
- norm_in_grad: float32 [2048], P('shard')
- w_query_grad: float32 [2048, 2048], P('shard')
- w_key_grad: float32 [2048, 2048], P('shard')
- w_value_grad: float32 [2048, 2048], P('shard')
- norm_query_grad: float32 [2048], P('shard')
- norm_key_grad: float32 [2048], P('shard')
- w_out_grad: float32 [2048, 2048], P('shard')
- norm_mid_grad: float32 [2048], P('shard')
- w_router_grad: float32 [2048, 4], P('shard')
- w_gate_grad: float32 [4, 2048, 1024], P(None, 'shard')
- w_up_grad: float32 [4, 2048, 1024], P(None, 'shard')
- w_down_grad: float32 [4, 1024, 2048], P(None, 'shard')
The draws below stay inside these ranges and needn't reach their ends.
Inputs may be any that keep to these rules, and one draw needn't show every extreme that they name: Of a device's 256 rows, the first live_counts of them are live and the rest are unused; some device holds exactly 256 live rows and some exactly 128.
All inputs are finite; a program needn't handle non-finite values.
Results may differ from the reference program's by a relative error of at most 0.024.
Values may be sent and summed in bfloat16 or wider, within the bound.
No kernel may reach another device: no remote copies, remote signals or barrier semaphores. Data moves between devices by JAX's collectives and lax.ppermute only.
A program may use at most 512 MiB of HBM per device.

```python
import jax
import jax.numpy as jnp
from jax import lax

D = 2048
HEADS = 16
HEAD = 128
F = 1024
E = 4
TOP = 2
CAP = 256
LEAST = 128
ROWS = 8192
N_REP = 8
N_SHARD = 4


def draw_live_counts(key, part):
    key = jax.random.fold_in(key, 11)
    count_key, pick_key = jax.random.split(key)
    device_total = N_REP * N_SHARD
    counts = jax.random.randint(count_key, (device_total,), LEAST, CAP + 1)
    order = jax.random.permutation(pick_key, device_total)
    counts = counts.at[order[0]].set(CAP).at[order[1]].set(LEAST)
    return counts.reshape(N_REP, N_SHARD).astype(jnp.int32)


def block_levels(stream_key, extent, cuts, least, top_value):
    loudness = 1.0
    for position, parts in cuts:
        draws = jax.random.uniform(jax.random.fold_in(jax.random.fold_in(stream_key, 6), position), (parts,), jnp.float32, least / len(cuts), top_value / len(cuts))
        loudness = loudness * jnp.repeat(jnp.exp(draws), extent[position] // parts).reshape((-1,) + (1,) * (len(extent) - 1 - position))
    return loudness


def choose_distinct(key, rows, number_of, top, lift):
    ranking = jax.random.permutation(jax.random.fold_in(key, 1), number_of)
    favour = ranking
    for power in range(3):
        favour = favour * favour // number_of
    favour = favour * lift // number_of
    lots = jax.random.randint(jax.random.fold_in(key, 2), (rows, number_of), 0, 4096) + favour
    sure = jax.random.permutation(jax.random.fold_in(key, 3), rows)[jnp.arange(number_of) % rows]
    lots = jnp.where(jnp.arange(rows)[:, None] == sure[None, :], 1 << 14, lots)
    score = lots * number_of + jnp.arange(number_of)
    return lax.top_k(score.astype(jnp.int32), top)[1].astype(jnp.int32)


def centred(stream_key, shape, scale, most, cuts=(), held_as=jnp.bfloat16):
    factor_of = block_levels(stream_key, shape, cuts, -0.22, 0.18) if cuts else 1.0
    entries = jax.random.normal(stream_key, shape, jnp.float32) * scale * factor_of
    return jnp.minimum(jnp.maximum(entries, -most), most).astype(held_as)


def setup_inputs(seed: int = 0) -> dict:
    keys = jax.random.split(jax.random.key(seed), 17)
    return {
        "tokens": centred(keys[0], (ROWS, D), 1.0, 6.0, ((0, 32),)),
        "cotangent": centred(keys[1], (ROWS, D), 1.0, 6.0, ((0, 32),)),
        "live_counts": draw_live_counts(jax.random.fold_in(keys[16], 71), 0),
        "routes": choose_distinct(keys[3], ROWS, E, TOP, 4096),
        "norm_in": jnp.clip(1.0 + 0.1 * jax.random.normal(keys[4], (D,), jnp.float32), 0.5, 1.5).astype(jnp.bfloat16),
        "w_query": centred(keys[5], (D, D), D ** -0.5, 0.125, ((0, 4),)),
        "w_key": centred(keys[6], (D, D), D ** -0.5, 0.125, ((0, 4),)),
        "w_value": centred(keys[7], (D, D), D ** -0.5, 0.125, ((0, 4),)),
        "norm_query": jnp.clip(1.0 + 0.1 * jax.random.normal(keys[8], (D,), jnp.float32), 0.5, 1.5).astype(jnp.bfloat16),
        "norm_key": jnp.clip(1.0 + 0.1 * jax.random.normal(keys[9], (D,), jnp.float32), 0.5, 1.5).astype(jnp.bfloat16),
        "w_out": centred(keys[10], (D, D), (D // 64) ** -0.5, 1.0, ((0, 4),)),
        "norm_mid": jnp.clip(1.0 + 0.1 * jax.random.normal(keys[11], (D,), jnp.float32), 0.5, 1.5).astype(jnp.bfloat16),
        "w_router": centred(keys[12], (D, E), (2 * D) ** -0.5, 0.09375, ((0, 4),)),
        "w_gate": centred(keys[13], (E, D, F), D ** -0.5, 0.125, ((1, 4),)),
        "w_up": centred(keys[14], (E, D, F), D ** -0.5, 0.125, ((1, 4),)),
        "w_down": centred(keys[15], (E, F, D), (F // 8) ** -0.5, 0.5, ((1, 4),)),
    }


EPS = 1e-05
THETA = 10000.0
MASKED = -1e+30
HIGH = lax.Precision.HIGHEST

@jax.custom_vjp
def low(v):
    return lax.optimization_barrier(v.astype(jnp.bfloat16)).astype(jnp.float32)

@jax.custom_vjp
def low_back(v):
    return v

def low_keep(v):
    return (low(v), None)

def low_pass(kept, grad):
    return (grad,)

def back_keep(v):
    return (v, None)

def back_low(kept, grad):
    return (low(grad),)
low.defvjp(low_keep, low_pass)
low_back.defvjp(back_keep, back_low)

def matmul(left, right):
    return jnp.dot(left, right, precision=HIGH, preferred_element_type=jnp.float32)

def rms_norm(values, gain):
    return values * lax.rsqrt(lax.optimization_barrier(jnp.mean(values * values, axis=-1, keepdims=True)) + EPS) * gain

def angles(positions, head_size):
    half_size = head_size // 2
    frequency = THETA ** (-jnp.arange(half_size, dtype=jnp.float32) * 2.0 / head_size)
    phases = positions.astype(jnp.float32)[:, None] * frequency[None, :]
    phases = jnp.concatenate([phases, phases], axis=-1)
    return (jnp.cos(phases), jnp.sin(phases))

def rotate(values, cosine, sine):
    half_size = values.shape[-1] // 2
    turned = jnp.concatenate([-values[..., half_size:], values[..., :half_size]], axis=-1)
    return values * cosine[:, None, :] + turned * sine[:, None, :]

def attend(query_rot, key_rot, value_rot, limits, key_positions, key_live):
    total_rows = query_rot.shape[0]
    block_rows = 512 if total_rows % 512 == 0 else total_rows
    block_count = total_rows // block_rows
    inv_root = query_rot.shape[-1] ** (-0.5)

    def query_block(operands):
        block_query, block_limit = operands
        scores = jnp.einsum('qhd,khd->hqk', block_query, key_rot, precision=HIGH) * inv_root
        scores = low_back(scores)
        allowed = key_live[None, None, :] & (key_positions[None, None, :] <= block_limit[None, :, None])
        scores = jnp.where(allowed, scores, MASKED)
        peak = lax.optimization_barrier(jnp.max(scores, axis=-1, keepdims=True))
        expo = jnp.exp(scores - peak)
        probs = low(expo / lax.optimization_barrier(jnp.sum(expo, axis=-1, keepdims=True)))
        return jnp.einsum('hqk,khd->qhd', probs, value_rot, precision=HIGH)
    mixed = lax.map(jax.checkpoint(query_block), (query_rot.reshape((block_count, block_rows) + query_rot.shape[1:]), limits.reshape(block_count, block_rows)))
    return mixed.reshape(query_rot.shape)

def layer_forward(inputs, weights, live_row, group_routes):
    gain_in, query_w, key_w, value_w, gain_query, gain_key, out_w, gain_mid, router_w, gate_w, up_w, down_w = weights
    total_rows = inputs.shape[0]
    row_ids = jnp.arange(total_rows, dtype=jnp.int32)
    owner = (row_ids // CAP).astype(jnp.int32)
    local_ids = (row_ids % CAP).astype(jnp.int32)
    starts = (jnp.cumsum(live_row) - live_row).astype(jnp.int32)
    live = local_ids < live_row[owner]
    positions = (starts[owner] + local_ids).astype(jnp.int32)
    limits = jnp.where(live, positions, total_rows + CAP).astype(jnp.int32)
    normed = low(rms_norm(inputs, gain_in))
    query_lin = low_back(matmul(normed, query_w))
    key_lin = low_back(matmul(normed, key_w))
    value_lin = low(low_back(matmul(normed, value_w)))
    cosine, sine = angles(positions, HEAD)
    head_shape = (total_rows, HEADS, HEAD)
    query_rot = low(rotate(rms_norm(query_lin, gain_query).reshape(head_shape), cosine, sine))
    key_rot = low(rotate(rms_norm(key_lin, gain_key).reshape(head_shape), cosine, sine))
    mixed = attend(query_rot, key_rot, value_lin.reshape(head_shape), limits, positions, live).reshape(total_rows, D)
    mixed = low(low_back(mixed))
    residual = inputs + low_back(matmul(mixed, out_w))
    middle = low(rms_norm(residual, gain_mid))
    logits = low_back(matmul(middle, router_w))
    peak = lax.optimization_barrier(jnp.max(logits, axis=-1, keepdims=True))
    expo = jnp.exp(logits - peak)
    router_probs = expo / lax.optimization_barrier(jnp.sum(expo, axis=-1, keepdims=True))
    chosen = lax.optimization_barrier(jnp.sum((group_routes[:, :, None] == jnp.arange(E, dtype=jnp.int32)[None, None, :]).astype(jnp.float32), axis=1))
    mix = router_probs * chosen
    expert_sum = jnp.zeros_like(residual)
    for expert in range(E):
        gate_lin = low_back(matmul(middle, gate_w[expert]))
        up_lin = low_back(matmul(middle, up_w[expert]))
        activated = low(jax.nn.silu(gate_lin) * up_lin)
        expert_sum = expert_sum + mix[:, expert:expert + 1] * low_back(matmul(activated, down_w[expert]))
    return (residual + expert_sum) * live[:, None].astype(jnp.float32)

def reference(tokens, cotangent, live_counts, routes, norm_in, w_query, w_key, w_value, norm_query, norm_key, w_out, norm_mid, w_router, w_gate, w_up, w_down):
    params = tuple((item.astype(jnp.float32) for item in (norm_in, w_query, w_key, w_value, norm_query, norm_key, w_out, norm_mid, w_router, w_gate, w_up, w_down)))
    group_rows = CAP * N_SHARD
    inputs = tokens.astype(jnp.float32).reshape(N_REP, group_rows, D)
    upstream = cotangent.astype(jnp.float32).reshape(N_REP, group_rows, D)
    routed = routes.reshape(N_REP, group_rows, TOP)

    def group_step(totals, operands):
        group_in, group_up, group_live, group_routes = operands

        def forward(values, weights):
            return layer_forward(values, weights, group_live, group_routes)
        result, pull = jax.vjp(forward, group_in, params)
        input_grad, weight_grads = pull(group_up)
        totals = jax.tree.map(lambda left, right: left + right, totals, weight_grads)
        return (totals, (result.astype(jnp.bfloat16), input_grad.astype(jnp.bfloat16)))
    zeros = tuple((jnp.zeros_like(item) for item in params))
    totals, (results, input_grads) = lax.scan(group_step, zeros, (inputs, upstream, live_counts, routed))
    return (results.reshape(N_REP * group_rows, D), input_grads.reshape(N_REP * group_rows, D), totals[0], totals[1], totals[2], totals[3], totals[4], totals[5], totals[6], totals[7], totals[8], totals[9], totals[10], totals[11])
```

```python
import functools

import jax
import jax.numpy as jnp
from jax import lax
from jax.experimental import pallas as pl
from jax.experimental.pallas import tpu as pltpu
from jax.sharding import Mesh
from jax.sharding import PartitionSpec as P

HEADS = 16
EPS = 1e-05
THETA = 10000.0
MASKED = -1e30
FAR = 1 << 30
F32 = jnp.float32
BF16 = jnp.bfloat16
VMEM_BYTES = 56 * 1024 * 1024


def dot(left, right):
    return jnp.dot(left, right, preferred_element_type=F32)


def dot_nt(left, right):
    return lax.dot_general(left, right, (((1,), (1,)), ((), ())), preferred_element_type=F32)


def dot_tn(left, right):
    return lax.dot_general(left, right, (((0,), (0,)), ((), ())), preferred_element_type=F32)


def swap(value, axis, step):
    size = lax.axis_size(axis)
    return lax.ppermute(value, axis, [(i, i ^ step) for i in range(size)])


def exchange(parts, axis):
    me = lax.axis_index(axis)
    out = parts
    for step in range(1, lax.axis_size(axis)):
        sent = lax.dynamic_index_in_dim(parts, me ^ step, 0, keepdims=True)
        out = lax.dynamic_update_slice_in_dim(out, swap(sent, axis, step), me ^ step, 0)
    return out


def gather_chips(block):
    chips = lax.axis_size("chip")
    if chips != 4:
        return [block] + [swap(block, "chip", step) for step in range(1, chips)]
    half = block.shape[0] // 2
    one = swap(block, "chip", 1)
    two = swap(block, "chip", 2)
    top = swap(two[:half], "chip", 1)
    low = swap(one[half:], "chip", 2)
    return [block, one, two, jnp.concatenate([top, low], axis=0)]


def scatter_chips(own, others):
    chips = lax.axis_size("chip")
    if chips != 4:
        for step in range(1, chips):
            own = own + swap(others[step - 1], "chip", step).astype(F32)
        return own
    cut = own.shape[1] // 2
    one, two, three = others
    left = lambda v: v[:, :cut]
    right = lambda v: v[:, cut:]
    one_left = swap(left(one), "chip", 1)
    three_left = swap(left(three), "chip", 1)
    two_right = swap(right(two), "chip", 2)
    three_right = swap(right(three), "chip", 2)
    pass_left = (left(two).astype(F32) + three_left.astype(F32)).astype(BF16)
    pass_right = (right(one).astype(F32) + three_right.astype(F32)).astype(BF16)
    last_left = swap(pass_left, "chip", 2)
    last_right = swap(pass_right, "chip", 1)
    return jnp.concatenate(
        [
            left(own) + one_left.astype(F32) + last_left.astype(F32),
            right(own) + two_right.astype(F32) + last_right.astype(F32),
        ],
        axis=1,
    )


def sum_chips(value):
    step = 1
    while step < lax.axis_size("chip"):
        value = value + swap(value, "chip", step)
        step *= 2
    return value


def sum_rows(values):
    chips, shards = lax.axis_size("chip"), lax.axis_size("shard")
    total = values.reshape(values.shape[0], shards, chips, -1)
    step = 1
    while step < chips:
        other = swap(total, "chip", step)
        total = total + jnp.concatenate([other[:, :, i ^ step : (i ^ step) + 1] for i in range(chips)], axis=2)
        step *= 2
    return total.reshape(values.shape)


def rehome(rows):
    chips = lax.axis_size("chip")
    parts = rows.reshape(chips, rows.shape[0] // chips, rows.shape[1])
    return exchange(exchange(parts, "chip"), "shard").reshape(rows.shape)


def send_home(rows):
    shards = lax.axis_size("shard")
    parts = rows.reshape(shards, rows.shape[0] // shards, rows.shape[1])
    return exchange(exchange(parts, "shard"), "chip").reshape(rows.shape)


def lane_roll(values):
    return pltpu.roll(values, values.shape[1] // 2, 1)


def attend_forward(
    block_rows, scale,
    query_ref, key_ref, value_ref, inv_ref, gain_query_ref, gain_key_ref, cos_ref, sin_ref, pos_ref, key_pos_ref,
    mixed_ref, query_rot_ref, key_rot_ref, value_low_ref, lse_ref,
):
    cosine, sine = cos_ref[...], sin_ref[...]
    query = query_ref[...] * inv_ref[:, 0:1] * gain_query_ref[...]
    query_rot_ref[...] = (query * cosine + lane_roll(query) * sine).astype(BF16)
    key = key_ref[...] * inv_ref[:, 1:2] * gain_key_ref[...]
    key_rot_ref[...] = (key * cosine + lane_roll(key) * sine).astype(BF16)
    value_low_ref[...] = value_ref[...].astype(BF16)
    for block in range(query_ref.shape[0] // block_rows):
        rows = pl.ds(block * block_rows, block_rows)
        seen = pl.ds(0, (block + 1) * block_rows)
        scores = dot_nt(query_rot_ref[rows, :], key_rot_ref[seen, :]) * scale
        scores = jnp.where(key_pos_ref[:, seen] <= pos_ref[rows, :], scores, MASKED)
        peak = jnp.max(scores, axis=-1, keepdims=True)
        expo = jnp.exp(scores - peak)
        total = jnp.sum(expo, axis=-1, keepdims=True)
        probs_low = (expo * (1.0 / total)).astype(BF16)
        mixed_ref[rows, :] = dot(probs_low, value_low_ref[seen, :]).astype(BF16)
        lse_ref[rows, :] = jnp.broadcast_to(peak + jnp.log(total), (block_rows, lse_ref.shape[1]))


def attend_backward(
    block_rows, scale,
    query_rot_ref, key_rot_ref, value_low_ref, lse_ref, grad_ref, cos_ref, sin_ref, pos_ref, key_pos_ref,
    query_back_ref, key_back_ref, value_back_ref, key_sum, value_sum,
):
    cosine, sine = cos_ref[...], sin_ref[...]
    key_sum[...] = jnp.zeros_like(key_sum)
    value_sum[...] = jnp.zeros_like(value_sum)
    for block in range(query_rot_ref.shape[0] // block_rows):
        rows = pl.ds(block * block_rows, block_rows)
        seen = pl.ds(0, (block + 1) * block_rows)
        query = query_rot_ref[rows, :]
        grad = grad_ref[rows, :]
        scores = dot_nt(query, key_rot_ref[seen, :]) * scale
        scores = jnp.where(key_pos_ref[:, seen] <= pos_ref[rows, :], scores, MASKED)
        probs = jnp.exp(scores - lse_ref[rows, 0:1])
        probs_grad = dot_nt(grad, value_low_ref[seen, :])
        weighted = jnp.sum(probs * probs_grad, axis=-1, keepdims=True)
        score_grad = (probs * (probs_grad - weighted)).astype(BF16)
        query_grad = dot(score_grad, key_rot_ref[seen, :]) * scale
        query_back_ref[rows, :] = query_grad * cosine[block * block_rows : (block + 1) * block_rows] - lane_roll(
            query_grad
        ) * sine[block * block_rows : (block + 1) * block_rows]
        key_sum[seen, :] += dot_tn(score_grad, query)
        value_sum[seen, :] += dot_tn(probs.astype(BF16), grad)
    key_grad = key_sum[...] * scale
    key_back_ref[...] = key_grad * cosine - lane_roll(key_grad) * sine
    value_back_ref[...] = value_sum[...].astype(BF16)


def attention_specs(rows, head_size, heads):
    column = lambda index: pl.BlockSpec((rows, head_size), index)
    whole = lambda shape: pl.BlockSpec(shape, lambda h: (0, 0))
    half = heads // 2
    part = lambda which: (lambda h: (0, (h // half) * 3 * half + which * half + h % half))
    plain = lambda h: (0, h)
    return column, whole, part, plain


def run_attend_forward(qkv, inv, gain_query, gain_key, cosine, sine, pos, key_pos, heads, head_size, block_rows):
    rows = qkv.shape[0]
    column, whole, part, plain = attention_specs(rows, head_size, heads)
    gain = pl.BlockSpec((1, head_size), plain)
    wide = heads * head_size
    low = jax.ShapeDtypeStruct((rows, wide), BF16)
    return pl.pallas_call(
        functools.partial(attend_forward, block_rows, head_size**-0.5),
        grid=(heads,),
        in_specs=[
            column(part(0)), column(part(1)), column(part(2)), whole(inv.shape), gain, gain,
            whole(cosine.shape), whole(sine.shape), whole(pos.shape), whole(key_pos.shape),
        ],
        out_specs=[column(plain)] * 5,
        out_shape=[low, low, low, low, jax.ShapeDtypeStruct((rows, wide), F32)],
        compiler_params=pltpu.CompilerParams(vmem_limit_bytes=VMEM_BYTES),
        cost_estimate=pl.CostEstimate(
            flops=4 * rows * rows * wide * 5 // 8, bytes_accessed=rows * wide * 24, transcendentals=rows * rows * heads * 5 // 8
        ),
        name="attend_forward",
    )(qkv, qkv, qkv, inv, gain_query, gain_key, cosine, sine, pos, key_pos)


def run_attend_backward(query_rot, key_rot, value_low, lse, grad, cosine, sine, pos, key_pos, heads, head_size, block_rows):
    rows = query_rot.shape[0]
    column, whole, _, plain = attention_specs(rows, head_size, heads)
    wide = heads * head_size
    full = jax.ShapeDtypeStruct((rows, wide), F32)
    return pl.pallas_call(
        functools.partial(attend_backward, block_rows, head_size**-0.5),
        grid=(heads,),
        in_specs=[column(plain)] * 5 + [whole(cosine.shape), whole(sine.shape), whole(pos.shape), whole(key_pos.shape)],
        out_specs=[column(plain)] * 3,
        out_shape=[full, full, jax.ShapeDtypeStruct((rows, wide), BF16)],
        scratch_shapes=[pltpu.VMEM((rows, head_size), F32)] * 2,
        compiler_params=pltpu.CompilerParams(vmem_limit_bytes=VMEM_BYTES),
        cost_estimate=pl.CostEstimate(
            flops=10 * rows * rows * wide * 5 // 8, bytes_accessed=rows * wide * 24, transcendentals=rows * rows * heads * 5 // 8
        ),
        name="attend_backward",
    )(query_rot, key_rot, value_low, lse, grad, cosine, sine, pos, key_pos)


def experts_middle(experts, width, lin_ref, back_ref, mix_ref, act_ref, grad_ref, mix_grad_ref):
    half = experts * width
    columns = []
    for expert in range(experts):
        mix = mix_ref[:, expert : expert + 1]
        total = 0.0
        for core in range(2):
            at = expert * width
            gate_at, up_at, act_at = 2 * half * core + at, 2 * half * core + half + at, half * core + at
            gate = lin_ref[:, gate_at : gate_at + width]
            up = lin_ref[:, up_at : up_at + width]
            back = back_ref[:, act_at : act_at + width]
            sigma = 1.0 / (1.0 + jnp.exp(-gate))
            silu = gate * sigma
            act = silu * up
            total = total + jnp.sum(act * back, axis=-1, keepdims=True)
            back = back * mix
            act_ref[:, act_at : act_at + width] = (act * mix).astype(BF16)
            grad_ref[:, gate_at : gate_at + width] = (back * up * sigma * (1.0 + gate * (1.0 - sigma))).astype(BF16)
            grad_ref[:, up_at : up_at + width] = (back * silu).astype(BF16)
        columns.append(total)
    mix_grad_ref[...] = jnp.concatenate(columns, axis=1)


def run_experts_middle(lin, back, mix, experts, width):
    rows = lin.shape[0]
    tile = min(rows, 256)
    spec = lambda cols: pl.BlockSpec((tile, cols), lambda i: (i, 0))
    return pl.pallas_call(
        functools.partial(experts_middle, experts, width),
        grid=(rows // tile,),
        in_specs=[spec(lin.shape[1]), spec(back.shape[1]), spec(experts)],
        out_specs=[spec(back.shape[1]), spec(lin.shape[1]), spec(experts)],
        out_shape=[
            jax.ShapeDtypeStruct(back.shape, BF16),
            jax.ShapeDtypeStruct(lin.shape, BF16),
            jax.ShapeDtypeStruct((rows, experts), F32),
        ],
        compiler_params=pltpu.CompilerParams(vmem_limit_bytes=VMEM_BYTES),
        cost_estimate=pl.CostEstimate(
            flops=20 * lin.size, bytes_accessed=6 * lin.size + 6 * back.size, transcendentals=lin.size
        ),
        name="experts_middle",
    )(lin, back, mix)


def part_owners(where_ref, chips):
    return [(where_ref[0] ^ step, where_ref[1] ^ turn) for turn in range(2) for step in range(chips)]


def place_heads(chips, half_heads, head_size, where_ref, *refs):
    parts, outs = refs[: 2 * chips], refs[2 * chips :]
    for part, (chip, core) in zip(parts, part_owners(where_ref, chips)):
        for which, out in enumerate(outs):
            for i in range(half_heads):
                first = (which * half_heads + i) * head_size
                column = pl.multiple_of(((core * half_heads + i) * chips + chip) * head_size, head_size)
                out[:, pl.ds(column, head_size)] = part[:, first : first + head_size].astype(F32)


def place_hidden(chips, experts, width, where_ref, *refs):
    parts, order, outs = refs[: 2 * chips], refs[2 * chips], refs[2 * chips + 1 :]
    for which, out in enumerate(outs):
        for expert in range(experts):
            first = (which * experts + expert) * width
            row = jnp.concatenate([part[:, first : first + width] for part in parts], axis=1)
            out[expert] = dot(row, order[...])


def place_rows(chips, where_ref, *refs):
    parts, out = refs[: 2 * chips], refs[-1]
    height = parts[0].shape[0]
    for part, (chip, core) in zip(parts, part_owners(where_ref, chips)):
        row = pl.multiple_of((2 * chip + core) * height, height)
        out[0, pl.ds(row, height), :] = part[...].astype(F32)


def place_blocks(chips, where_ref, *refs):
    parts, out = refs[: 2 * chips], refs[-1]
    wide = parts[0].shape[1]
    for part, (chip, core) in zip(parts, part_owners(where_ref, chips)):
        out[chip, :, pl.ds(pl.multiple_of(core * wide, wide), wide)] = part[...].astype(F32)


def place(kernel, where, parts, part_block, out_shapes, out_block, grid, name, extra=()):
    moved = sum(p.size * 2 for p in parts) + sum(o.size * 4 for o in out_shapes)
    return pl.pallas_call(
        kernel,
        grid_spec=pltpu.PrefetchScalarGridSpec(
            num_scalar_prefetch=1,
            grid=grid,
            in_specs=[pl.BlockSpec(*part_block)] * len(parts)
            + [pl.BlockSpec(v.shape, lambda i, where: (0, 0)) for v in extra],
            out_specs=[pl.BlockSpec(*out_block)] * len(out_shapes),
        ),
        out_shape=out_shapes,
        compiler_params=pltpu.CompilerParams(vmem_limit_bytes=VMEM_BYTES),
        cost_estimate=pl.CostEstimate(flops=0, bytes_accessed=moved, transcendentals=0),
        name=name,
    )(where, *parts, *extra)


def norm_stats(values):
    inv_root = lax.rsqrt(jnp.mean(values * values, axis=-1, keepdims=True) + EPS)
    return (inv_root, values * inv_root)


def norm_back(gradient, unit_rows, inv_root, gain):
    scaled = gain * gradient
    rows_part = inv_root * (scaled - unit_rows * jnp.mean(unit_rows * scaled, axis=-1, keepdims=True))
    return (rows_part, jnp.sum(gradient * unit_rows, axis=0))


def body(
    tokens, cotangent, live_counts, routes, norm_in, w_query, w_key, w_value, norm_query, norm_key, w_out, norm_mid,
    w_router, w_gate, w_up, w_down,
):
    chips, shards = lax.axis_size("chip"), lax.axis_size("shard")
    chip, core, shard = lax.axis_index("chip"), lax.axis_index("core"), lax.axis_index("shard")
    rows_here, width = tokens.shape
    head_size = width // HEADS
    heads = HEADS // chips
    half_heads = heads // 2
    experts = w_gate.shape[0]
    piece = rows_here // chips
    group_rows = rows_here * shards
    shard_rows = w_query.shape[0]
    shard_hidden, hidden = w_down.shape[1], w_gate.shape[2]
    own_hidden = shard_hidden // (2 * chips)
    part_hidden = own_hidden * shards
    half_heads_wide = half_heads * head_size
    first_core = core == 0

    def full_rows(pieces):
        stacked = [v.reshape(shards, 1, piece, v.shape[1]) for v in pieces]
        return jnp.concatenate(stacked, axis=1).reshape(group_rows, pieces[0].shape[1])

    def chip_rows(rows, step):
        split = rows.reshape(shards, chips, piece, rows.shape[1])
        return split[:, step].reshape(rows_here, rows.shape[1])

    def reduce_rows(partial):
        return scatter_chips(
            chip_rows(partial, 0), [chip_rows(partial, step).astype(BF16) for step in range(1, chips)]
        )

    with jax.named_scope("rehome_tokens"):
        inputs = rehome(tokens).astype(F32)
    with jax.named_scope("small_gathers"):
        small = jnp.concatenate(
            [v.astype(F32)[None] for v in (norm_in, norm_query, norm_key, norm_mid)] + [w_router.astype(F32).T], axis=0
        )
        small_all = exchange(jnp.broadcast_to(small[None], (shards,) + small.shape), "shard")
        small_all = small_all.transpose(1, 0, 2).reshape(small.shape[0], width)
        gain_in, gain_query, gain_key, gain_mid = (small_all[i] for i in range(4))
        router = small_all[4:].astype(BF16)
        counts = lax.ppermute(
            live_counts,
            ("chip", "core", "shard"),
            [
                ((i * 2 + k) * shards + j, (j * 2 + k) * shards + i)
                for i in range(chips)
                for k in range(2)
                for j in range(shards)
            ],
        )[0]

    half_head_ids = [(core * half_heads + i) * chips + chip for i in range(half_heads)]
    other_head_ids = [((1 - core) * half_heads + i) * chips + chip for i in range(half_heads)]
    head_ids = half_head_ids + other_head_ids

    with jax.named_scope("weights_qkv"):
        qkv_piece = jnp.concatenate(
            [
                lax.dynamic_slice_in_dim(w, head * head_size, head_size, 1)
                for w in (w_query, w_key, w_value)
                for head in half_head_ids
            ],
            axis=1,
        )
        qkv_own = lax.all_gather(qkv_piece, "shard", axis=0, tiled=True)
        qkv_full = jnp.concatenate([qkv_own, swap(qkv_own, "core", 1)], axis=1)
    heads_spread = HEADS // shards == chips
    with jax.named_scope("weights_out"):
        if heads_spread:
            out_piece = lax.dynamic_slice(w_out, (chip * head_size, core * (width // 2)), (head_size, width // 2))
            out_own = lax.all_gather(out_piece, "shard", axis=0, tiled=True)
            out_other = swap(out_own, "core", 1)
            out_full = jnp.concatenate(
                [jnp.where(first_core, out_own, out_other), jnp.where(first_core, out_other, out_own)], axis=1
            )
            top, low = out_full[:half_heads_wide], out_full[half_heads_wide:]
            out_full = jnp.concatenate([jnp.where(first_core, top, low), jnp.where(first_core, low, top)], axis=0)
        else:
            out_all = lax.all_gather(w_out, "shard", axis=0, tiled=True)
            out_full = jnp.concatenate(
                [lax.dynamic_slice_in_dim(out_all, head * head_size, head_size, 0) for head in head_ids], axis=0
            )
    hidden_at = (2 * chip + core) * own_hidden
    with jax.named_scope("weights_gate_up"):
        wanted = jnp.arange(part_hidden, dtype=jnp.int32)
        wanted = (wanted // own_hidden) * shard_hidden + hidden_at + wanted % own_hidden
        choose = (jnp.arange(hidden, dtype=jnp.int32)[:, None] == wanted[None, :]).astype(BF16)
        gate_up_piece = jnp.concatenate(
            [dot(w[expert], choose).astype(BF16) for w in (w_gate, w_up) for expert in range(experts)], axis=1
        )
        gate_up_own = lax.all_gather(gate_up_piece, "shard", axis=0, tiled=True)
        gate_up_full = jnp.concatenate([gate_up_own, swap(gate_up_own, "core", 1)], axis=1)
    with jax.named_scope("weights_down"):
        down_piece = lax.dynamic_slice_in_dim(w_down, hidden_at, own_hidden, 1)
        down_all = lax.all_gather(down_piece.reshape(experts * own_hidden, width), "shard", axis=0, tiled=True)
        down_own = (
            down_all.reshape(shards, experts, own_hidden, width).transpose(1, 0, 2, 3).reshape(experts * part_hidden, width)
        )
        down_full = jnp.concatenate([down_own, swap(down_own, "core", 1)], axis=0)

    starts = jnp.cumsum(counts) - counts
    chip_of = chip ^ jnp.arange(chips, dtype=jnp.int32)
    in_block = (chip_of[:, None] * piece + jnp.arange(piece, dtype=jnp.int32)[None, :]).reshape(1, rows_here)
    positions = (starts[:, None] + in_block).reshape(group_rows)
    live = (in_block < counts[:, None]).reshape(group_rows)
    live_float = live.astype(F32)
    live_own = live_float.reshape(shards, chips, piece)[:, 0].reshape(rows_here, 1)
    pos_column = positions[:, None]
    key_pos = jnp.where(live, positions, FAR)[None, :]
    half_size = head_size // 2
    frequency = THETA ** (-jnp.arange(half_size, dtype=F32) * 2.0 / head_size)
    phases = positions.astype(F32)[:, None] * frequency[None, :]
    cosine, sine = jnp.cos(phases), jnp.sin(phases)
    cosine = jnp.concatenate([cosine, cosine], axis=1)
    sine = jnp.concatenate([-sine, sine], axis=1)

    inv_in, unit_in = norm_stats(inputs)
    normed_own = (unit_in * gain_in).astype(BF16)
    with jax.named_scope("gather_normed"):
        normed = full_rows(gather_chips(normed_own))
    with jax.named_scope("rehome_cotangent"):
        route_columns = jnp.pad(routes.astype(BF16), ((0, 0), (0, 128 - routes.shape[1])))
        extended = rehome(jnp.concatenate([cotangent, route_columns], axis=1))
        own_routes = extended[:, width : width + routes.shape[1]]
        upstream_own = extended[:, :width].astype(F32) * live_own
        upstream_low = upstream_own.astype(BF16)
    with jax.named_scope("qkv"):
        qkv = dot(normed, qkv_full)
    wide = half_heads_wide

    def column_blocks(matrix, which):
        first = which * wide
        return (matrix[:, first : first + wide], matrix[:, 3 * wide + first : 3 * wide + first + wide])

    with jax.named_scope("qk_stats"):
        squares = jnp.stack(
            [sum(jnp.sum(v * v, axis=-1) for v in column_blocks(qkv, which)) for which in range(2)], axis=0
        )
        inv_qk = lax.rsqrt(sum_rows(squares) / width + EPS).T
    pick = (jnp.arange(HEADS, dtype=jnp.int32)[None, :] == jnp.stack(head_ids)[:, None]).astype(F32)

    def head_gain(gain):
        spread = gain.reshape(1, HEADS, head_size) * pick[:, :, None]
        return jnp.sum(spread, axis=1).reshape(1, heads * head_size)

    own_gain_query, own_gain_key = head_gain(gain_query), head_gain(gain_key)
    mixed, query_rot, key_rot, value_low, lse = run_attend_forward(
        qkv, inv_qk, own_gain_query, own_gain_key, cosine, sine, pos_column, key_pos, heads, head_size, rows_here
    )
    with jax.named_scope("out_proj"):
        residual = inputs + reduce_rows(dot(mixed, out_full))

    inv_mid, unit_mid = norm_stats(residual)
    middle_own = (unit_mid * gain_mid).astype(BF16)
    with jax.named_scope("gather_middle"):
        middle = full_rows(gather_chips(middle_own))
    with jax.named_scope("router"):
        logits = dot_nt(router, middle_own)
        router_expo = jnp.exp(logits - jnp.max(logits, axis=0, keepdims=True))
        router_probs = router_expo / jnp.sum(router_expo, axis=0, keepdims=True)
        expert_ids = jnp.arange(experts, dtype=F32)
        chosen = jnp.sum(
            (own_routes.astype(F32).T[None, :, :] == expert_ids[:, None, None]).astype(F32), axis=1
        )
        mix_own = router_probs * chosen
        mix_pieces = [mix_own] + [swap(mix_own, "chip", step) for step in range(1, chips)]
        mix = full_rows([v.T for v in mix_pieces])
    with jax.named_scope("gather_upstream"):
        upstream = full_rows(gather_chips(upstream_low))
    with jax.named_scope("experts"):
        gate_up_lin = dot(middle, gate_up_full)
        act_back = dot_nt(upstream, down_full)
        mixed_act, gate_up_grad, mix_grad = run_experts_middle(gate_up_lin, act_back, mix, experts, part_hidden)
    with jax.named_scope("middle_grad"):
        middle_grad = reduce_rows(dot_nt(gate_up_grad, gate_up_full))
        mix_grad_parts = mix_grad.reshape(shards, chips, piece, experts)
        mix_grad_own = mix_grad_parts[:, 0].reshape(rows_here, experts).T
        for step in range(1, chips):
            mix_grad_own = mix_grad_own + swap(mix_grad_parts[:, step].reshape(rows_here, experts).T, "chip", step)
        prob_grad = mix_grad_own * chosen
        logit_grad = (router_probs * (prob_grad - jnp.sum(router_probs * prob_grad, axis=0, keepdims=True))).astype(BF16)
        middle_grad = middle_grad + dot_tn(logit_grad, router)
        resid_part, gain_mid_grad = norm_back(middle_grad, unit_mid, inv_mid, gain_mid)
        resid_grad = upstream_own + resid_part
        branch_own = resid_grad.astype(BF16)
    with jax.named_scope("gather_branch"):
        branch = full_rows(gather_chips(branch_own))
    with jax.named_scope("mixed_grad"):
        mixed_grad = dot_nt(branch, out_full).astype(BF16)
    query_back, key_back, value_back = run_attend_backward(
        query_rot, key_rot, value_low, lse, mixed_grad, cosine, sine, pos_column, key_pos, heads, head_size, rows_here
    )
    with jax.named_scope("output"):
        expert_sum = reduce_rows(dot(mixed_act, down_full))
        output = send_home(((residual + expert_sum) * live_own).astype(BF16))

    with jax.named_scope("qk_back"):
        units, scaled, sums, gain_grads = [], [], [], []
        for which, (back, gain) in enumerate(((query_back, own_gain_query), (key_back, own_gain_key))):
            unit = jnp.concatenate(column_blocks(qkv, which), axis=1) * inv_qk[:, which : which + 1]
            units.append(unit)
            scaled.append(gain * back)
            sums.append(jnp.sum(unit * gain * back, axis=-1))
            gain_grads.append(jnp.sum(back * unit, axis=0))
        means = (sum_rows(jnp.stack(sums, axis=0)) / width).T
        lin_grads = [
            (inv_qk[:, i : i + 1] * (scaled[i] - units[i] * means[:, i : i + 1])).astype(BF16) for i in range(2)
        ] + [value_back]
        qkv_grad = jnp.concatenate(
            [v[:, :wide] for v in lin_grads] + [v[:, wide:] for v in lin_grads], axis=1
        )
    with jax.named_scope("normed_grad"):
        normed_grad = reduce_rows(dot_nt(qkv_grad, qkv_full))
        input_part, gain_in_grad = norm_back(normed_grad, unit_in, inv_in, gain_in)
        input_grad = send_home((resid_grad + input_part).astype(BF16))

    def reduce_weight(own, other):
        total = (own + swap(other.astype(BF16), "core", 1).astype(F32)).astype(BF16)
        return lax.psum_scatter(total, "shard", scatter_dimension=0, tiled=True)

    fast = chips == 4 and part_hidden % 128 == 0 and heads_spread
    where = jnp.stack([chip, core]).astype(jnp.int32)

    def everywhere(part):
        return lax.all_gather(part, ("chip", "core"), axis=0, tiled=False).reshape((chips, 2) + part.shape)

    def plane_parts(part):
        own = gather_chips(part)
        return own + [swap(v, "core", 1) for v in own]

    def shapes(count, *shape):
        return [jax.ShapeDtypeStruct(shape, F32)] * count

    half_gate_up = gate_up_grad.shape[1] // 2
    with jax.named_scope("w_gate_up_grad"):
        gate_up_part = reduce_weight(
            dot_tn(middle, gate_up_grad[:, :half_gate_up]), dot_tn(middle, gate_up_grad[:, half_gate_up:])
        )
        if fast:
            owners = [(chip ^ step, core ^ turn) for turn in range(2) for step in range(chips)]
            columns = jnp.concatenate(
                [wanted - hidden_at + (2 * its_chip + its_core) * own_hidden for its_chip, its_core in owners]
            )
            order = (columns[:, None] == jnp.arange(hidden, dtype=jnp.int32)[None, :]).astype(BF16)
            tile = 128
            w_gate_grad, w_up_grad = place(
                functools.partial(place_hidden, chips, experts, part_hidden),
                where,
                plane_parts(gate_up_part),
                ((tile, gate_up_part.shape[1]), lambda i, where: (i, 0)),
                shapes(2, experts, shard_rows, hidden),
                ((experts, tile, hidden), lambda i, where: (0, i, 0)),
                (shard_rows // tile,),
                "place_hidden",
                (order,),
            )
        else:
            gate_up_parts = everywhere(gate_up_part).reshape(chips, 2, shard_rows, 2, experts, shards, own_hidden)
            gate_up_parts = gate_up_parts.transpose(3, 4, 2, 5, 0, 1, 6).reshape(2, experts, shard_rows, hidden)
            w_gate_grad, w_up_grad = gate_up_parts[0].astype(F32), gate_up_parts[1].astype(F32)
    half_act = mixed_act.shape[1] // 2
    with jax.named_scope("w_down_grad"):

        def by_shard(matrix):
            split = matrix.reshape(experts, shards, own_hidden, width).transpose(1, 0, 2, 3)
            return split.reshape(matrix.shape)

        down_part = reduce_weight(
            by_shard(dot_tn(mixed_act[:, :half_act], upstream)), by_shard(dot_tn(mixed_act[:, half_act:], upstream))
        )
        if fast:
            (w_down_grad,) = place(
                functools.partial(place_rows, chips),
                where,
                plane_parts(down_part),
                ((own_hidden, width), lambda i, where: (i, 0)),
                shapes(1, experts, shard_hidden, width),
                ((1, shard_hidden, width), lambda i, where: (i, 0, 0)),
                (experts,),
                "place_rows",
            )
        else:
            down_parts = everywhere(down_part).reshape(chips, 2, experts, own_hidden, width)
            w_down_grad = down_parts.transpose(2, 0, 1, 3, 4).reshape(experts, shard_hidden, width).astype(F32)
    with jax.named_scope("w_out_grad"):
        out_grad = dot_tn(mixed, branch)
        if heads_spread:
            top, low = out_grad[:half_heads_wide], out_grad[half_heads_wide:]
            out_grad = jnp.concatenate([jnp.where(first_core, top, low), jnp.where(first_core, low, top)], axis=0)
            left, right = out_grad[:, : width // 2], out_grad[:, width // 2 :]
            out_part = reduce_weight(jnp.where(first_core, left, right), jnp.where(first_core, right, left))
            if fast:
                tile = 32
                (w_out_grad,) = place(
                    functools.partial(place_blocks, chips),
                    where,
                    plane_parts(out_part),
                    ((tile, width // 2), lambda i, where: (i, 0)),
                    shapes(1, chips, head_size, width),
                    ((chips, tile, width), lambda i, where: (0, i, 0)),
                    (head_size // tile,),
                    "place_blocks",
                )
                w_out_grad = w_out_grad.reshape(shard_rows, width)
            else:
                w_out_grad = everywhere(out_part).transpose(0, 2, 1, 3).reshape(shard_rows, width).astype(F32)
        else:
            spread = jnp.zeros((width, width), BF16)
            for i, head in enumerate(head_ids):
                spread = lax.dynamic_update_slice_in_dim(
                    spread, out_grad[i * head_size : (i + 1) * head_size].astype(BF16), head * head_size, 0
                )
            spread = lax.psum_scatter(spread, "shard", scatter_dimension=0, tiled=True)
            w_out_grad = lax.psum(spread, ("chip", "core")).astype(F32)
    with jax.named_scope("w_qkv_grad"):
        qkv_part = reduce_weight(dot_tn(normed, qkv_grad[:, : 3 * wide]), dot_tn(normed, qkv_grad[:, 3 * wide :]))
        if fast:
            tile = 64
            w_query_grad, w_key_grad, w_value_grad = place(
                functools.partial(place_heads, chips, half_heads, head_size),
                where,
                plane_parts(qkv_part),
                ((tile, qkv_part.shape[1]), lambda i, where: (i, 0)),
                shapes(3, shard_rows, width),
                ((tile, width), lambda i, where: (i, 0)),
                (shard_rows // tile,),
                "place_heads",
            )
        else:
            qkv_parts = everywhere(qkv_part).reshape(chips, 2, shard_rows, 3, half_heads, head_size)
            qkv_parts = qkv_parts.transpose(3, 2, 1, 4, 0, 5).reshape(3, shard_rows, width).astype(F32)
            w_query_grad, w_key_grad, w_value_grad = qkv_parts[0], qkv_parts[1], qkv_parts[2]
    with jax.named_scope("small_grads"):
        router_grad = dot(logit_grad, middle_own)

        def spread_heads(gradient):
            by_head = gradient.reshape(heads, 1, head_size) * pick[:, :, None]
            return jnp.sum(by_head, axis=0).reshape(1, width)

        small_grads = jnp.concatenate(
            [
                gain_in_grad[None],
                spread_heads(gain_grads[0]),
                spread_heads(gain_grads[1]),
                gain_mid_grad[None],
                router_grad,
            ],
            axis=0,
        )
        by_owner = small_grads.reshape(small_grads.shape[0], shards, shard_rows).transpose(1, 0, 2)
        small_sum = sum_chips(jnp.sum(exchange(by_owner, "shard"), axis=0))
        small_sum = small_sum + swap(small_sum, "core", 1)
    return (
        output,
        input_grad,
        small_sum[0],
        w_query_grad,
        w_key_grad,
        w_value_grad,
        small_sum[1],
        small_sum[2],
        w_out_grad,
        small_sum[3],
        small_sum[4:].T,
        w_gate_grad,
        w_up_grad,
        w_down_grad,
    )


def solution(mesh):
    reps, shards = mesh.devices.shape
    split = Mesh(mesh.devices.reshape(reps // 2, 2, shards), ("chip", "core", "shard"))
    rows = P(("chip", "core", "shard"), None)
    first, second = P("shard", None), P(None, "shard", None)
    gain = P("shard")
    in_specs = (
        rows, rows, P(("chip", "core"), None), rows, gain, first, first, first, gain, gain, first, gain, first,
        second, second, second,
    )
    out_specs = (rows, rows, gain, first, first, first, gain, gain, first, gain, first, second, second, second)
    return jax.shard_map(body, mesh=split, in_specs=in_specs, out_specs=out_specs, check_vma=False)
```

```python
import functools

import jax
import jax.numpy as jnp
from jax import lax
from jax.experimental import pallas as pl
from jax.experimental.pallas import tpu as pltpu
from jax.sharding import Mesh
from jax.sharding import PartitionSpec as P

HEADS = 16
EPS = 1e-05
THETA = 10000.0
MASKED = -1e30
FAR = 1 << 30
F32 = jnp.float32
BF16 = jnp.bfloat16
VMEM_BYTES = 56 * 1024 * 1024


def dot(left, right):
    return jnp.dot(left, right, preferred_element_type=F32)


def dot_nt(left, right):
    return lax.dot_general(left, right, (((1,), (1,)), ((), ())), preferred_element_type=F32)


def dot_tn(left, right):
    return lax.dot_general(left, right, (((0,), (0,)), ((), ())), preferred_element_type=F32)


def tie(*values):
    return lax.optimization_barrier(values)


def tie_lists(*lists):
    return lax.optimization_barrier([list(values) for values in lists])


def swap(value, axis, step):
    size = lax.axis_size(axis)
    return lax.ppermute(value, axis, [(i, i ^ step) for i in range(size)])


def exchange(parts, axis):
    me = lax.axis_index(axis)
    out = parts
    for step in range(1, lax.axis_size(axis)):
        sent = lax.dynamic_index_in_dim(parts, me ^ step, 0, keepdims=True)
        out = lax.dynamic_update_slice_in_dim(out, swap(sent, axis, step), me ^ step, 0)
    return out


def gather_first(block):
    chips = lax.axis_size("chip")
    if chips != 4:
        return [block] + [swap(block, "chip", step) for step in range(1, chips)]
    half = block.shape[0] // 2
    top, low = block[:half], block[half:]
    two_top, one_low = swap(top, "chip", 2), swap(low, "chip", 1)
    one_top, two_low = swap(top, "chip", 1), swap(low, "chip", 2)
    return [block, one_top, one_low, two_top, two_low]


def gather_last(pieces):
    if lax.axis_size("chip") != 4:
        return pieces
    return pieces + [swap(pieces[3], "chip", 1), swap(pieces[2], "chip", 2)]


def scatter_first(split):
    if len(split) == 2:
        return split
    own_left, own_right, to_one, to_two, keep_left, keep_right = split
    return (own_left, own_right, swap(to_one, "chip", 1), swap(to_two, "chip", 2), keep_left, keep_right)


def scatter_pass(first):
    if len(first) == 2:
        return (first[1][0],)
    _, _, from_one, from_two, keep_left, keep_right = first
    return (
        (keep_left.astype(F32) + from_one[1].astype(F32)).astype(BF16),
        (keep_right.astype(F32) + from_two[1].astype(F32)).astype(BF16),
    )


def scatter_second(passed):
    if len(passed) == 1:
        return list(passed)
    return [swap(passed[0], "chip", 2), swap(passed[1], "chip", 1)]


def scatter_sum(first, arrived):
    if len(first) == 2:
        own, others = first
        for step, other in enumerate(tuple(arrived) + tuple(others[1:])):
            own = own + swap(other, "chip", step + 1).astype(F32)
        return own
    own_left, own_right, from_one, from_two, _, _ = first
    return jnp.concatenate(
        [
            own_left + from_one[0].astype(F32) + arrived[0].astype(F32),
            own_right + from_two[0].astype(F32) + arrived[1].astype(F32),
        ],
        axis=1,
    )


def scatter_chips(split):
    first = scatter_first(split)
    return scatter_sum(first, scatter_second(scatter_pass(first)))


def sum_chips(value):
    step = 1
    while step < lax.axis_size("chip"):
        value = value + swap(value, "chip", step)
        step *= 2
    return value


def sum_rows(values):
    chips = lax.axis_size("chip")
    total = values.reshape(values.shape[0], chips, -1)
    step = 1
    while step < chips:
        other = swap(total, "chip", step)
        total = total + jnp.concatenate([other[:, i ^ step : (i ^ step) + 1] for i in range(chips)], axis=1)
        step *= 2
    return total.reshape(values.shape)


def rehome_chips(rows):
    chips = lax.axis_size("chip")
    parts = rows.reshape(chips, rows.shape[0] // chips, rows.shape[1])
    return lax.all_to_all(parts, "chip", 0, 0, tiled=True)


def rehome_planes(parts):
    return lax.all_to_all(parts, "shard", 0, 0, tiled=True).reshape(-1, parts.shape[2])


def home_planes(rows):
    shards = lax.axis_size("shard")
    parts = rows.reshape(shards, rows.shape[0] // shards, rows.shape[1])
    return lax.all_to_all(parts, "shard", 0, 0, tiled=True)


def home_chips(parts):
    return lax.all_to_all(parts, "chip", 0, 0, tiled=True).reshape(-1, parts.shape[2])


ANYWHERE = pl.BlockSpec(memory_space=pl.ANY)


def run(kernel, name, micros, grid, in_specs, out_specs, out_shape, args, scratch=()):
    return pl.pallas_call(
        kernel,
        grid=grid,
        in_specs=in_specs,
        out_specs=out_specs,
        out_shape=out_shape,
        scratch_shapes=list(scratch),
        compiler_params=pltpu.CompilerParams(vmem_limit_bytes=VMEM_BYTES),
        cost_estimate=pl.CostEstimate(flops=micros * 550_000_000, bytes_accessed=1024, transcendentals=0),
        name=name,
    )(*args)


def load_rows(pieces, target, sems):
    copies, at = [], 0
    for i, piece in enumerate(pieces):
        copies.append(pltpu.make_async_copy(piece, target.at[pl.ds(at, piece.shape[0]), :], sems.at[i]))
        at += piece.shape[0]
    for copy in copies:
        copy.start()
    for copy in copies:
        copy.wait()


def rows_scratch(pieces):
    rows = sum(piece.shape[0] for piece in pieces)
    return [pltpu.VMEM((rows, pieces[0].shape[1]), BF16), pltpu.SemaphoreType.DMA((len(pieces),))]


def column_sums(values):
    ones = jnp.ones((8, values.shape[1]), F32)
    return lax.dot_general(
        ones, values, (((1,), (1,)), ((), ())), precision=lax.Precision.HIGHEST, preferred_element_type=F32
    )


def project_kernel(count, *refs):
    pieces, (weight, out, squares, rows, sems) = refs[:count], refs[count:]

    @pl.when(pl.program_id(0) == 0)
    def _():
        load_rows(pieces, rows, sems)

    result = dot(rows[...], weight[...])
    out[...] = result
    squares[...] = column_sums(result * result)


def run_project(pieces, weight, tile):
    depth, columns = weight.shape
    rows = sum(piece.shape[0] for piece in pieces)
    steps = columns // tile
    return run(
        functools.partial(project_kernel, len(pieces)), "project", 16, (steps,),
        [ANYWHERE] * len(pieces) + [pl.BlockSpec((depth, tile), lambda i: (0, i))],
        [pl.BlockSpec((rows, tile), lambda i: (0, i)), pl.BlockSpec((8, rows), lambda i: (i, 0))],
        [jax.ShapeDtypeStruct((rows, columns), F32), jax.ShapeDtypeStruct((8 * steps, rows), F32)],
        (*pieces, weight),
        rows_scratch(pieces),
    )


def back_kernel(count, *refs):
    pieces, (weight, out, rows, sems) = refs[:count], refs[count:]

    @pl.when(pl.program_id(0) == 0)
    def _():
        load_rows(pieces, rows, sems)

    out[...] = dot_nt(rows[...], weight[...]).astype(BF16)


def run_back(pieces, weight, tile):
    rows = sum(piece.shape[0] for piece in pieces)
    return run(
        functools.partial(back_kernel, len(pieces)), "back", 7, (weight.shape[0] // tile,),
        [ANYWHERE] * len(pieces) + [pl.BlockSpec((tile, weight.shape[1]), lambda i: (i, 0))],
        pl.BlockSpec((rows, tile), lambda i: (0, i)),
        jax.ShapeDtypeStruct((rows, weight.shape[0]), BF16),
        (*pieces, weight),
        rows_scratch(pieces),
    )


def join_experts(ref):
    parts, experts, units, columns = ref.shape
    if parts == 1:
        return ref[...].reshape(experts * units, columns)
    return jnp.concatenate([ref[:, expert].reshape(parts * units, columns) for expert in range(experts)], axis=0)


def split_kernel(block, turned, left, left_w, right_w, own_left, own_right, to_one, to_two, keep_left, keep_right):
    def product(weight):
        if turned:
            return dot_nt(left[...], weight[...])
        return dot(left[...], weight[...] if len(weight.shape) == 2 else join_experts(weight))

    result = product(left_w)
    own_left[...] = result[:block]
    to_one[0] = result[block : 2 * block].astype(BF16)
    keep_left[...] = result[2 * block : 3 * block].astype(BF16)
    to_one[1] = result[3 * block :].astype(BF16)
    result = product(right_w)
    own_right[...] = result[:block]
    keep_right[...] = result[block : 2 * block].astype(BF16)
    to_two[0] = result[2 * block : 3 * block].astype(BF16)
    to_two[1] = result[3 * block :].astype(BF16)


def split_matmul(left, weight, turned, micros):
    chips = lax.axis_size("chip")
    rows = left.shape[0]
    block = rows // chips
    width = weight.shape[0] if turned else weight.shape[-1]
    if chips != 4:
        if weight.ndim == 4:
            weight = weight.transpose(1, 0, 2, 3).reshape(-1, width)
        whole = (dot_nt if turned else dot)(left, weight)
        return (whole[:block], [whole[i * block : (i + 1) * block].astype(BF16) for i in range(1, chips)])
    half, tile = width // 2, 256
    steps = half // tile

    def weight_spec(first):
        if turned:
            return pl.BlockSpec((tile, weight.shape[1]), lambda i: (first + i, 0))
        return pl.BlockSpec((*weight.shape[:-1], tile), lambda i: (0,) * (weight.ndim - 1) + (first + i,))

    one = pl.BlockSpec((block, tile), lambda i: (0, i))
    two = pl.BlockSpec((2, block, tile), lambda i: (0, 0, i))
    wide, low = jax.ShapeDtypeStruct((block, half), F32), jax.ShapeDtypeStruct((block, half), BF16)
    pair = jax.ShapeDtypeStruct((2, block, half), BF16)
    return run(
        functools.partial(split_kernel, block, turned), "split_matmul", micros, (steps,),
        [pl.BlockSpec(left.shape, lambda i: (0, 0)), weight_spec(0), weight_spec(steps)],
        [one, one, two, two, one, one],
        [wide, wide, pair, pair, low, low],
        (left, weight, weight),
    )


def weight_grad_kernel(count, tile, *refs):
    pieces, (grad, out, rows, sems) = refs[:count], refs[count:]

    @pl.when(pl.program_id(0) == 0)
    def _():
        load_rows(pieces, rows, sems)

    columns = pl.ds(pl.multiple_of(pl.program_id(0) * tile, tile), tile)
    out[...] = dot_tn(rows[:, columns], grad[...]).astype(BF16)


def run_weight_grad(pieces, grad, micros, columns=None):
    tile = 512
    depth, columns = pieces[0].shape[1], columns or grad.shape[1]
    return run(
        functools.partial(weight_grad_kernel, len(pieces), tile), "weight_grad", micros, (depth // tile,),
        [ANYWHERE] * len(pieces) + [pl.BlockSpec((grad.shape[0], columns), lambda i: (0, 0))],
        pl.BlockSpec((tile, columns), lambda i: (i, 0)),
        jax.ShapeDtypeStruct((depth, columns), BF16),
        (*pieces, grad),
        rows_scratch(pieces),
    )


def down_grad_kernel(experts, parts, act, upstream, out):
    result = dot_tn(act[...], upstream[...]).astype(BF16)
    own = result.shape[0] // (experts * parts)
    for expert in range(experts):
        for part in range(parts):
            at = (expert * parts + part) * own
            out[part, expert * own : (expert + 1) * own, :] = result[at : at + own]


def run_down_grad(act, upstream, width, experts, parts):
    hidden, tile = act.shape[1], 512
    return run(
        functools.partial(down_grad_kernel, experts, parts), "down_grad", 9, (width // tile,),
        [pl.BlockSpec(act.shape, lambda i: (0, 0)), pl.BlockSpec((upstream.shape[0], tile), lambda i: (0, i))],
        pl.BlockSpec((parts, hidden // parts, tile), lambda i: (0, 0, i)),
        jax.ShapeDtypeStruct((parts, hidden // parts, width), BF16),
        (act, upstream),
    )


def out_grad_kernel(count, tile, *refs):
    pieces, (mixed, out, rows, sems) = refs[:count], refs[count:]

    @pl.when(pl.program_id(0) == 0)
    def _():
        load_rows(pieces, rows, sems)

    columns = pl.ds(pl.multiple_of(pl.program_id(0) * tile, tile), tile)
    out[...] = dot_tn(mixed[...], rows[:, columns]).astype(BF16)


def run_out_grad(mixed, pieces):
    tile, width = 512, pieces[0].shape[1]
    return run(
        functools.partial(out_grad_kernel, len(pieces), tile), "out_grad", 7, (width // tile,),
        [ANYWHERE] * len(pieces) + [pl.BlockSpec(mixed.shape, lambda i: (0, 0))],
        pl.BlockSpec((mixed.shape[1], tile), lambda i: (0, i)),
        jax.ShapeDtypeStruct((mixed.shape[1], width), BF16),
        (*pieces, mixed),
        rows_scratch(pieces),
    )


def lane_roll(values):
    return pltpu.roll(values, values.shape[1] // 2, 1)


def take_block(ref, block, chips, block_rows):
    piece = block_rows // chips
    at = lambda chip: chip * block_rows + block * piece
    return jnp.concatenate([ref[at(chip) : at(chip) + piece, :] for chip in range(chips)], axis=0)


def put_block(ref, block, chips, block_rows, values):
    piece = block_rows // chips
    for chip in range(chips):
        at = chip * block_rows + block * piece
        ref[at : at + piece, :] = values[chip * piece : (chip + 1) * piece]


def attend_forward(
    chips, block_rows, scale,
    query_ref, key_ref, value_ref, inv_ref, gain_q, gain_k, cos_ref, sin_ref, pos_ref, key_pos_ref,
    mixed, query_rot, key_rot, value_low, lse,
):
    blocks = inv_ref.shape[0] // block_rows
    for block in range(blocks):
        rows = pl.ds(block * block_rows, block_rows)
        cosine, sine = cos_ref[rows, :], sin_ref[rows, :]
        inv = take_block(inv_ref, block, chips, block_rows)
        query = take_block(query_ref, block, chips, block_rows) * inv[:, 0:1] * gain_q[...]
        query_rot[rows, :] = (query * cosine + lane_roll(query) * sine).astype(BF16)
        key = take_block(key_ref, block, chips, block_rows) * inv[:, 1:2] * gain_k[...]
        key_rot[rows, :] = (key * cosine + lane_roll(key) * sine).astype(BF16)
        value_low[rows, :] = take_block(value_ref, block, chips, block_rows).astype(BF16)
    for block in range(blocks):
        rows = pl.ds(block * block_rows, block_rows)
        seen = pl.ds(0, (block + 1) * block_rows)
        scores = dot_nt(query_rot[rows, :], key_rot[seen, :]) * scale
        scores = jnp.where(key_pos_ref[:, seen] <= pos_ref[rows, :], scores, MASKED)
        peak = jnp.max(scores, axis=-1, keepdims=True)
        expo = jnp.exp(scores - peak)
        total = jnp.sum(expo, axis=-1, keepdims=True)
        probs_low = (expo * (1.0 / total)).astype(BF16)
        put_block(mixed, block, chips, block_rows, dot(probs_low, value_low[seen, :]).astype(BF16))
        lse[rows, :] = jnp.broadcast_to(peak + jnp.log(total), (block_rows, lse.shape[1]))


def attend_backward(
    chips, block_rows, scale,
    grad_ref, query_ref, key_ref, query_rot, key_rot, value_low, lse, gain_q, gain_k,
    inv_ref, cos_ref, sin_ref, pos_ref, key_pos_ref,
    query_back, key_back, value_back, gains, sums_ref,
    key_sum, value_sum,
):
    blocks = inv_ref.shape[0] // block_rows

    @pl.when(pl.program_id(0) == 0)
    def _():
        sums_ref[...] = jnp.zeros_like(sums_ref)

    key_sum[...] = jnp.zeros_like(key_sum)
    value_sum[...] = jnp.zeros_like(value_sum)
    for block in range(blocks):
        rows = pl.ds(block * block_rows, block_rows)
        seen = pl.ds(0, (block + 1) * block_rows)
        query = query_rot[rows, :]
        grad = take_block(grad_ref, block, chips, block_rows)
        scores = dot_nt(query, key_rot[seen, :]) * scale
        scores = jnp.where(key_pos_ref[:, seen] <= pos_ref[rows, :], scores, MASKED)
        probs = jnp.exp(scores - lse[rows, 0:1])
        probs_grad = dot_nt(grad, value_low[seen, :])
        weighted = jnp.sum(probs * probs_grad, axis=-1, keepdims=True)
        score_grad = (probs * (probs_grad - weighted)).astype(BF16)
        query_grad = dot(score_grad, key_rot[seen, :]) * scale
        turned = query_grad * cos_ref[rows, :] - lane_roll(query_grad) * sin_ref[rows, :]
        put_block(query_back, block, chips, block_rows, turned)
        key_sum[seen, :] += dot_tn(score_grad, query)
        value_sum[seen, :] += dot_tn(probs.astype(BF16), grad)
    for block in range(blocks):
        rows = pl.ds(block * block_rows, block_rows)
        key_grad = key_sum[rows, :] * scale
        turned = key_grad * cos_ref[rows, :] - lane_roll(key_grad) * sin_ref[rows, :]
        put_block(key_back, block, chips, block_rows, turned)
        put_block(value_back, block, chips, block_rows, value_sum[rows, :].astype(BF16))
    for which, (lin, back, gain) in enumerate(((query_ref, query_back, gain_q), (key_ref, key_back, gain_k))):
        product = back[...] * lin[...] * inv_ref[:, which : which + 1]
        sums_ref[pl.ds(8 * which, 8), :] += column_sums(product * gain[...])
        gains[pl.ds(8 * which, 8), :] = jnp.broadcast_to(jnp.sum(product, axis=0, keepdims=True), (8, product.shape[1]))


def attention_specs(rows, head_size, heads):
    column = pl.BlockSpec((rows, head_size), lambda h: (0, h))
    whole = lambda shape: pl.BlockSpec(shape, lambda h: (0, 0))
    part = [pl.BlockSpec((rows, head_size), lambda h, which=which: (0, which * heads + h)) for which in range(3)]
    gain = pl.BlockSpec((1, head_size), lambda h: (0, h))
    return column, whole, part, gain


def run_attend_forward(lin, inv, gains, angles, chips, heads, head_size, block_rows):
    rows, wide = lin.shape[0], heads * head_size
    column, whole, part, gain = attention_specs(rows, head_size, heads)
    low = jax.ShapeDtypeStruct((rows, wide), BF16)
    return run(
        functools.partial(attend_forward, chips, block_rows, head_size**-0.5), "attend_forward", 17, (heads,),
        part + [whole(inv.shape), gain, gain] + [whole(v.shape) for v in angles],
        [column] * 5,
        [low, low, low, low, jax.ShapeDtypeStruct((rows, wide), F32)],
        (lin, lin, lin, inv, *gains, *angles),
    )


def run_attend_backward(mixed_grad, lin, kept, inv, gains, angles, chips, heads, head_size, block_rows):
    rows, wide = mixed_grad.shape
    column, whole, part, gain = attention_specs(rows, head_size, heads)
    full = jax.ShapeDtypeStruct((rows, wide), F32)
    return run(
        functools.partial(attend_backward, chips, block_rows, head_size**-0.5), "attend_backward", 20, (heads,),
        [column, part[0], part[1]] + [column] * 4 + [gain, gain, whole(inv.shape)] + [whole(v.shape) for v in angles],
        [column] * 3 + [pl.BlockSpec((16, head_size), lambda h: (0, h)), whole((16, rows))],
        [full, full, jax.ShapeDtypeStruct((rows, wide), BF16), jax.ShapeDtypeStruct((16, wide), F32),
         jax.ShapeDtypeStruct((16, rows), F32)],
        (mixed_grad, lin, lin, *kept, *gains, inv, *angles),
        [pltpu.VMEM((rows, head_size), F32)] * 2,
    )


def finish_kernel(wide, query_back, key_back, value_back, lin, gain_q, gain_k, inv_ref, mean_ref, out):
    for which, (back, gain) in enumerate(((query_back, gain_q), (key_back, gain_k))):
        inv = inv_ref[:, which : which + 1]
        columns = slice(which * wide, (which + 1) * wide)
        unit = lin[:, columns] * inv
        out[:, columns] = (inv * (gain[...] * back[...] - unit * mean_ref[:, which : which + 1])).astype(BF16)
    out[:, 2 * wide :] = value_back[...]


def run_finish(backs, lin, gains, inv, means, tile):
    rows, wide = backs[0].shape
    spec = lambda columns: pl.BlockSpec((tile, columns), lambda i: (i, 0))
    gain = pl.BlockSpec((1, wide), lambda i: (0, 0))
    return run(
        functools.partial(finish_kernel, wide), "finish", 7, (rows // tile,),
        [spec(wide)] * 3 + [spec(3 * wide), gain, gain, spec(2), spec(2)],
        spec(3 * wide),
        jax.ShapeDtypeStruct((rows, 3 * wide), BF16),
        (*backs, lin, *gains, inv, means),
    )


def experts_kernel(count, experts, top, *refs):
    middles, upstreams, refs = refs[:count], refs[count : 2 * count], refs[2 * count :]
    gate_w, up_w, down_w, router_w, act_out, grad_out, mix_grad, middle, upstream, mix, middle_sems, upstream_sems = refs
    step, tile = pl.program_id(0), gate_w.shape[1]
    rows, depth = middle.shape
    lane = lax.broadcasted_iota(jnp.int32, (1, mix.shape[1]), 1)

    @pl.when(step == 0)
    def _():
        load_rows(middles, middle, middle_sems)
        load_rows(upstreams, upstream, upstream_sems)
        mix_grad[...] = jnp.zeros_like(mix_grad)
        logits = jnp.where(lane < experts, dot_nt(middle[...], router_w[...]), MASKED)
        expo = jnp.exp(logits - jnp.max(logits, axis=-1, keepdims=True))
        chosen = jnp.zeros_like(expo)
        for i in range(top):
            route = upstream[:, depth + i : depth + i + 1].astype(F32)
            chosen = chosen + jnp.where(route == lane.astype(F32), 1.0, 0.0)
        mix[...] = expo / jnp.sum(expo, axis=-1, keepdims=True) * chosen

    mine = lane == step
    mix_column = jnp.sum(jnp.where(mine, mix[...], 0.0), axis=-1, keepdims=True)
    gate = dot(middle[...], gate_w[...])
    up = dot(middle[...], up_w[...])
    back = dot_nt(upstream[:, :depth], down_w[...].reshape(tile, depth))
    sigma = 1.0 / (1.0 + jnp.exp(-gate))
    silu = gate * sigma
    act = silu * up
    mix_grad[...] += jnp.where(mine, jnp.sum(act * back, axis=-1, keepdims=True), 0.0)
    back = back * mix_column
    act_out[...] = (act * mix_column).astype(BF16)
    columns = pl.ds(pl.multiple_of(step * tile, tile), tile)
    up_columns = pl.ds(pl.multiple_of((experts + step) * tile, tile), tile)
    grad_out[:, columns] = (back * up * sigma * (1.0 + gate * (1.0 - sigma))).astype(BF16)
    grad_out[:, up_columns] = (back * silu).astype(BF16)


def run_experts(middles, upstreams, gate_up, down, router, experts, top):
    rows, depth = sum(piece.shape[0] for piece in middles), middles[0].shape[1]
    parts, _, units, _ = down.shape
    tile = parts * units
    whole = lambda shape: pl.BlockSpec(shape, lambda i: (0, 0))
    grad_shape, mix_shape = (rows, 2 * experts * tile), (rows, router.shape[0])
    buffers, sems = zip(rows_scratch(middles), rows_scratch(upstreams))
    return run(
        functools.partial(experts_kernel, len(middles), experts, top), "experts", 26, (experts,),
        [ANYWHERE] * (2 * len(middles))
        + [
            pl.BlockSpec((depth, tile), lambda i: (0, i)),
            pl.BlockSpec((depth, tile), lambda i: (0, experts + i)),
            pl.BlockSpec((parts, 1, units, depth), lambda i: (0, i, 0, 0)),
            whole(router.shape),
        ],
        [pl.BlockSpec((rows, tile), lambda i: (0, i)), whole(grad_shape), whole(mix_shape)],
        [
            jax.ShapeDtypeStruct((rows, experts * tile), BF16),
            jax.ShapeDtypeStruct(grad_shape, BF16),
            jax.ShapeDtypeStruct(mix_shape, F32),
        ],
        (*middles, *upstreams, gate_up, gate_up, down, router),
        [*buffers, pltpu.VMEM(mix_shape, F32), *sems],
    )


def part_owners(where_ref, chips):
    return [(where_ref[0] ^ step, where_ref[1] ^ turn) for turn in range(2) for step in range(chips)]


def place_heads(chips, heads, head_size, where_ref, *refs):
    parts, outs = refs[: 2 * chips], refs[2 * chips :]
    for part, (chip, core) in zip(parts, part_owners(where_ref, chips)):
        for which, out in enumerate(outs):
            for i in range(heads):
                first = (which * heads + i) * head_size
                column = pl.multiple_of((i * chips + chip) * head_size, head_size)
                out[core, :, pl.ds(column, head_size)] = part[:, first : first + head_size].astype(F32)


def place_hidden(chips, where_ref, *refs):
    count = 2 * chips
    order, outs = refs[2 * count], refs[2 * count + 1 :]
    owners = part_owners(where_ref, chips)
    for which, out in enumerate(outs):
        parts = refs[which * count : (which + 1) * count]
        for turn in range(2):
            row = jnp.concatenate([part[...] for part in parts[turn * chips : (turn + 1) * chips]], axis=1)
            out[0, owners[turn * chips][1]] = dot(row, order[...])


def place_rows(chips, where_ref, *refs):
    parts, out = refs[: 2 * chips], refs[-1]
    height = parts[0].shape[0]
    for part, (chip, core) in zip(parts, part_owners(where_ref, chips)):
        row = pl.multiple_of((2 * chip + core) * height, height)
        out[0, pl.ds(row, height), :] = part[...].astype(F32)


def place(kernel, where, parts, part_blocks, out_shapes, out_block, grid, name, extra=()):
    return pl.pallas_call(
        kernel,
        grid_spec=pltpu.PrefetchScalarGridSpec(
            num_scalar_prefetch=1,
            grid=grid,
            in_specs=[pl.BlockSpec(*block) for block in part_blocks for _ in parts]
            + [pl.BlockSpec(v.shape, lambda i, where: (0, 0)) for v in extra],
            out_specs=[pl.BlockSpec(*out_block)] * len(out_shapes),
        ),
        out_shape=out_shapes,
        compiler_params=pltpu.CompilerParams(vmem_limit_bytes=VMEM_BYTES),
        cost_estimate=pl.CostEstimate(flops=8 * 550_000_000, bytes_accessed=1024, transcendentals=0),
        name=name,
    )(where, *(parts * len(part_blocks)), *extra)


def norm_stats(values):
    inv_root = lax.rsqrt(jnp.mean(values * values, axis=-1, keepdims=True) + EPS)
    return (inv_root, values * inv_root)


def norm_back(gradient, unit_rows, inv_root, gain):
    scaled = gain * gradient
    rows_part = inv_root * (scaled - unit_rows * jnp.mean(unit_rows * scaled, axis=-1, keepdims=True))
    return (rows_part, jnp.sum(gradient * unit_rows, axis=0))


def body(
    tokens, cotangent, live_counts, routes, norm_in, w_query, w_key, w_value, norm_query, norm_key, w_out, norm_mid,
    w_router, w_gate, w_up, w_down,
):
    chips, shards = lax.axis_size("chip"), lax.axis_size("shard")
    chip, core = lax.axis_index("chip"), lax.axis_index("core")
    rows_here, width = tokens.shape
    head_size = width // HEADS
    heads = HEADS // chips
    wide = heads * head_size
    experts, top = w_gate.shape[0], routes.shape[1]
    piece = rows_here // chips
    group_rows = rows_here * shards
    shard_rows = w_query.shape[0]
    half_rows = shard_rows // 2
    shard_hidden, hidden = w_down.shape[1], w_gate.shape[2]
    own_hidden = shard_hidden // (2 * chips)
    parts = 2 * shards
    heads_spread = HEADS // shards == chips
    fast = chips == 4 and own_hidden % 16 == 0 and heads_spread
    where = jnp.stack([chip, core]).astype(jnp.int32)
    owners = ("shard", "core")

    def from_owners(part):
        return lax.all_gather(part, owners, axis=0, tiled=True)

    def to_owners(total):
        return lax.psum_scatter(total, owners, scatter_dimension=0, tiled=True)

    with jax.named_scope("rehome_tokens"):
        token_parts = rehome_chips(tokens)

    head_ids = [i * chips + chip for i in range(heads)]
    with jax.named_scope("weights_qkv"):
        qkv_piece = jnp.concatenate(
            [
                lax.dynamic_slice(w, (core * half_rows, head * head_size), (half_rows, head_size))
                for w in (w_query, w_key, w_value)
                for head in head_ids
            ],
            axis=1,
        )
        qkv_w = from_owners(qkv_piece)
    route_columns = jnp.pad(routes.astype(BF16), ((0, 0), (0, 128 - top)))
    extended = jnp.concatenate([cotangent, route_columns], axis=1)
    small = jnp.concatenate(
        [v.astype(F32)[None] for v in (norm_in, norm_query, norm_key, norm_mid)] + [w_router.astype(F32).T], axis=0
    )
    extended, token_parts = tie(extended, token_parts)
    with jax.named_scope("norm_in"):
        inputs = rehome_planes(token_parts).astype(F32)
    with jax.named_scope("small_gathers"):
        small_all = exchange(jnp.broadcast_to(small[None], (shards,) + small.shape), "shard")
        small_all = small_all.transpose(1, 0, 2).reshape(small.shape[0], width)
        gain_in, gain_query, gain_key, gain_mid = (small_all[i] for i in range(4))
        router = jnp.pad(small_all[4:], ((0, 8 - experts), (0, 0))).astype(BF16)
        counts = lax.ppermute(
            live_counts,
            ("chip", "core", "shard"),
            [
                ((i * 2 + k) * shards + j, (j * 2 + k) * shards + i)
                for i in range(chips)
                for k in range(2)
                for j in range(shards)
            ],
        )[0]
    with jax.named_scope("rehome_cotangent"):
        cotangent_parts = exchange(extended.reshape(chips, piece, extended.shape[1]), "chip")
    hidden_at = 2 * chip * own_hidden
    with jax.named_scope("weights_gate_up"):
        unit = jnp.arange(parts * own_hidden, dtype=jnp.int32)
        wanted = (unit // (2 * own_hidden)) * shard_hidden + hidden_at + unit % (2 * own_hidden)
        choose = (jnp.arange(hidden, dtype=jnp.int32)[:, None] == wanted[None, :]).astype(BF16)
        gate_up_rows = [lax.dynamic_slice_in_dim(w, core * half_rows, half_rows, 1) for w in (w_gate, w_up)]
        gate_up_piece = jnp.concatenate(
            [dot(w[expert], choose).astype(BF16) for w in gate_up_rows for expert in range(experts)], axis=1
        )
    down_piece = lax.dynamic_slice_in_dim(w_down, hidden_at + core * own_hidden, own_hidden, 1)
    down_piece = down_piece.reshape(experts * own_hidden, width)
    if heads_spread:
        out_piece = lax.dynamic_slice_in_dim(w_out, chip * head_size + core * (head_size // 2), head_size // 2, 0)
    else:
        out_piece = lax.dynamic_slice_in_dim(w_out, core * half_rows, half_rows, 0)

    starts = jnp.cumsum(counts) - counts
    chip_of = chip ^ jnp.arange(chips, dtype=jnp.int32)
    in_block = (chip_of[:, None] * piece + jnp.arange(piece, dtype=jnp.int32)[None, :]).reshape(1, rows_here)
    positions = (starts[:, None] + in_block).reshape(group_rows)
    live = (in_block < counts[:, None]).reshape(group_rows)
    live_own = live.astype(F32).reshape(shards, chips, piece)[:, 0].reshape(rows_here, 1)
    half_size = head_size // 2
    frequency = THETA ** (-jnp.arange(half_size, dtype=F32) * 2.0 / head_size)
    phases = positions.astype(F32)[:, None] * frequency[None, :]
    cosine, sine = jnp.cos(phases), jnp.sin(phases)
    angles = (
        jnp.concatenate([cosine, cosine], axis=1),
        jnp.concatenate([-sine, sine], axis=1),
        positions[:, None],
        jnp.where(live, positions, FAR)[None, :],
    )

    with jax.named_scope("norm_in"):
        inv_in, unit_in = norm_stats(inputs)
        normed_own = (unit_in * gain_in).astype(BF16)
        normed_own, cotangent_parts = tie(normed_own, cotangent_parts)
    with jax.named_scope("rehome_cotangent"):
        extended = rehome_planes(cotangent_parts)
    with jax.named_scope("gather_normed"):
        normed = gather_first(normed_own)
        normed = gather_last(normed)
        *normed, qkv_w, out_piece, extended = tie(*normed, qkv_w, out_piece, extended)
    with jax.named_scope("weights_out"):
        out_w = from_owners(out_piece)
    with jax.named_scope("gather_upstream"):
        own_routes = extended[:, width : width + top]
        upstream_own = extended[:, :width].astype(F32) * live_own
        upstream = gather_first(jnp.concatenate([upstream_own.astype(BF16), extended[:, width:]], axis=1))
    with jax.named_scope("qkv"):
        lin, squares = run_project(normed, qkv_w, wide)
        inv_qk = lax.rsqrt(sum_rows(jnp.stack([squares[0], squares[8]], axis=0)) / width + EPS).T
        *upstream, inv_qk, out_w, gate_up_piece = tie(*upstream, inv_qk, out_w, gate_up_piece)
        upstream = gather_last(upstream)
    with jax.named_scope("weights_gate_up"):
        gate_up_w = from_owners(gate_up_piece)
    pick = (jnp.arange(HEADS, dtype=jnp.int32)[None, :] == jnp.stack(head_ids)[:, None]).astype(F32)

    def head_gain(gain):
        spread = gain.reshape(1, HEADS, head_size) * pick[:, :, None]
        return jnp.sum(spread, axis=1).reshape(1, wide)

    gains = (head_gain(gain_query), head_gain(gain_key))
    attention = (chips, heads, head_size, rows_here)
    mixed, *kept = run_attend_forward(lin, inv_qk, gains, angles, *attention)
    if not heads_spread:
        out_w = jnp.concatenate([lax.dynamic_slice_in_dim(out_w, h * head_size, head_size, 0) for h in head_ids], axis=0)
    with jax.named_scope("out_proj"):
        out_split = split_matmul(mixed, out_w, False, 6)
        upstream_full = jnp.concatenate(upstream, axis=0)
        upstream_full, *out_split = tie(upstream_full, *out_split)
        residual = inputs + scatter_chips(tuple(out_split))

    with jax.named_scope("gather_middle"):
        inv_mid, unit_mid = norm_stats(residual)
        middle_own = (unit_mid * gain_mid).astype(BF16)
        middle_own, gate_up_w, down_piece = tie(middle_own, gate_up_w, down_piece)
        middle = gather_last(gather_first(middle_own))
    with jax.named_scope("weights_down"):
        down_w = from_owners(down_piece).reshape(parts, experts, own_hidden, width)
        if not fast:
            down_w = down_w.transpose(1, 0, 2, 3).reshape(1, experts, parts * own_hidden, width)
    with jax.named_scope("router"):
        logits = dot_nt(router[:experts], middle_own)
        router_expo = jnp.exp(logits - jnp.max(logits, axis=0, keepdims=True))
        router_probs = router_expo / jnp.sum(router_expo, axis=0, keepdims=True)
        expert_ids = jnp.arange(experts, dtype=F32)
        chosen = jnp.sum(
            (own_routes.astype(F32).T[None, :, :] == expert_ids[:, None, None]).astype(F32), axis=1
        )
    with jax.named_scope("experts"):
        act, lin_grad, mix_grad = run_experts(middle, upstream, gate_up_w, down_w, router, experts, top)
        middle_split = split_matmul(lin_grad, gate_up_w, True, 14)

    with jax.named_scope("middle_grad"):
        *middle_split, mix_grad, act = tie(*middle_split, mix_grad, act)
        middle_first = scatter_first(tuple(middle_split))
        mix_grad_own = mix_grad[:rows_here].T
        for step in range(1, chips):
            part = mix_grad[step * rows_here : (step + 1) * rows_here].T
            mix_grad_own = mix_grad_own + swap(part, "chip", step)
        mix_grad_own = mix_grad_own[:experts]
    with jax.named_scope("w_down_grad"):
        if fast:
            down_total = run_down_grad(act, upstream_full, width, experts, parts)
        else:
            down_total = dot_tn(act, upstream_full[:, :width]).astype(BF16)
            down_total = down_total.reshape(experts, parts, own_hidden, width).transpose(1, 0, 2, 3)
        down_total = down_total.reshape(parts * experts * own_hidden, width)
        down_part = to_owners(down_total)
    with jax.named_scope("w_gate_up_grad"):
        gate_up_total = run_weight_grad(middle, lin_grad, 14)
    with jax.named_scope("middle_grad"):
        passed = scatter_pass(middle_first)
        *passed, gate_up_total = tie(*passed, gate_up_total)
        arrived = scatter_second(tuple(passed))
        prob_grad = mix_grad_own * chosen
        logit_grad = (router_probs * (prob_grad - jnp.sum(router_probs * prob_grad, axis=0, keepdims=True))).astype(BF16)
        middle_grad = scatter_sum(middle_first, arrived) + dot_tn(logit_grad, router[:experts])
        resid_part, gain_mid_grad = norm_back(middle_grad, unit_mid, inv_mid, gain_mid)
        resid_grad = upstream_own + resid_part
        branch_own = resid_grad.astype(BF16)
    with jax.named_scope("gather_branch"):
        branch = gather_first(branch_own)
        *branch, down_part, gate_up_total = tie(*branch, down_part, gate_up_total)
        gate_up_part = to_owners(gate_up_total)
    with jax.named_scope("output"):
        act, branch[0] = tie(act, branch[0])
        sum_split = split_matmul(act, down_w, False, 8)
    with jax.named_scope("mixed_grad"):
        branch = gather_last(branch)
        branch, sum_split = tie_lists(branch, sum_split)
        mixed_grad = run_back(branch, out_w, min(wide, 256))
        sum_first = scatter_first(tuple(sum_split))
    query_back, key_back, value_back, gain_grads, row_sums = run_attend_backward(
        mixed_grad, lin, kept, inv_qk, gains, angles, *attention
    )

    with jax.named_scope("qk_back"):
        *sum_first, row_sums = tie(*sum_first, row_sums)
        sum_first = tuple(sum_first)
        means = (sum_rows(jnp.stack([row_sums[0], row_sums[8]], axis=0)) / width).T
    with jax.named_scope("w_out_grad"):
        out_total = run_out_grad(mixed, branch)
        if not heads_spread:
            spread = jnp.zeros((width, width), BF16)
            for i, head in enumerate(head_ids):
                spread = lax.dynamic_update_slice_in_dim(
                    spread, out_total[i * head_size : (i + 1) * head_size], head * head_size, 0
                )
            out_total = spread
    with jax.named_scope("qk_back"):
        passed = scatter_pass(sum_first)
        *passed, means, out_total = tie(*passed, means, out_total)
        arrived = scatter_second(tuple(passed))
        qkv_grad = run_finish((query_back, key_back, value_back), lin, gains, inv_qk, means, rows_here)
    with jax.named_scope("output"):
        expert_sum = scatter_sum(sum_first, arrived)
        output_low = ((residual + expert_sum) * live_own).astype(BF16)
    with jax.named_scope("normed_grad"):
        normed_split = split_matmul(qkv_grad, qkv_w, True, 11)
        *normed_split, output_low, qkv_grad, value_back = tie(*normed_split, output_low, qkv_grad, value_back)
        normed_first = scatter_first(tuple(normed_split))
    with jax.named_scope("output"):
        output_parts = home_planes(output_low)
    with jax.named_scope("w_value_grad"):
        value_total = run_weight_grad(normed, value_back, 6)
        value_total, out_total, gate_up_part = tie(value_total, out_total, gate_up_part)
        out_part = to_owners(out_total)
    with jax.named_scope("w_query_key_grad"):
        lin_total = run_weight_grad(normed, qkv_grad, 9, 2 * wide)
    with jax.named_scope("normed_grad"):
        passed = scatter_pass(normed_first)
        *passed, value_total, lin_total, output_parts = tie(*passed, value_total, lin_total, output_parts)
        arrived = scatter_second(tuple(passed))
        normed_grad = scatter_sum(normed_first, arrived)
        input_part, gain_in_grad = norm_back(normed_grad, unit_in, inv_in, gain_in)
        input_low = (resid_grad + input_part).astype(BF16)
        input_low, out_part, value_total = tie(input_low, out_part, value_total)
        value_part = to_owners(value_total)

    with jax.named_scope("plane_gathers"):
        down_first, gate_up_first = [gather_first(v) for v in (down_part, gate_up_part)]
        down_first, gate_up_first, (value_part, lin_total) = tie_lists(
            down_first, gate_up_first, (value_part, lin_total)
        )
        lin_part = to_owners(lin_total)
    with jax.named_scope("input_grad"):
        input_parts = home_planes(input_low)

    def everywhere(part):
        return lax.all_gather(part, ("chip", "core"), axis=0, tiled=False).reshape((chips, 2) + part.shape)

    def plane_parts(first):
        own = gather_last(first)
        if len(own) != chips:
            own = own[:1] + [jnp.concatenate(own[i : i + 2], axis=0) for i in range(1, len(own), 2)]
        return own + [swap(v, "core", 1) for v in own]

    def shapes(count, *shape):
        return [jax.ShapeDtypeStruct(shape, F32)] * count

    if fast:
        with jax.named_scope("plane_gathers"):
            out_first, value_first = gather_first(out_part), gather_first(value_part)
            down_parts, gate_up_parts = plane_parts(down_first), plane_parts(gate_up_first)
            down_parts, gate_up_parts, out_first, value_first = tie_lists(
                down_parts, gate_up_parts, out_first, value_first
            )
            out_parts, value_parts = plane_parts(out_first), plane_parts(value_first)
            out_parts, value_parts, (lin_part, input_parts, output_parts) = tie_lists(
                out_parts, value_parts, (lin_part, input_parts, output_parts)
            )
            lin_first = gather_first(lin_part)
        input_grad, output = home_chips(input_parts), home_chips(output_parts)
        with jax.named_scope("w_down_grad"):
            (w_down_grad,) = place(
                functools.partial(place_rows, chips), where, down_parts,
                (((own_hidden, width), lambda i, where: (i, 0)),),
                shapes(1, experts, shard_hidden, width),
                ((1, shard_hidden, width), lambda i, where: (i, 0, 0)),
                (experts,), "place_down",
            )
        with jax.named_scope("w_out_grad"):
            (w_out_grad,) = place(
                functools.partial(place_rows, chips), where, out_parts,
                (((head_size // 2, width // 4), lambda i, where: (0, i)),),
                shapes(1, 1, shard_rows, width),
                ((1, shard_rows, width // 4), lambda i, where: (0, 0, i)),
                (4,), "place_out",
            )
            w_out_grad = w_out_grad.reshape(shard_rows, width)
        with jax.named_scope("w_gate_up_grad"):
            columns = jnp.concatenate([wanted + 2 * own_hidden * ((chip ^ step) - chip) for step in range(chips)])
            order = (columns[:, None] == jnp.arange(hidden, dtype=jnp.int32)[None, :]).astype(BF16)
            tile = parts * own_hidden
            w_gate_grad, w_up_grad = place(
                functools.partial(place_hidden, chips), where, gate_up_parts,
                (
                    ((half_rows, tile), lambda i, where: (0, i)),
                    ((half_rows, tile), lambda i, where: (0, experts + i)),
                ),
                shapes(2, experts, 2, half_rows, hidden),
                ((1, 2, half_rows, hidden), lambda i, where: (i, 0, 0, 0)),
                (experts,), "place_gate_up", (order,),
            )
            w_gate_grad = w_gate_grad.reshape(experts, shard_rows, hidden)
            w_up_grad = w_up_grad.reshape(experts, shard_rows, hidden)
        with jax.named_scope("w_qkv_grad"):
            tile = 64

            def place_lin(its_parts, count):
                placed = place(
                    functools.partial(place_heads, chips, heads, head_size), where, its_parts,
                    (((tile, its_parts[0].shape[1]), lambda i, where: (i, 0)),),
                    shapes(count, 2, half_rows, width),
                    ((2, tile, width), lambda i, where: (0, i, 0)),
                    (half_rows // tile,), "place_heads",
                )
                return [v.reshape(shard_rows, width) for v in placed]

            (w_value_grad,) = place_lin(value_parts, 1)
            lin_first, (w_down_grad, w_gate_grad, w_up_grad, w_out_grad, w_value_grad) = tie_lists(
                lin_first, (w_down_grad, w_gate_grad, w_up_grad, w_out_grad, w_value_grad)
            )
            lin_parts, (output, input_grad) = tie_lists(plane_parts(lin_first), (output, input_grad))
            w_query_grad, w_key_grad = place_lin(lin_parts, 2)
    else:
        input_grad, output = home_chips(input_parts), home_chips(output_parts)
        spread = everywhere(down_part).reshape(chips, 2, experts, own_hidden, width)
        w_down_grad = spread.transpose(2, 0, 1, 3, 4).reshape(experts, shard_hidden, width).astype(F32)
        spread = everywhere(gate_up_part).reshape(chips, 2, half_rows, 2, experts, shards, 2 * own_hidden)
        spread = spread.transpose(3, 4, 1, 2, 5, 0, 6).reshape(2, experts, shard_rows, hidden).astype(F32)
        w_gate_grad, w_up_grad = spread[0], spread[1]
        if heads_spread:
            w_out_grad = everywhere(out_part).reshape(shard_rows, width).astype(F32)
        else:
            spread = lax.psum(out_part.astype(F32), "chip")
            w_out_grad = lax.all_gather(spread, "core", axis=0, tiled=True)

        def heads_back(part, count):
            spread = everywhere(part).reshape(chips, 2, half_rows, count, heads, head_size)
            return spread.transpose(3, 1, 2, 4, 0, 5).reshape(count, shard_rows, width).astype(F32)

        (w_value_grad,) = heads_back(value_part, 1)
        w_query_grad, w_key_grad = heads_back(lin_part, 2)
    with jax.named_scope("small_grads"):
        router_grad = dot(logit_grad, middle_own)

        def spread_heads(which):
            by_head = gain_grads[8 * which].reshape(heads, 1, head_size) * pick[:, :, None]
            return jnp.sum(by_head, axis=0).reshape(1, width)

        small_grads = jnp.concatenate(
            [gain_in_grad[None], spread_heads(0), spread_heads(1), gain_mid_grad[None], router_grad], axis=0
        )
        by_owner = small_grads.reshape(small_grads.shape[0], shards, shard_rows).transpose(1, 0, 2)
        small_sum = sum_chips(jnp.sum(exchange(by_owner, "shard"), axis=0))
        small_sum = small_sum + swap(small_sum, "core", 1)
    return (
        output,
        input_grad,
        small_sum[0],
        w_query_grad,
        w_key_grad,
        w_value_grad,
        small_sum[1],
        small_sum[2],
        w_out_grad,
        small_sum[3],
        small_sum[4:].T,
        w_gate_grad,
        w_up_grad,
        w_down_grad,
    )


def solution(mesh):
    reps, shards = mesh.devices.shape
    split = Mesh(mesh.devices.reshape(reps // 2, 2, shards), ("chip", "core", "shard"))
    rows = P(("chip", "core", "shard"), None)
    first, second = P("shard", None), P(None, "shard", None)
    gain = P("shard")
    in_specs = (
        rows, rows, P(("chip", "core"), None), rows, gain, first, first, first, gain, gain, first, gain, first,
        second, second, second,
    )
    out_specs = (rows, rows, gain, first, first, first, gain, gain, first, gain, first, second, second, second)
    return jax.shard_map(body, mesh=split, in_specs=in_specs, out_specs=out_specs, check_vma=False)
```

```python
import functools

import jax
import jax.numpy as jnp
from jax import lax
from jax.experimental import pallas as pl
from jax.experimental.pallas import tpu as pltpu
from jax.sharding import Mesh
from jax.sharding import PartitionSpec as P

HEADS = 16
EPS = 1e-05
THETA = 10000.0
MASKED = -1e30
FAR = 1 << 30
F32 = jnp.float32
BF16 = jnp.bfloat16
VMEM_BYTES = 56 * 1024 * 1024


def dot(left, right):
    return jnp.dot(left, right, preferred_element_type=F32)


def dot_nt(left, right):
    return lax.dot_general(left, right, (((1,), (1,)), ((), ())), preferred_element_type=F32)


def dot_tn(left, right):
    return lax.dot_general(left, right, (((0,), (0,)), ((), ())), preferred_element_type=F32)


def tie(*values):
    return lax.optimization_barrier(values)


def tie_lists(*lists):
    return lax.optimization_barrier([list(values) for values in lists])


def swap(value, axis, step):
    size = lax.axis_size(axis)
    return lax.ppermute(value, axis, [(i, i ^ step) for i in range(size)])


def exchange(parts, axis):
    me = lax.axis_index(axis)
    out = parts
    for step in range(1, lax.axis_size(axis)):
        sent = lax.dynamic_index_in_dim(parts, me ^ step, 0, keepdims=True)
        out = lax.dynamic_update_slice_in_dim(out, swap(sent, axis, step), me ^ step, 0)
    return out


def gather_first(block):
    chips = lax.axis_size("chip")
    if chips != 4:
        return [block] + [swap(block, "chip", step) for step in range(1, chips)]
    half = block.shape[0] // 2
    top, low = block[:half], block[half:]
    two_top, one_low = swap(top, "chip", 2), swap(low, "chip", 1)
    one_top, two_low = swap(top, "chip", 1), swap(low, "chip", 2)
    return [block, one_top, one_low, two_top, two_low]


def gather_last(pieces):
    if lax.axis_size("chip") != 4:
        return pieces
    return pieces + [swap(pieces[3], "chip", 1), swap(pieces[2], "chip", 2)]


def scatter_first(split):
    if len(split) == 2:
        return split
    own_left, own_right, to_one, to_two, keep_left, keep_right = split
    return (own_left, own_right, swap(to_one, "chip", 1), swap(to_two, "chip", 2), keep_left, keep_right)


def scatter_pass(first):
    if len(first) == 2:
        return (first[1][0],)
    _, _, from_one, from_two, keep_left, keep_right = first
    return (
        (keep_left.astype(F32) + from_one[1].astype(F32)).astype(BF16),
        (keep_right.astype(F32) + from_two[1].astype(F32)).astype(BF16),
    )


def scatter_second(passed):
    if len(passed) == 1:
        return list(passed)
    return [swap(passed[0], "chip", 2), swap(passed[1], "chip", 1)]


def scatter_sum(first, arrived):
    if len(first) == 2:
        own, others = first
        for step, other in enumerate(tuple(arrived) + tuple(others[1:])):
            own = own + swap(other, "chip", step + 1).astype(F32)
        return own
    own_left, own_right, from_one, from_two, _, _ = first
    return jnp.concatenate(
        [
            own_left + from_one[0].astype(F32) + arrived[0].astype(F32),
            own_right + from_two[0].astype(F32) + arrived[1].astype(F32),
        ],
        axis=1,
    )


def scatter_chips(split):
    first = scatter_first(split)
    return scatter_sum(first, scatter_second(scatter_pass(first)))


def sum_chips(value):
    step = 1
    while step < lax.axis_size("chip"):
        value = value + swap(value, "chip", step)
        step *= 2
    return value


def sum_rows(values):
    chips = lax.axis_size("chip")
    total = values.reshape(values.shape[0], chips, -1)
    step = 1
    while step < chips:
        other = swap(total, "chip", step)
        total = total + jnp.concatenate([other[:, i ^ step : (i ^ step) + 1] for i in range(chips)], axis=1)
        step *= 2
    return total.reshape(values.shape)


def rehome_chips(rows):
    chips = lax.axis_size("chip")
    parts = rows.reshape(chips, rows.shape[0] // chips, rows.shape[1])
    return lax.all_to_all(parts, "chip", 0, 0, tiled=True)


def rehome_planes(parts):
    return lax.all_to_all(parts, "shard", 0, 0, tiled=True).reshape(-1, parts.shape[2])


def home_planes(rows):
    shards = lax.axis_size("shard")
    parts = rows.reshape(shards, rows.shape[0] // shards, rows.shape[1])
    return lax.all_to_all(parts, "shard", 0, 0, tiled=True)


def home_chips(parts):
    return lax.all_to_all(parts, "chip", 0, 0, tiled=True).reshape(-1, parts.shape[2])


ANYWHERE = pl.BlockSpec(memory_space=pl.ANY)


def run(kernel, name, micros, grid, in_specs, out_specs, out_shape, args, scratch=()):
    return pl.pallas_call(
        kernel,
        grid=grid,
        in_specs=in_specs,
        out_specs=out_specs,
        out_shape=out_shape,
        scratch_shapes=list(scratch),
        compiler_params=pltpu.CompilerParams(vmem_limit_bytes=VMEM_BYTES),
        cost_estimate=pl.CostEstimate(flops=micros * 550_000_000, bytes_accessed=1024, transcendentals=0),
        name=name,
    )(*args)


def load_rows(pieces, target, sems):
    copies, at = [], 0
    for i, piece in enumerate(pieces):
        copies.append(pltpu.make_async_copy(piece, target.at[pl.ds(at, piece.shape[0]), :], sems.at[i]))
        at += piece.shape[0]
    for copy in copies:
        copy.start()
    for copy in copies:
        copy.wait()


def rows_scratch(pieces):
    rows = sum(piece.shape[0] for piece in pieces)
    return [pltpu.VMEM((rows, pieces[0].shape[1]), BF16), pltpu.SemaphoreType.DMA((len(pieces),))]


def column_sums(values):
    ones = jnp.ones((8, values.shape[1]), F32)
    return lax.dot_general(
        ones, values, (((1,), (1,)), ((), ())), precision=lax.Precision.HIGHEST, preferred_element_type=F32
    )


def project_kernel(count, *refs):
    pieces, (weight, out, squares, rows, sems) = refs[:count], refs[count:]

    @pl.when(pl.program_id(0) == 0)
    def _():
        load_rows(pieces, rows, sems)

    result = dot(rows[...], weight[...])
    out[...] = result
    squares[...] = column_sums(result * result)


def run_project(pieces, weight, tile):
    depth, columns = weight.shape
    rows = sum(piece.shape[0] for piece in pieces)
    steps = columns // tile
    return run(
        functools.partial(project_kernel, len(pieces)), "project", 16, (steps,),
        [ANYWHERE] * len(pieces) + [pl.BlockSpec((depth, tile), lambda i: (0, i))],
        [pl.BlockSpec((rows, tile), lambda i: (0, i)), pl.BlockSpec((8, rows), lambda i: (i, 0))],
        [jax.ShapeDtypeStruct((rows, columns), F32), jax.ShapeDtypeStruct((8 * steps, rows), F32)],
        (*pieces, weight),
        rows_scratch(pieces),
    )


def back_kernel(count, *refs):
    pieces, (weight, out, rows, sems) = refs[:count], refs[count:]

    @pl.when(pl.program_id(0) == 0)
    def _():
        load_rows(pieces, rows, sems)

    out[...] = dot_nt(rows[...], weight[...]).astype(BF16)


def run_back(pieces, weight, tile):
    rows = sum(piece.shape[0] for piece in pieces)
    return run(
        functools.partial(back_kernel, len(pieces)), "back", 7, (weight.shape[0] // tile,),
        [ANYWHERE] * len(pieces) + [pl.BlockSpec((tile, weight.shape[1]), lambda i: (i, 0))],
        pl.BlockSpec((rows, tile), lambda i: (0, i)),
        jax.ShapeDtypeStruct((rows, weight.shape[0]), BF16),
        (*pieces, weight),
        rows_scratch(pieces),
    )


def join_experts(ref):
    parts, experts, units, columns = ref.shape
    if parts == 1:
        return ref[...].reshape(experts * units, columns)
    return jnp.concatenate([ref[:, expert].reshape(parts * units, columns) for expert in range(experts)], axis=0)


def split_kernel(block, turned, left, left_w, right_w, own_left, own_right, to_one, to_two, keep_left, keep_right):
    def product(weight):
        if turned:
            return dot_nt(left[...], weight[...])
        return dot(left[...], weight[...] if len(weight.shape) == 2 else join_experts(weight))

    result = product(left_w)
    own_left[...] = result[:block]
    to_one[0] = result[block : 2 * block].astype(BF16)
    keep_left[...] = result[2 * block : 3 * block].astype(BF16)
    to_one[1] = result[3 * block :].astype(BF16)
    result = product(right_w)
    own_right[...] = result[:block]
    keep_right[...] = result[block : 2 * block].astype(BF16)
    to_two[0] = result[2 * block : 3 * block].astype(BF16)
    to_two[1] = result[3 * block :].astype(BF16)


def split_matmul(left, weight, turned, micros):
    chips = lax.axis_size("chip")
    rows = left.shape[0]
    block = rows // chips
    width = weight.shape[0] if turned else weight.shape[-1]
    if chips != 4:
        if weight.ndim == 4:
            weight = weight.transpose(1, 0, 2, 3).reshape(-1, width)
        whole = (dot_nt if turned else dot)(left, weight)
        return (whole[:block], [whole[i * block : (i + 1) * block].astype(BF16) for i in range(1, chips)])
    half, tile = width // 2, 256
    steps = half // tile

    def weight_spec(first):
        if turned:
            return pl.BlockSpec((tile, weight.shape[1]), lambda i: (first + i, 0))
        return pl.BlockSpec((*weight.shape[:-1], tile), lambda i: (0,) * (weight.ndim - 1) + (first + i,))

    one = pl.BlockSpec((block, tile), lambda i: (0, i))
    two = pl.BlockSpec((2, block, tile), lambda i: (0, 0, i))
    wide, low = jax.ShapeDtypeStruct((block, half), F32), jax.ShapeDtypeStruct((block, half), BF16)
    pair = jax.ShapeDtypeStruct((2, block, half), BF16)
    return run(
        functools.partial(split_kernel, block, turned), "split_matmul", micros, (steps,),
        [pl.BlockSpec(left.shape, lambda i: (0, 0)), weight_spec(0), weight_spec(steps)],
        [one, one, two, two, one, one],
        [wide, wide, pair, pair, low, low],
        (left, weight, weight),
    )


def weight_grad_kernel(count, tile, *refs):
    pieces, (grad, out, rows, sems) = refs[:count], refs[count:]

    @pl.when(pl.program_id(0) == 0)
    def _():
        load_rows(pieces, rows, sems)

    columns = pl.ds(pl.multiple_of(pl.program_id(0) * tile, tile), tile)
    out[...] = dot_tn(rows[:, columns], grad[...]).astype(BF16)


def run_weight_grad(pieces, grad, micros, columns=None):
    tile = 512
    depth, columns = pieces[0].shape[1], columns or grad.shape[1]
    return run(
        functools.partial(weight_grad_kernel, len(pieces), tile), "weight_grad", micros, (depth // tile,),
        [ANYWHERE] * len(pieces) + [pl.BlockSpec((grad.shape[0], columns), lambda i: (0, 0))],
        pl.BlockSpec((tile, columns), lambda i: (i, 0)),
        jax.ShapeDtypeStruct((depth, columns), BF16),
        (*pieces, grad),
        rows_scratch(pieces),
    )


def down_grad_kernel(experts, parts, act, upstream, out):
    result = dot_tn(act[...], upstream[...]).astype(BF16)
    own = result.shape[0] // (experts * parts)
    for expert in range(experts):
        for part in range(parts):
            at = (expert * parts + part) * own
            out[part, expert * own : (expert + 1) * own, :] = result[at : at + own]


def run_down_grad(act, upstream, width, experts, parts):
    hidden, tile = act.shape[1], 512
    return run(
        functools.partial(down_grad_kernel, experts, parts), "down_grad", 9, (width // tile,),
        [pl.BlockSpec(act.shape, lambda i: (0, 0)), pl.BlockSpec((upstream.shape[0], tile), lambda i: (0, i))],
        pl.BlockSpec((parts, hidden // parts, tile), lambda i: (0, 0, i)),
        jax.ShapeDtypeStruct((parts, hidden // parts, width), BF16),
        (act, upstream),
    )


def out_grad_kernel(count, tile, *refs):
    pieces, (mixed, out, rows, sems) = refs[:count], refs[count:]

    @pl.when(pl.program_id(0) == 0)
    def _():
        load_rows(pieces, rows, sems)

    columns = pl.ds(pl.multiple_of(pl.program_id(0) * tile, tile), tile)
    out[...] = dot_tn(mixed[...], rows[:, columns]).astype(BF16)


def run_out_grad(mixed, pieces):
    tile, width = 512, pieces[0].shape[1]
    return run(
        functools.partial(out_grad_kernel, len(pieces), tile), "out_grad", 7, (width // tile,),
        [ANYWHERE] * len(pieces) + [pl.BlockSpec(mixed.shape, lambda i: (0, 0))],
        pl.BlockSpec((mixed.shape[1], tile), lambda i: (0, i)),
        jax.ShapeDtypeStruct((mixed.shape[1], width), BF16),
        (*pieces, mixed),
        rows_scratch(pieces),
    )


def lane_roll(values):
    return pltpu.roll(values, values.shape[1] // 2, 1)


def take_block(ref, block, chips, block_rows):
    piece = block_rows // chips
    at = lambda chip: chip * block_rows + block * piece
    return jnp.concatenate([ref[at(chip) : at(chip) + piece, :] for chip in range(chips)], axis=0)


def put_block(ref, block, chips, block_rows, values):
    piece = block_rows // chips
    for chip in range(chips):
        at = chip * block_rows + block * piece
        ref[at : at + piece, :] = values[chip * piece : (chip + 1) * piece]


def attend_forward(
    chips, block_rows, scale,
    query_ref, key_ref, value_ref, inv_ref, gain_q, gain_k, cos_ref, sin_ref, pos_ref, key_pos_ref,
    mixed, query_rot, key_rot, value_low, lse,
):
    blocks = inv_ref.shape[0] // block_rows
    for block in range(blocks):
        rows = pl.ds(block * block_rows, block_rows)
        cosine, sine = cos_ref[rows, :], sin_ref[rows, :]
        inv = take_block(inv_ref, block, chips, block_rows)
        query = take_block(query_ref, block, chips, block_rows) * inv[:, 0:1] * gain_q[...]
        query_rot[rows, :] = (query * cosine + lane_roll(query) * sine).astype(BF16)
        key = take_block(key_ref, block, chips, block_rows) * inv[:, 1:2] * gain_k[...]
        key_rot[rows, :] = (key * cosine + lane_roll(key) * sine).astype(BF16)
        value_low[rows, :] = take_block(value_ref, block, chips, block_rows).astype(BF16)
    for block in range(blocks):
        rows = pl.ds(block * block_rows, block_rows)
        seen = pl.ds(0, (block + 1) * block_rows)
        scores = dot_nt(query_rot[rows, :], key_rot[seen, :]) * scale
        scores = jnp.where(key_pos_ref[:, seen] <= pos_ref[rows, :], scores, MASKED)
        peak = jnp.max(scores, axis=-1, keepdims=True)
        expo = jnp.exp(scores - peak)
        total = jnp.sum(expo, axis=-1, keepdims=True)
        probs_low = (expo * (1.0 / total)).astype(BF16)
        put_block(mixed, block, chips, block_rows, dot(probs_low, value_low[seen, :]).astype(BF16))
        lse[rows, :] = jnp.broadcast_to(peak + jnp.log(total), (block_rows, lse.shape[1]))


def attend_backward(
    chips, block_rows, scale,
    grad_ref, query_ref, key_ref, query_rot, key_rot, value_low, lse, gain_q, gain_k,
    inv_ref, cos_ref, sin_ref, pos_ref, key_pos_ref,
    query_back, key_back, value_back, gains, sums_ref,
    key_sum, value_sum,
):
    blocks = inv_ref.shape[0] // block_rows

    @pl.when(pl.program_id(0) == 0)
    def _():
        sums_ref[...] = jnp.zeros_like(sums_ref)

    key_sum[...] = jnp.zeros_like(key_sum)
    value_sum[...] = jnp.zeros_like(value_sum)
    for block in range(blocks):
        rows = pl.ds(block * block_rows, block_rows)
        seen = pl.ds(0, (block + 1) * block_rows)
        query = query_rot[rows, :]
        grad = take_block(grad_ref, block, chips, block_rows)
        scores = dot_nt(query, key_rot[seen, :]) * scale
        scores = jnp.where(key_pos_ref[:, seen] <= pos_ref[rows, :], scores, MASKED)
        probs = jnp.exp(scores - lse[rows, 0:1])
        probs_grad = dot_nt(grad, value_low[seen, :])
        weighted = jnp.sum(probs * probs_grad, axis=-1, keepdims=True)
        score_grad = (probs * (probs_grad - weighted)).astype(BF16)
        query_grad = dot(score_grad, key_rot[seen, :]) * scale
        turned = query_grad * cos_ref[rows, :] - lane_roll(query_grad) * sin_ref[rows, :]
        put_block(query_back, block, chips, block_rows, turned)
        key_sum[seen, :] += dot_tn(score_grad, query)
        value_sum[seen, :] += dot_tn(probs.astype(BF16), grad)
    for block in range(blocks):
        rows = pl.ds(block * block_rows, block_rows)
        key_grad = key_sum[rows, :] * scale
        turned = key_grad * cos_ref[rows, :] - lane_roll(key_grad) * sin_ref[rows, :]
        put_block(key_back, block, chips, block_rows, turned)
        put_block(value_back, block, chips, block_rows, value_sum[rows, :].astype(BF16))
    for which, (lin, back, gain) in enumerate(((query_ref, query_back, gain_q), (key_ref, key_back, gain_k))):
        product = back[...] * lin[...] * inv_ref[:, which : which + 1]
        sums_ref[pl.ds(8 * which, 8), :] += column_sums(product * gain[...])
        gains[pl.ds(8 * which, 8), :] = jnp.broadcast_to(jnp.sum(product, axis=0, keepdims=True), (8, product.shape[1]))


def attention_specs(rows, head_size, heads):
    column = pl.BlockSpec((rows, head_size), lambda h: (0, h))
    whole = lambda shape: pl.BlockSpec(shape, lambda h: (0, 0))
    part = [pl.BlockSpec((rows, head_size), lambda h, which=which: (0, which * heads + h)) for which in range(3)]
    gain = pl.BlockSpec((1, head_size), lambda h: (0, h))
    return column, whole, part, gain


def run_attend_forward(lin, inv, gains, angles, chips, heads, head_size, block_rows):
    rows, wide = lin.shape[0], heads * head_size
    column, whole, part, gain = attention_specs(rows, head_size, heads)
    low = jax.ShapeDtypeStruct((rows, wide), BF16)
    return run(
        functools.partial(attend_forward, chips, block_rows, head_size**-0.5), "attend_forward", 17, (heads,),
        part + [whole(inv.shape), gain, gain] + [whole(v.shape) for v in angles],
        [column] * 5,
        [low, low, low, low, jax.ShapeDtypeStruct((rows, wide), F32)],
        (lin, lin, lin, inv, *gains, *angles),
    )


def run_attend_backward(mixed_grad, lin, kept, inv, gains, angles, chips, heads, head_size, block_rows):
    rows, wide = mixed_grad.shape
    column, whole, part, gain = attention_specs(rows, head_size, heads)
    full = jax.ShapeDtypeStruct((rows, wide), F32)
    return run(
        functools.partial(attend_backward, chips, block_rows, head_size**-0.5), "attend_backward", 20, (heads,),
        [column, part[0], part[1]] + [column] * 4 + [gain, gain, whole(inv.shape)] + [whole(v.shape) for v in angles],
        [column] * 3 + [pl.BlockSpec((16, head_size), lambda h: (0, h)), whole((16, rows))],
        [full, full, jax.ShapeDtypeStruct((rows, wide), BF16), jax.ShapeDtypeStruct((16, wide), F32),
         jax.ShapeDtypeStruct((16, rows), F32)],
        (mixed_grad, lin, lin, *kept, *gains, inv, *angles),
        [pltpu.VMEM((rows, head_size), F32)] * 2,
    )


def finish_kernel(wide, query_back, key_back, value_back, lin, gain_q, gain_k, inv_ref, mean_ref, out):
    for which, (back, gain) in enumerate(((query_back, gain_q), (key_back, gain_k))):
        inv = inv_ref[:, which : which + 1]
        columns = slice(which * wide, (which + 1) * wide)
        unit = lin[:, columns] * inv
        out[:, columns] = (inv * (gain[...] * back[...] - unit * mean_ref[:, which : which + 1])).astype(BF16)
    out[:, 2 * wide :] = value_back[...]


def run_finish(backs, lin, gains, inv, means, tile):
    rows, wide = backs[0].shape
    spec = lambda columns: pl.BlockSpec((tile, columns), lambda i: (i, 0))
    gain = pl.BlockSpec((1, wide), lambda i: (0, 0))
    return run(
        functools.partial(finish_kernel, wide), "finish", 7, (rows // tile,),
        [spec(wide)] * 3 + [spec(3 * wide), gain, gain, spec(2), spec(2)],
        spec(3 * wide),
        jax.ShapeDtypeStruct((rows, 3 * wide), BF16),
        (*backs, lin, *gains, inv, means),
    )


def experts_kernel(count, experts, top, *refs):
    middles, upstreams, refs = refs[:count], refs[count : 2 * count], refs[2 * count :]
    gate_w, up_w, down_w, router_w, act_out, grad_out, mix_grad, middle, upstream, mix, middle_sems, upstream_sems = refs
    step, tile = pl.program_id(0), gate_w.shape[1]
    rows, depth = middle.shape
    lane = lax.broadcasted_iota(jnp.int32, (1, mix.shape[1]), 1)

    @pl.when(step == 0)
    def _():
        load_rows(middles, middle, middle_sems)
        load_rows(upstreams, upstream, upstream_sems)
        mix_grad[...] = jnp.zeros_like(mix_grad)
        logits = jnp.where(lane < experts, dot_nt(middle[...], router_w[...]), MASKED)
        expo = jnp.exp(logits - jnp.max(logits, axis=-1, keepdims=True))
        chosen = jnp.zeros_like(expo)
        for i in range(top):
            route = upstream[:, depth + i : depth + i + 1].astype(F32)
            chosen = chosen + jnp.where(route == lane.astype(F32), 1.0, 0.0)
        mix[...] = expo / jnp.sum(expo, axis=-1, keepdims=True) * chosen

    mine = lane == step
    mix_column = jnp.sum(jnp.where(mine, mix[...], 0.0), axis=-1, keepdims=True)
    gate = dot(middle[...], gate_w[...])
    up = dot(middle[...], up_w[...])
    back = dot_nt(upstream[:, :depth], down_w[...].reshape(tile, depth))
    sigma = 1.0 / (1.0 + jnp.exp(-gate))
    silu = gate * sigma
    act = silu * up
    mix_grad[...] += jnp.where(mine, jnp.sum(act * back, axis=-1, keepdims=True), 0.0)
    back = back * mix_column
    act_out[...] = (act * mix_column).astype(BF16)
    columns = pl.ds(pl.multiple_of(step * tile, tile), tile)
    up_columns = pl.ds(pl.multiple_of((experts + step) * tile, tile), tile)
    grad_out[:, columns] = (back * up * sigma * (1.0 + gate * (1.0 - sigma))).astype(BF16)
    grad_out[:, up_columns] = (back * silu).astype(BF16)


def run_experts(middles, upstreams, gate_up, down, router, experts, top):
    rows, depth = sum(piece.shape[0] for piece in middles), middles[0].shape[1]
    parts, _, units, _ = down.shape
    tile = parts * units
    whole = lambda shape: pl.BlockSpec(shape, lambda i: (0, 0))
    grad_shape, mix_shape = (rows, 2 * experts * tile), (rows, router.shape[0])
    buffers, sems = zip(rows_scratch(middles), rows_scratch(upstreams))
    return run(
        functools.partial(experts_kernel, len(middles), experts, top), "experts", 26, (experts,),
        [ANYWHERE] * (2 * len(middles))
        + [
            pl.BlockSpec((depth, tile), lambda i: (0, i)),
            pl.BlockSpec((depth, tile), lambda i: (0, experts + i)),
            pl.BlockSpec((parts, 1, units, depth), lambda i: (0, i, 0, 0)),
            whole(router.shape),
        ],
        [pl.BlockSpec((rows, tile), lambda i: (0, i)), whole(grad_shape), whole(mix_shape)],
        [
            jax.ShapeDtypeStruct((rows, experts * tile), BF16),
            jax.ShapeDtypeStruct(grad_shape, BF16),
            jax.ShapeDtypeStruct(mix_shape, F32),
        ],
        (*middles, *upstreams, gate_up, gate_up, down, router),
        [*buffers, pltpu.VMEM(mix_shape, F32), *sems],
    )


def part_owners(where_ref, chips):
    return [(where_ref[0] ^ step, where_ref[1] ^ turn) for turn in range(2) for step in range(chips)]


def place_heads(chips, heads, head_size, where_ref, *refs):
    parts, outs = refs[: 2 * chips], refs[2 * chips :]
    for part, (chip, core) in zip(parts, part_owners(where_ref, chips)):
        for which, out in enumerate(outs):
            for i in range(heads):
                first = (which * heads + i) * head_size
                column = pl.multiple_of((i * chips + chip) * head_size, head_size)
                out[core, :, pl.ds(column, head_size)] = part[:, first : first + head_size].astype(F32)


def place_hidden(chips, where_ref, *refs):
    count = 2 * chips
    order, outs = refs[2 * count], refs[2 * count + 1 :]
    owners = part_owners(where_ref, chips)
    for which, out in enumerate(outs):
        parts = refs[which * count : (which + 1) * count]
        for turn in range(2):
            row = jnp.concatenate([part[...] for part in parts[turn * chips : (turn + 1) * chips]], axis=1)
            out[0, owners[turn * chips][1]] = dot(row, order[...])


def place_rows(chips, where_ref, *refs):
    parts, out = refs[: 2 * chips], refs[-1]
    height = parts[0].shape[0]
    for part, (chip, core) in zip(parts, part_owners(where_ref, chips)):
        row = pl.multiple_of((2 * chip + core) * height, height)
        out[0, pl.ds(row, height), :] = part[...].astype(F32)


def place(kernel, where, parts, part_blocks, out_shapes, out_block, grid, name, extra=()):
    return pl.pallas_call(
        kernel,
        grid_spec=pltpu.PrefetchScalarGridSpec(
            num_scalar_prefetch=1,
            grid=grid,
            in_specs=[pl.BlockSpec(*block) for block in part_blocks for _ in parts]
            + [pl.BlockSpec(v.shape, lambda i, where: (0, 0)) for v in extra],
            out_specs=[pl.BlockSpec(*out_block)] * len(out_shapes),
        ),
        out_shape=out_shapes,
        compiler_params=pltpu.CompilerParams(vmem_limit_bytes=VMEM_BYTES),
        cost_estimate=pl.CostEstimate(flops=8 * 550_000_000, bytes_accessed=1024, transcendentals=0),
        name=name,
    )(where, *(parts * len(part_blocks)), *extra)


def norm_stats(values):
    inv_root = lax.rsqrt(jnp.mean(values * values, axis=-1, keepdims=True) + EPS)
    return (inv_root, values * inv_root)


def norm_back(gradient, unit_rows, inv_root, gain):
    scaled = gain * gradient
    rows_part = inv_root * (scaled - unit_rows * jnp.mean(unit_rows * scaled, axis=-1, keepdims=True))
    return (rows_part, jnp.sum(gradient * unit_rows, axis=0))


def body(
    tokens, cotangent, live_counts, routes, norm_in, w_query, w_key, w_value, norm_query, norm_key, w_out, norm_mid,
    w_router, w_gate, w_up, w_down,
):
    chips, shards = lax.axis_size("chip"), lax.axis_size("shard")
    chip, core = lax.axis_index("chip"), lax.axis_index("core")
    rows_here, width = tokens.shape
    head_size = width // HEADS
    heads = HEADS // chips
    wide = heads * head_size
    experts, top = w_gate.shape[0], routes.shape[1]
    piece = rows_here // chips
    group_rows = rows_here * shards
    shard_rows = w_query.shape[0]
    half_rows = shard_rows // 2
    shard_hidden, hidden = w_down.shape[1], w_gate.shape[2]
    own_hidden = shard_hidden // (2 * chips)
    parts = 2 * shards
    heads_spread = HEADS // shards == chips
    fast = chips == 4 and own_hidden % 16 == 0 and heads_spread
    where = jnp.stack([chip, core]).astype(jnp.int32)
    owners = ("shard", "core")

    def from_owners(part):
        return lax.all_gather(part, owners, axis=0, tiled=True)

    def to_owners(total):
        return lax.psum_scatter(total, owners, scatter_dimension=0, tiled=True)

    with jax.named_scope("rehome_tokens"):
        token_parts = rehome_chips(tokens)

    head_ids = [i * chips + chip for i in range(heads)]
    with jax.named_scope("weights_qkv"):
        qkv_piece = jnp.concatenate(
            [
                lax.dynamic_slice(w, (core * half_rows, head * head_size), (half_rows, head_size))
                for w in (w_query, w_key, w_value)
                for head in head_ids
            ],
            axis=1,
        )
        qkv_w = from_owners(qkv_piece)
    route_columns = jnp.pad(routes.astype(BF16), ((0, 0), (0, 128 - top)))
    extended = jnp.concatenate([cotangent, route_columns], axis=1)
    small = jnp.concatenate(
        [v.astype(F32)[None] for v in (norm_in, norm_query, norm_key, norm_mid)] + [w_router.astype(F32).T], axis=0
    )
    extended, token_parts = tie(extended, token_parts)
    with jax.named_scope("norm_in"):
        inputs = rehome_planes(token_parts).astype(F32)
    with jax.named_scope("small_gathers"):
        small_all = exchange(jnp.broadcast_to(small[None], (shards,) + small.shape), "shard")
        small_all = small_all.transpose(1, 0, 2).reshape(small.shape[0], width)
        gain_in, gain_query, gain_key, gain_mid = (small_all[i] for i in range(4))
        router = jnp.pad(small_all[4:], ((0, 8 - experts), (0, 0))).astype(BF16)
        counts = lax.ppermute(
            live_counts,
            ("chip", "core", "shard"),
            [
                ((i * 2 + k) * shards + j, (j * 2 + k) * shards + i)
                for i in range(chips)
                for k in range(2)
                for j in range(shards)
            ],
        )[0]
    with jax.named_scope("rehome_cotangent"):
        cotangent_parts = exchange(extended.reshape(chips, piece, extended.shape[1]), "chip")
    hidden_at = 2 * chip * own_hidden
    with jax.named_scope("weights_gate_up"):
        unit = jnp.arange(parts * own_hidden, dtype=jnp.int32)
        wanted = (unit // (2 * own_hidden)) * shard_hidden + hidden_at + unit % (2 * own_hidden)
        choose = (jnp.arange(hidden, dtype=jnp.int32)[:, None] == wanted[None, :]).astype(BF16)
        gate_up_rows = [lax.dynamic_slice_in_dim(w, core * half_rows, half_rows, 1) for w in (w_gate, w_up)]
        gate_up_piece = jnp.concatenate(
            [dot(w[expert], choose).astype(BF16) for w in gate_up_rows for expert in range(experts)], axis=1
        )
    down_piece = lax.dynamic_slice_in_dim(w_down, hidden_at + core * own_hidden, own_hidden, 1)
    down_piece = down_piece.reshape(experts * own_hidden, width)
    if heads_spread:
        out_piece = lax.dynamic_slice_in_dim(w_out, chip * head_size + core * (head_size // 2), head_size // 2, 0)
    else:
        out_piece = lax.dynamic_slice_in_dim(w_out, core * half_rows, half_rows, 0)

    starts = jnp.cumsum(counts) - counts
    chip_of = chip ^ jnp.arange(chips, dtype=jnp.int32)
    in_block = (chip_of[:, None] * piece + jnp.arange(piece, dtype=jnp.int32)[None, :]).reshape(1, rows_here)
    positions = (starts[:, None] + in_block).reshape(group_rows)
    live = (in_block < counts[:, None]).reshape(group_rows)
    live_own = live.astype(F32).reshape(shards, chips, piece)[:, 0].reshape(rows_here, 1)
    half_size = head_size // 2
    frequency = THETA ** (-jnp.arange(half_size, dtype=F32) * 2.0 / head_size)
    phases = positions.astype(F32)[:, None] * frequency[None, :]
    cosine, sine = jnp.cos(phases), jnp.sin(phases)
    angles = (
        jnp.concatenate([cosine, cosine], axis=1),
        jnp.concatenate([-sine, sine], axis=1),
        positions[:, None],
        jnp.where(live, positions, FAR)[None, :],
    )

    with jax.named_scope("norm_in"):
        inv_in, unit_in = norm_stats(inputs)
        normed_own = (unit_in * gain_in).astype(BF16)
        normed_own, cotangent_parts = tie(normed_own, cotangent_parts)
    with jax.named_scope("rehome_cotangent"):
        extended = rehome_planes(cotangent_parts)
    with jax.named_scope("gather_normed"):
        normed = gather_first(normed_own)
        normed = gather_last(normed)
        *normed, qkv_w, out_piece, extended = tie(*normed, qkv_w, out_piece, extended)
    with jax.named_scope("weights_out"):
        out_w = from_owners(out_piece)
    with jax.named_scope("gather_upstream"):
        own_routes = extended[:, width : width + top]
        upstream_own = extended[:, :width].astype(F32) * live_own
        upstream = gather_first(jnp.concatenate([upstream_own.astype(BF16), extended[:, width:]], axis=1))
    with jax.named_scope("qkv"):
        lin, squares = run_project(normed, qkv_w, wide)
        inv_qk = lax.rsqrt(sum_rows(jnp.stack([squares[0], squares[8]], axis=0)) / width + EPS).T
        *upstream, inv_qk, out_w, gate_up_piece = tie(*upstream, inv_qk, out_w, gate_up_piece)
        upstream = gather_last(upstream)
    with jax.named_scope("weights_gate_up"):
        gate_up_w = from_owners(gate_up_piece)
    pick = (jnp.arange(HEADS, dtype=jnp.int32)[None, :] == jnp.stack(head_ids)[:, None]).astype(F32)

    def head_gain(gain):
        spread = gain.reshape(1, HEADS, head_size) * pick[:, :, None]
        return jnp.sum(spread, axis=1).reshape(1, wide)

    gains = (head_gain(gain_query), head_gain(gain_key))
    attention = (chips, heads, head_size, rows_here)
    mixed, *kept = run_attend_forward(lin, inv_qk, gains, angles, *attention)
    if not heads_spread:
        out_w = jnp.concatenate([lax.dynamic_slice_in_dim(out_w, h * head_size, head_size, 0) for h in head_ids], axis=0)
    with jax.named_scope("out_proj"):
        out_split = split_matmul(mixed, out_w, False, 6)
        upstream_full = jnp.concatenate(upstream, axis=0)
        upstream_full, *out_split = tie(upstream_full, *out_split)
        residual = inputs + scatter_chips(tuple(out_split))

    with jax.named_scope("gather_middle"):
        inv_mid, unit_mid = norm_stats(residual)
        middle_own = (unit_mid * gain_mid).astype(BF16)
        middle_own, gate_up_w, down_piece = tie(middle_own, gate_up_w, down_piece)
        middle = gather_last(gather_first(middle_own))
    with jax.named_scope("weights_down"):
        down_w = from_owners(down_piece).reshape(parts, experts, own_hidden, width)
        if not fast:
            down_w = down_w.transpose(1, 0, 2, 3).reshape(1, experts, parts * own_hidden, width)
    with jax.named_scope("router"):
        logits = dot_nt(router[:experts], middle_own)
        router_expo = jnp.exp(logits - jnp.max(logits, axis=0, keepdims=True))
        router_probs = router_expo / jnp.sum(router_expo, axis=0, keepdims=True)
        expert_ids = jnp.arange(experts, dtype=F32)
        chosen = jnp.sum(
            (own_routes.astype(F32).T[None, :, :] == expert_ids[:, None, None]).astype(F32), axis=1
        )
    with jax.named_scope("experts"):
        act, lin_grad, mix_grad = run_experts(middle, upstream, gate_up_w, down_w, router, experts, top)
        middle_split = split_matmul(lin_grad, gate_up_w, True, 14)

    with jax.named_scope("middle_grad"):
        *middle_split, mix_grad, act = tie(*middle_split, mix_grad, act)
        middle_first = scatter_first(tuple(middle_split))
        mix_grad_own = mix_grad[:rows_here].T
        for step in range(1, chips):
            part = mix_grad[step * rows_here : (step + 1) * rows_here].T
            mix_grad_own = mix_grad_own + swap(part, "chip", step)
        mix_grad_own = mix_grad_own[:experts]
    with jax.named_scope("w_down_grad"):
        if fast:
            down_total = run_down_grad(act, upstream_full, width, experts, parts)
        else:
            down_total = dot_tn(act, upstream_full[:, :width]).astype(BF16)
            down_total = down_total.reshape(experts, parts, own_hidden, width).transpose(1, 0, 2, 3)
        down_total = down_total.reshape(parts * experts * own_hidden, width)
        down_part = to_owners(down_total)
    with jax.named_scope("w_gate_up_grad"):
        gate_up_total = run_weight_grad(middle, lin_grad, 14)
    with jax.named_scope("middle_grad"):
        passed = scatter_pass(middle_first)
        *passed, gate_up_total = tie(*passed, gate_up_total)
        arrived = scatter_second(tuple(passed))
        prob_grad = mix_grad_own * chosen
        logit_grad = (router_probs * (prob_grad - jnp.sum(router_probs * prob_grad, axis=0, keepdims=True))).astype(BF16)
        middle_grad = scatter_sum(middle_first, arrived) + dot_tn(logit_grad, router[:experts])
        resid_part, gain_mid_grad = norm_back(middle_grad, unit_mid, inv_mid, gain_mid)
        resid_grad = upstream_own + resid_part
        branch_own = resid_grad.astype(BF16)
    with jax.named_scope("gather_branch"):
        branch = gather_first(branch_own)
        *branch, down_part, gate_up_total = tie(*branch, down_part, gate_up_total)
        gate_up_part = to_owners(gate_up_total)
    with jax.named_scope("output"):
        act, branch[0] = tie(act, branch[0])
        sum_split = split_matmul(act, down_w, False, 8)
    with jax.named_scope("mixed_grad"):
        branch = gather_last(branch)
        branch, sum_split = tie_lists(branch, sum_split)
        mixed_grad = run_back(branch, out_w, min(wide, 256))
        sum_first = scatter_first(tuple(sum_split))
    query_back, key_back, value_back, gain_grads, row_sums = run_attend_backward(
        mixed_grad, lin, kept, inv_qk, gains, angles, *attention
    )

    with jax.named_scope("qk_back"):
        *sum_first, row_sums = tie(*sum_first, row_sums)
        sum_first = tuple(sum_first)
        means = (sum_rows(jnp.stack([row_sums[0], row_sums[8]], axis=0)) / width).T
    with jax.named_scope("w_out_grad"):
        out_total = run_out_grad(mixed, branch)
        if not heads_spread:
            spread = jnp.zeros((width, width), BF16)
            for i, head in enumerate(head_ids):
                spread = lax.dynamic_update_slice_in_dim(
                    spread, out_total[i * head_size : (i + 1) * head_size], head * head_size, 0
                )
            out_total = spread
    with jax.named_scope("qk_back"):
        passed = scatter_pass(sum_first)
        *passed, means, out_total = tie(*passed, means, out_total)
        arrived = scatter_second(tuple(passed))
        qkv_grad = run_finish((query_back, key_back, value_back), lin, gains, inv_qk, means, rows_here)
    with jax.named_scope("output"):
        expert_sum = scatter_sum(sum_first, arrived)
        output_low = ((residual + expert_sum) * live_own).astype(BF16)
    with jax.named_scope("normed_grad"):
        normed_split = split_matmul(qkv_grad, qkv_w, True, 11)
        *normed_split, output_low, qkv_grad = tie(*normed_split, output_low, qkv_grad)
        normed_first = scatter_first(tuple(normed_split))
    with jax.named_scope("output"):
        output_parts = home_planes(output_low)
    with jax.named_scope("w_out_grad"):
        out_total, gate_up_part = tie(out_total, gate_up_part)
        out_part = to_owners(out_total)
    with jax.named_scope("w_qkv_grad"):
        qkv_total = run_weight_grad(normed, qkv_grad, 13)
    with jax.named_scope("normed_grad"):
        passed = scatter_pass(normed_first)
        *passed, qkv_total, output_parts = tie(*passed, qkv_total, output_parts)
        arrived = scatter_second(tuple(passed))
        normed_grad = scatter_sum(normed_first, arrived)
        input_part, gain_in_grad = norm_back(normed_grad, unit_in, inv_in, gain_in)
        input_low = (resid_grad + input_part).astype(BF16)
        output = home_chips(output_parts)
        input_low, out_part, qkv_total, output = tie(input_low, out_part, qkv_total, output)
        qkv_part = to_owners(qkv_total)
    with jax.named_scope("input_grad"):
        input_parts = home_planes(input_low)

    if fast:
        with jax.named_scope("plane_gathers"):
            wide_first = gather_first(jnp.concatenate([gate_up_part, down_part, out_part], axis=0))
            wide_first, (input_parts,) = tie_lists(wide_first, (input_parts,))
            wide_last = gather_last(wide_first)
    with jax.named_scope("small_grads"):
        router_grad = dot(logit_grad, middle_own)

        def spread_heads(which):
            by_head = gain_grads[8 * which].reshape(heads, 1, head_size) * pick[:, :, None]
            return jnp.sum(by_head, axis=0).reshape(1, width)

        small_grads = jnp.concatenate(
            [gain_in_grad[None], spread_heads(0), spread_heads(1), gain_mid_grad[None], router_grad], axis=0
        )
        by_owner = small_grads.reshape(small_grads.shape[0], shards, shard_rows).transpose(1, 0, 2)
        small_sum = sum_chips(jnp.sum(exchange(by_owner, "shard"), axis=0))
        small_sum = small_sum + swap(small_sum, "core", 1)

    def everywhere(part):
        return lax.all_gather(part, ("chip", "core"), axis=0, tiled=False).reshape((chips, 2) + part.shape)

    def plane_parts(pieces):
        own = list(pieces)
        if len(own) != chips:
            own = own[:1] + [jnp.concatenate(own[i : i + 2], axis=0) for i in range(1, len(own), 2)]
        return own + [swap(v, "core", 1) for v in own]

    def shapes(count, *shape):
        return [jax.ShapeDtypeStruct(shape, F32)] * count

    if fast:
        with jax.named_scope("plane_gathers"):
            wide_last, (input_parts, small_sum) = tie_lists(wide_last, (input_parts, small_sum))
            qkv_first = gather_first(qkv_part)
            wide_parts = plane_parts(wide_last)
        input_grad = home_chips(input_parts)
        with jax.named_scope("w_down_grad"):
            (w_down_grad,) = place(
                functools.partial(place_rows, chips), where, wide_parts,
                (((own_hidden, width), lambda i, where: (half_rows // own_hidden + i, 0)),),
                shapes(1, experts, shard_hidden, width),
                ((1, shard_hidden, width), lambda i, where: (i, 0, 0)),
                (experts,), "place_down",
            )
        with jax.named_scope("w_out_grad"):
            out_at = half_rows + experts * own_hidden
            (w_out_grad,) = place(
                functools.partial(place_rows, chips), where, wide_parts,
                (((head_size // 2, width // 4), lambda i, where: (out_at // (head_size // 2), i)),),
                shapes(1, 1, shard_rows, width),
                ((1, shard_rows, width // 4), lambda i, where: (0, 0, i)),
                (4,), "place_out",
            )
            w_out_grad = w_out_grad.reshape(shard_rows, width)
        with jax.named_scope("w_gate_up_grad"):
            columns = jnp.concatenate([wanted + 2 * own_hidden * ((chip ^ step) - chip) for step in range(chips)])
            order = (columns[:, None] == jnp.arange(hidden, dtype=jnp.int32)[None, :]).astype(BF16)
            tile = parts * own_hidden
            w_gate_grad, w_up_grad = place(
                functools.partial(place_hidden, chips), where, wide_parts,
                (
                    ((half_rows, tile), lambda i, where: (0, i)),
                    ((half_rows, tile), lambda i, where: (0, experts + i)),
                ),
                shapes(2, experts, 2, half_rows, hidden),
                ((1, 2, half_rows, hidden), lambda i, where: (i, 0, 0, 0)),
                (experts,), "place_gate_up", (order,),
            )
            w_gate_grad = w_gate_grad.reshape(experts, shard_rows, hidden)
            w_up_grad = w_up_grad.reshape(experts, shard_rows, hidden)
        with jax.named_scope("w_qkv_grad"):
            tile = 64

            qkv_first, (w_down_grad, w_out_grad, w_gate_grad, w_up_grad) = tie_lists(
                qkv_first, (w_down_grad, w_out_grad, w_gate_grad, w_up_grad)
            )
            qkv_parts, (input_grad,) = tie_lists(plane_parts(gather_last(qkv_first)), (input_grad,))
            w_query_grad, w_key_grad, w_value_grad = (
                v.reshape(shard_rows, width)
                for v in place(
                    functools.partial(place_heads, chips, heads, head_size), where, qkv_parts,
                    (((tile, 3 * wide), lambda i, where: (i, 0)),),
                    shapes(3, 2, half_rows, width),
                    ((2, tile, width), lambda i, where: (0, i, 0)),
                    (half_rows // tile,), "place_heads",
                )
            )
    else:
        input_grad = home_chips(input_parts)
        spread = everywhere(down_part).reshape(chips, 2, experts, own_hidden, width)
        w_down_grad = spread.transpose(2, 0, 1, 3, 4).reshape(experts, shard_hidden, width).astype(F32)
        spread = everywhere(gate_up_part).reshape(chips, 2, half_rows, 2, experts, shards, 2 * own_hidden)
        spread = spread.transpose(3, 4, 1, 2, 5, 0, 6).reshape(2, experts, shard_rows, hidden).astype(F32)
        w_gate_grad, w_up_grad = spread[0], spread[1]
        if heads_spread:
            w_out_grad = everywhere(out_part).reshape(shard_rows, width).astype(F32)
        else:
            spread = lax.psum(out_part.astype(F32), "chip")
            w_out_grad = lax.all_gather(spread, "core", axis=0, tiled=True)

        def heads_back(part, count):
            spread = everywhere(part).reshape(chips, 2, half_rows, count, heads, head_size)
            return spread.transpose(3, 1, 2, 4, 0, 5).reshape(count, shard_rows, width).astype(F32)

        w_query_grad, w_key_grad, w_value_grad = heads_back(qkv_part, 3)
    return (
        output,
        input_grad,
        small_sum[0],
        w_query_grad,
        w_key_grad,
        w_value_grad,
        small_sum[1],
        small_sum[2],
        w_out_grad,
        small_sum[3],
        small_sum[4:].T,
        w_gate_grad,
        w_up_grad,
        w_down_grad,
    )


def solution(mesh):
    reps, shards = mesh.devices.shape
    split = Mesh(mesh.devices.reshape(reps // 2, 2, shards), ("chip", "core", "shard"))
    rows = P(("chip", "core", "shard"), None)
    first, second = P("shard", None), P(None, "shard", None)
    gain = P("shard")
    in_specs = (
        rows, rows, P(("chip", "core"), None), rows, gain, first, first, first, gain, gain, first, gain, first,
        second, second, second,
    )
    out_specs = (rows, rows, gain, first, first, first, gain, gain, first, gain, first, second, second, second)
    return jax.shard_map(body, mesh=split, in_specs=in_specs, out_specs=out_specs, check_vma=False)
```

```python
import functools

import jax
import jax.numpy as jnp
from jax import lax
from jax.experimental import pallas as pl
from jax.experimental.pallas import tpu as pltpu
from jax.sharding import Mesh
from jax.sharding import PartitionSpec as P

HEADS = 16
EPS = 1e-05
THETA = 10000.0
MASKED = -1e30
FAR = 1 << 30
F32 = jnp.float32
BF16 = jnp.bfloat16
VMEM_BYTES = 56 * 1024 * 1024


def dot(left, right):
    return jnp.dot(left, right, preferred_element_type=F32)


def dot_nt(left, right):
    return lax.dot_general(left, right, (((1,), (1,)), ((), ())), preferred_element_type=F32)


def dot_tn(left, right):
    return lax.dot_general(left, right, (((0,), (0,)), ((), ())), preferred_element_type=F32)


def tie(*values):
    return lax.optimization_barrier(values)


def tie_lists(*lists):
    return lax.optimization_barrier([list(values) for values in lists])


def swap(value, axis, step):
    size = lax.axis_size(axis)
    return lax.ppermute(value, axis, [(i, i ^ step) for i in range(size)])


def exchange(parts, axis):
    me = lax.axis_index(axis)
    out = parts
    for step in range(1, lax.axis_size(axis)):
        sent = lax.dynamic_index_in_dim(parts, me ^ step, 0, keepdims=True)
        out = lax.dynamic_update_slice_in_dim(out, swap(sent, axis, step), me ^ step, 0)
    return out


def gather_first(block):
    chips = lax.axis_size("chip")
    if chips != 4:
        return [block] + [swap(block, "chip", step) for step in range(1, chips)]
    half = block.shape[0] // 2
    top, low = block[:half], block[half:]
    two_top, one_low = swap(top, "chip", 2), swap(low, "chip", 1)
    one_top, two_low = swap(top, "chip", 1), swap(low, "chip", 2)
    return [block, one_top, one_low, two_top, two_low]


def gather_last(pieces):
    if lax.axis_size("chip") != 4:
        return pieces
    return pieces + [swap(pieces[3], "chip", 1), swap(pieces[2], "chip", 2)]


def scatter_first(split):
    if len(split) == 2:
        return split
    own_left, own_right, to_one, to_two, keep_left, keep_right = split
    return (own_left, own_right, swap(to_one, "chip", 1), swap(to_two, "chip", 2), keep_left, keep_right)


def scatter_pass(first):
    if len(first) == 2:
        return (first[1][0],)
    _, _, from_one, from_two, keep_left, keep_right = first
    return (
        (keep_left.astype(F32) + from_one[1].astype(F32)).astype(BF16),
        (keep_right.astype(F32) + from_two[1].astype(F32)).astype(BF16),
    )


def scatter_second(passed):
    if len(passed) == 1:
        return list(passed)
    return [swap(passed[0], "chip", 2), swap(passed[1], "chip", 1)]


def scatter_sum(first, arrived):
    if len(first) == 2:
        own, others = first
        for step, other in enumerate(tuple(arrived) + tuple(others[1:])):
            own = own + swap(other, "chip", step + 1).astype(F32)
        return own
    own_left, own_right, from_one, from_two, _, _ = first
    return jnp.concatenate(
        [
            own_left + from_one[0].astype(F32) + arrived[0].astype(F32),
            own_right + from_two[0].astype(F32) + arrived[1].astype(F32),
        ],
        axis=1,
    )


def scatter_chips(split):
    first = scatter_first(split)
    return scatter_sum(first, scatter_second(scatter_pass(first)))


def sum_chips(value):
    step = 1
    while step < lax.axis_size("chip"):
        value = value + swap(value, "chip", step)
        step *= 2
    return value


def sum_rows(values):
    chips = lax.axis_size("chip")
    total = values.reshape(values.shape[0], chips, -1)
    step = 1
    while step < chips:
        other = swap(total, "chip", step)
        total = total + jnp.concatenate([other[:, i ^ step : (i ^ step) + 1] for i in range(chips)], axis=1)
        step *= 2
    return total.reshape(values.shape)


def rehome_chips(rows):
    chips = lax.axis_size("chip")
    parts = rows.reshape(chips, rows.shape[0] // chips, rows.shape[1])
    return lax.all_to_all(parts, "chip", 0, 0, tiled=True)


def rehome_planes(parts):
    return lax.all_to_all(parts, "shard", 0, 0, tiled=True).reshape(-1, parts.shape[2])


def home_planes(rows):
    shards = lax.axis_size("shard")
    parts = rows.reshape(shards, rows.shape[0] // shards, rows.shape[1])
    return lax.all_to_all(parts, "shard", 0, 0, tiled=True)


def home_chips(parts):
    return lax.all_to_all(parts, "chip", 0, 0, tiled=True).reshape(-1, parts.shape[2])


ANYWHERE = pl.BlockSpec(memory_space=pl.ANY)


def run(kernel, name, micros, grid, in_specs, out_specs, out_shape, args, scratch=()):
    return pl.pallas_call(
        kernel,
        grid=grid,
        in_specs=in_specs,
        out_specs=out_specs,
        out_shape=out_shape,
        scratch_shapes=list(scratch),
        compiler_params=pltpu.CompilerParams(vmem_limit_bytes=VMEM_BYTES),
        cost_estimate=pl.CostEstimate(flops=micros * 550_000_000, bytes_accessed=1024, transcendentals=0),
        name=name,
    )(*args)


def load_rows(pieces, target, sems):
    copies, at = [], 0
    for i, piece in enumerate(pieces):
        copies.append(pltpu.make_async_copy(piece, target.at[pl.ds(at, piece.shape[0]), :], sems.at[i]))
        at += piece.shape[0]
    for copy in copies:
        copy.start()
    for copy in copies:
        copy.wait()


def rows_scratch(pieces):
    rows = sum(piece.shape[0] for piece in pieces)
    return [pltpu.VMEM((rows, pieces[0].shape[1]), BF16), pltpu.SemaphoreType.DMA((len(pieces),))]


def column_sums(values):
    ones = jnp.ones((8, values.shape[1]), F32)
    return lax.dot_general(
        ones, values, (((1,), (1,)), ((), ())), precision=lax.Precision.HIGHEST, preferred_element_type=F32
    )


def project_kernel(count, *refs):
    pieces, (weight, out, squares, rows, sems) = refs[:count], refs[count:]

    @pl.when(pl.program_id(0) == 0)
    def _():
        load_rows(pieces, rows, sems)

    result = dot(rows[...], weight[...])
    out[...] = result
    squares[...] = column_sums(result * result)


def run_project(pieces, weight, tile):
    depth, columns = weight.shape
    rows = sum(piece.shape[0] for piece in pieces)
    steps = columns // tile
    return run(
        functools.partial(project_kernel, len(pieces)), "project", 16, (steps,),
        [ANYWHERE] * len(pieces) + [pl.BlockSpec((depth, tile), lambda i: (0, i))],
        [pl.BlockSpec((rows, tile), lambda i: (0, i)), pl.BlockSpec((8, rows), lambda i: (i, 0))],
        [jax.ShapeDtypeStruct((rows, columns), F32), jax.ShapeDtypeStruct((8 * steps, rows), F32)],
        (*pieces, weight),
        rows_scratch(pieces),
    )


def back_kernel(count, *refs):
    pieces, (weight, out, rows, sems) = refs[:count], refs[count:]

    @pl.when(pl.program_id(0) == 0)
    def _():
        load_rows(pieces, rows, sems)

    out[...] = dot_nt(rows[...], weight[...]).astype(BF16)


def run_back(pieces, weight, tile):
    rows = sum(piece.shape[0] for piece in pieces)
    return run(
        functools.partial(back_kernel, len(pieces)), "back", 7, (weight.shape[0] // tile,),
        [ANYWHERE] * len(pieces) + [pl.BlockSpec((tile, weight.shape[1]), lambda i: (i, 0))],
        pl.BlockSpec((rows, tile), lambda i: (0, i)),
        jax.ShapeDtypeStruct((rows, weight.shape[0]), BF16),
        (*pieces, weight),
        rows_scratch(pieces),
    )


def join_experts(ref):
    parts, experts, units, columns = ref.shape
    if parts == 1:
        return ref[...].reshape(experts * units, columns)
    return jnp.concatenate([ref[:, expert].reshape(parts * units, columns) for expert in range(experts)], axis=0)


def split_kernel(block, turned, left, left_w, right_w, own_left, own_right, to_one, to_two, keep_left, keep_right):
    def product(weight):
        if turned:
            return dot_nt(left[...], weight[...])
        return dot(left[...], weight[...] if len(weight.shape) == 2 else join_experts(weight))

    result = product(left_w)
    own_left[...] = result[:block]
    to_one[0] = result[block : 2 * block].astype(BF16)
    keep_left[...] = result[2 * block : 3 * block].astype(BF16)
    to_one[1] = result[3 * block :].astype(BF16)
    result = product(right_w)
    own_right[...] = result[:block]
    keep_right[...] = result[block : 2 * block].astype(BF16)
    to_two[0] = result[2 * block : 3 * block].astype(BF16)
    to_two[1] = result[3 * block :].astype(BF16)


def split_matmul(left, weight, turned, micros):
    chips = lax.axis_size("chip")
    rows = left.shape[0]
    block = rows // chips
    width = weight.shape[0] if turned else weight.shape[-1]
    if chips != 4:
        if weight.ndim == 4:
            weight = weight.transpose(1, 0, 2, 3).reshape(-1, width)
        whole = (dot_nt if turned else dot)(left, weight)
        return (whole[:block], [whole[i * block : (i + 1) * block].astype(BF16) for i in range(1, chips)])
    half, tile = width // 2, 256
    steps = half // tile

    def weight_spec(first):
        if turned:
            return pl.BlockSpec((tile, weight.shape[1]), lambda i: (first + i, 0))
        return pl.BlockSpec((*weight.shape[:-1], tile), lambda i: (0,) * (weight.ndim - 1) + (first + i,))

    one = pl.BlockSpec((block, tile), lambda i: (0, i))
    two = pl.BlockSpec((2, block, tile), lambda i: (0, 0, i))
    wide, low = jax.ShapeDtypeStruct((block, half), F32), jax.ShapeDtypeStruct((block, half), BF16)
    pair = jax.ShapeDtypeStruct((2, block, half), BF16)
    return run(
        functools.partial(split_kernel, block, turned), "split_matmul", micros, (steps,),
        [pl.BlockSpec(left.shape, lambda i: (0, 0)), weight_spec(0), weight_spec(steps)],
        [one, one, two, two, one, one],
        [wide, wide, pair, pair, low, low],
        (left, weight, weight),
    )


def weight_grad_kernel(count, tile, *refs):
    pieces, (grad, out, rows, sems) = refs[:count], refs[count:]

    @pl.when(pl.program_id(0) == 0)
    def _():
        load_rows(pieces, rows, sems)

    columns = pl.ds(pl.multiple_of(pl.program_id(0) * tile, tile), tile)
    out[...] = dot_tn(rows[:, columns], grad[...]).astype(BF16)


def run_weight_grad(pieces, grad, micros, columns=None):
    tile = 512
    depth, columns = pieces[0].shape[1], columns or grad.shape[1]
    return run(
        functools.partial(weight_grad_kernel, len(pieces), tile), "weight_grad", micros, (depth // tile,),
        [ANYWHERE] * len(pieces) + [pl.BlockSpec((grad.shape[0], columns), lambda i: (0, 0))],
        pl.BlockSpec((tile, columns), lambda i: (i, 0)),
        jax.ShapeDtypeStruct((depth, columns), BF16),
        (*pieces, grad),
        rows_scratch(pieces),
    )


def down_grad_kernel(experts, parts, act, upstream, out):
    result = dot_tn(act[...], upstream[...]).astype(BF16)
    own = result.shape[0] // (experts * parts)
    for expert in range(experts):
        for part in range(parts):
            at = (expert * parts + part) * own
            out[part, expert * own : (expert + 1) * own, :] = result[at : at + own]


def run_down_grad(act, upstream, width, experts, parts):
    hidden, tile = act.shape[1], 512
    return run(
        functools.partial(down_grad_kernel, experts, parts), "down_grad", 9, (width // tile,),
        [pl.BlockSpec(act.shape, lambda i: (0, 0)), pl.BlockSpec((upstream.shape[0], tile), lambda i: (0, i))],
        pl.BlockSpec((parts, hidden // parts, tile), lambda i: (0, 0, i)),
        jax.ShapeDtypeStruct((parts, hidden // parts, width), BF16),
        (act, upstream),
    )


def out_grad_kernel(count, tile, *refs):
    pieces, (mixed, out, rows, sems) = refs[:count], refs[count:]

    @pl.when(pl.program_id(0) == 0)
    def _():
        load_rows(pieces, rows, sems)

    columns = pl.ds(pl.multiple_of(pl.program_id(0) * tile, tile), tile)
    out[...] = dot_tn(mixed[...], rows[:, columns]).astype(BF16)


def run_out_grad(mixed, pieces):
    tile, width = 512, pieces[0].shape[1]
    return run(
        functools.partial(out_grad_kernel, len(pieces), tile), "out_grad", 7, (width // tile,),
        [ANYWHERE] * len(pieces) + [pl.BlockSpec(mixed.shape, lambda i: (0, 0))],
        pl.BlockSpec((mixed.shape[1], tile), lambda i: (0, i)),
        jax.ShapeDtypeStruct((mixed.shape[1], width), BF16),
        (*pieces, mixed),
        rows_scratch(pieces),
    )


def lane_roll(values):
    return pltpu.roll(values, values.shape[1] // 2, 1)


def take_block(ref, block, chips, block_rows):
    piece = block_rows // chips
    at = lambda chip: chip * block_rows + block * piece
    return jnp.concatenate([ref[at(chip) : at(chip) + piece, :] for chip in range(chips)], axis=0)


def put_block(ref, block, chips, block_rows, values):
    piece = block_rows // chips
    for chip in range(chips):
        at = chip * block_rows + block * piece
        ref[at : at + piece, :] = values[chip * piece : (chip + 1) * piece]


def attend_forward(
    chips, block_rows, scale,
    query_ref, key_ref, value_ref, inv_ref, gain_q, gain_k, cos_ref, sin_ref, pos_ref, key_pos_ref,
    mixed, query_rot, key_rot, value_low, lse,
):
    blocks = inv_ref.shape[0] // block_rows
    for block in range(blocks):
        rows = pl.ds(block * block_rows, block_rows)
        cosine, sine = cos_ref[rows, :], sin_ref[rows, :]
        inv = take_block(inv_ref, block, chips, block_rows)
        query = take_block(query_ref, block, chips, block_rows) * inv[:, 0:1] * gain_q[...]
        query_rot[rows, :] = (query * cosine + lane_roll(query) * sine).astype(BF16)
        key = take_block(key_ref, block, chips, block_rows) * inv[:, 1:2] * gain_k[...]
        key_rot[rows, :] = (key * cosine + lane_roll(key) * sine).astype(BF16)
        value_low[rows, :] = take_block(value_ref, block, chips, block_rows).astype(BF16)
    for block in range(blocks):
        rows = pl.ds(block * block_rows, block_rows)
        seen = pl.ds(0, (block + 1) * block_rows)
        scores = dot_nt(query_rot[rows, :], key_rot[seen, :]) * scale
        scores = jnp.where(key_pos_ref[:, seen] <= pos_ref[rows, :], scores, MASKED)
        peak = jnp.max(scores, axis=-1, keepdims=True)
        expo = jnp.exp(scores - peak)
        total = jnp.sum(expo, axis=-1, keepdims=True)
        probs_low = (expo * (1.0 / total)).astype(BF16)
        put_block(mixed, block, chips, block_rows, dot(probs_low, value_low[seen, :]).astype(BF16))
        lse[rows, :] = jnp.broadcast_to(peak + jnp.log(total), (block_rows, lse.shape[1]))


def attend_backward(
    chips, block_rows, scale,
    grad_ref, query_ref, key_ref, query_rot, key_rot, value_low, lse, gain_q, gain_k,
    inv_ref, cos_ref, sin_ref, pos_ref, key_pos_ref,
    query_back, key_back, value_back, gains, sums_ref,
    key_sum, value_sum,
):
    blocks = inv_ref.shape[0] // block_rows

    @pl.when(pl.program_id(0) == 0)
    def _():
        sums_ref[...] = jnp.zeros_like(sums_ref)

    key_sum[...] = jnp.zeros_like(key_sum)
    value_sum[...] = jnp.zeros_like(value_sum)
    for block in range(blocks):
        rows = pl.ds(block * block_rows, block_rows)
        seen = pl.ds(0, (block + 1) * block_rows)
        query = query_rot[rows, :]
        grad = take_block(grad_ref, block, chips, block_rows)
        scores = dot_nt(query, key_rot[seen, :]) * scale
        scores = jnp.where(key_pos_ref[:, seen] <= pos_ref[rows, :], scores, MASKED)
        probs = jnp.exp(scores - lse[rows, 0:1])
        probs_grad = dot_nt(grad, value_low[seen, :])
        weighted = jnp.sum(probs * probs_grad, axis=-1, keepdims=True)
        score_grad = (probs * (probs_grad - weighted)).astype(BF16)
        query_grad = dot(score_grad, key_rot[seen, :]) * scale
        turned = query_grad * cos_ref[rows, :] - lane_roll(query_grad) * sin_ref[rows, :]
        put_block(query_back, block, chips, block_rows, turned)
        key_sum[seen, :] += dot_tn(score_grad, query)
        value_sum[seen, :] += dot_tn(probs.astype(BF16), grad)
    for block in range(blocks):
        rows = pl.ds(block * block_rows, block_rows)
        key_grad = key_sum[rows, :] * scale
        turned = key_grad * cos_ref[rows, :] - lane_roll(key_grad) * sin_ref[rows, :]
        put_block(key_back, block, chips, block_rows, turned)
        put_block(value_back, block, chips, block_rows, value_sum[rows, :].astype(BF16))
    for which, (lin, back, gain) in enumerate(((query_ref, query_back, gain_q), (key_ref, key_back, gain_k))):
        product = back[...] * lin[...] * inv_ref[:, which : which + 1]
        sums_ref[pl.ds(8 * which, 8), :] += column_sums(product * gain[...])
        gains[pl.ds(8 * which, 8), :] = jnp.broadcast_to(jnp.sum(product, axis=0, keepdims=True), (8, product.shape[1]))


def attention_specs(rows, head_size, heads):
    column = pl.BlockSpec((rows, head_size), lambda h: (0, h))
    whole = lambda shape: pl.BlockSpec(shape, lambda h: (0, 0))
    part = [pl.BlockSpec((rows, head_size), lambda h, which=which: (0, which * heads + h)) for which in range(3)]
    gain = pl.BlockSpec((1, head_size), lambda h: (0, h))
    return column, whole, part, gain


def run_attend_forward(lin, inv, gains, angles, chips, heads, head_size, block_rows):
    rows, wide = lin.shape[0], heads * head_size
    column, whole, part, gain = attention_specs(rows, head_size, heads)
    low = jax.ShapeDtypeStruct((rows, wide), BF16)
    return run(
        functools.partial(attend_forward, chips, block_rows, head_size**-0.5), "attend_forward", 17, (heads,),
        part + [whole(inv.shape), gain, gain] + [whole(v.shape) for v in angles],
        [column] * 5,
        [low, low, low, low, jax.ShapeDtypeStruct((rows, wide), F32)],
        (lin, lin, lin, inv, *gains, *angles),
    )


def run_attend_backward(mixed_grad, lin, kept, inv, gains, angles, chips, heads, head_size, block_rows):
    rows, wide = mixed_grad.shape
    column, whole, part, gain = attention_specs(rows, head_size, heads)
    full = jax.ShapeDtypeStruct((rows, wide), F32)
    return run(
        functools.partial(attend_backward, chips, block_rows, head_size**-0.5), "attend_backward", 20, (heads,),
        [column, part[0], part[1]] + [column] * 4 + [gain, gain, whole(inv.shape)] + [whole(v.shape) for v in angles],
        [column] * 3 + [pl.BlockSpec((16, head_size), lambda h: (0, h)), whole((16, rows))],
        [full, full, jax.ShapeDtypeStruct((rows, wide), BF16), jax.ShapeDtypeStruct((16, wide), F32),
         jax.ShapeDtypeStruct((16, rows), F32)],
        (mixed_grad, lin, lin, *kept, *gains, inv, *angles),
        [pltpu.VMEM((rows, head_size), F32)] * 2,
    )


def finish_kernel(wide, query_back, key_back, value_back, lin, gain_q, gain_k, inv_ref, mean_ref, out):
    for which, (back, gain) in enumerate(((query_back, gain_q), (key_back, gain_k))):
        inv = inv_ref[:, which : which + 1]
        columns = slice(which * wide, (which + 1) * wide)
        unit = lin[:, columns] * inv
        out[:, columns] = (inv * (gain[...] * back[...] - unit * mean_ref[:, which : which + 1])).astype(BF16)
    out[:, 2 * wide :] = value_back[...]


def run_finish(backs, lin, gains, inv, means, tile):
    rows, wide = backs[0].shape
    spec = lambda columns: pl.BlockSpec((tile, columns), lambda i: (i, 0))
    gain = pl.BlockSpec((1, wide), lambda i: (0, 0))
    return run(
        functools.partial(finish_kernel, wide), "finish", 7, (rows // tile,),
        [spec(wide)] * 3 + [spec(3 * wide), gain, gain, spec(2), spec(2)],
        spec(3 * wide),
        jax.ShapeDtypeStruct((rows, 3 * wide), BF16),
        (*backs, lin, *gains, inv, means),
    )


def experts_kernel(count, experts, top, *refs):
    middles, upstreams, refs = refs[:count], refs[count : 2 * count], refs[2 * count :]
    gate_w, up_w, down_w, router_w, act_out, grad_out, mix_grad, middle, upstream, mix, middle_sems, upstream_sems = refs
    step, tile = pl.program_id(0), gate_w.shape[1]
    rows, depth = middle.shape
    lane = lax.broadcasted_iota(jnp.int32, (1, mix.shape[1]), 1)

    @pl.when(step == 0)
    def _():
        load_rows(middles, middle, middle_sems)
        load_rows(upstreams, upstream, upstream_sems)
        mix_grad[...] = jnp.zeros_like(mix_grad)
        logits = jnp.where(lane < experts, dot_nt(middle[...], router_w[...]), MASKED)
        expo = jnp.exp(logits - jnp.max(logits, axis=-1, keepdims=True))
        chosen = jnp.zeros_like(expo)
        for i in range(top):
            route = upstream[:, depth + i : depth + i + 1].astype(F32)
            chosen = chosen + jnp.where(route == lane.astype(F32), 1.0, 0.0)
        mix[...] = expo / jnp.sum(expo, axis=-1, keepdims=True) * chosen

    mine = lane == step
    mix_column = jnp.sum(jnp.where(mine, mix[...], 0.0), axis=-1, keepdims=True)
    gate = dot(middle[...], gate_w[...])
    up = dot(middle[...], up_w[...])
    back = dot_nt(upstream[:, :depth], down_w[...].reshape(tile, depth))
    sigma = 1.0 / (1.0 + jnp.exp(-gate))
    silu = gate * sigma
    act = silu * up
    mix_grad[...] += jnp.where(mine, jnp.sum(act * back, axis=-1, keepdims=True), 0.0)
    back = back * mix_column
    act_out[...] = (act * mix_column).astype(BF16)
    columns = pl.ds(pl.multiple_of(step * tile, tile), tile)
    up_columns = pl.ds(pl.multiple_of((experts + step) * tile, tile), tile)
    grad_out[:, columns] = (back * up * sigma * (1.0 + gate * (1.0 - sigma))).astype(BF16)
    grad_out[:, up_columns] = (back * silu).astype(BF16)


def run_experts(middles, upstreams, gate_up, down, router, experts, top):
    rows, depth = sum(piece.shape[0] for piece in middles), middles[0].shape[1]
    parts, _, units, _ = down.shape
    tile = parts * units
    whole = lambda shape: pl.BlockSpec(shape, lambda i: (0, 0))
    grad_shape, mix_shape = (rows, 2 * experts * tile), (rows, router.shape[0])
    buffers, sems = zip(rows_scratch(middles), rows_scratch(upstreams))
    return run(
        functools.partial(experts_kernel, len(middles), experts, top), "experts", 26, (experts,),
        [ANYWHERE] * (2 * len(middles))
        + [
            pl.BlockSpec((depth, tile), lambda i: (0, i)),
            pl.BlockSpec((depth, tile), lambda i: (0, experts + i)),
            pl.BlockSpec((parts, 1, units, depth), lambda i: (0, i, 0, 0)),
            whole(router.shape),
        ],
        [pl.BlockSpec((rows, tile), lambda i: (0, i)), whole(grad_shape), whole(mix_shape)],
        [
            jax.ShapeDtypeStruct((rows, experts * tile), BF16),
            jax.ShapeDtypeStruct(grad_shape, BF16),
            jax.ShapeDtypeStruct(mix_shape, F32),
        ],
        (*middles, *upstreams, gate_up, gate_up, down, router),
        [*buffers, pltpu.VMEM(mix_shape, F32), *sems],
    )


def part_owners(where_ref, chips):
    return [(where_ref[0] ^ step, where_ref[1] ^ turn) for turn in range(2) for step in range(chips)]


def place_heads(chips, heads, head_size, where_ref, *refs):
    parts, outs = refs[: 2 * chips], refs[2 * chips :]
    for part, (chip, core) in zip(parts, part_owners(where_ref, chips)):
        for which, out in enumerate(outs):
            for i in range(heads):
                first = (which * heads + i) * head_size
                column = pl.multiple_of((i * chips + chip) * head_size, head_size)
                out[core, :, pl.ds(column, head_size)] = part[:, first : first + head_size].astype(F32)


def place_hidden(chips, where_ref, *refs):
    count = 2 * chips
    order, outs = refs[2 * count], refs[2 * count + 1 :]
    owners = part_owners(where_ref, chips)
    for which, out in enumerate(outs):
        parts = refs[which * count : (which + 1) * count]
        for turn in range(2):
            row = jnp.concatenate([part[...] for part in parts[turn * chips : (turn + 1) * chips]], axis=1)
            out[0, owners[turn * chips][1]] = dot(row, order[...])


def place_rows(chips, where_ref, *refs):
    parts, out = refs[: 2 * chips], refs[-1]
    height = parts[0].shape[0]
    for part, (chip, core) in zip(parts, part_owners(where_ref, chips)):
        row = pl.multiple_of((2 * chip + core) * height, height)
        out[0, pl.ds(row, height), :] = part[...].astype(F32)


def place(kernel, where, parts, part_blocks, out_shapes, out_block, grid, name, extra=()):
    return pl.pallas_call(
        kernel,
        grid_spec=pltpu.PrefetchScalarGridSpec(
            num_scalar_prefetch=1,
            grid=grid,
            in_specs=[pl.BlockSpec(*block) for block in part_blocks for _ in parts]
            + [pl.BlockSpec(v.shape, lambda i, where: (0, 0)) for v in extra],
            out_specs=[pl.BlockSpec(*out_block)] * len(out_shapes),
        ),
        out_shape=out_shapes,
        compiler_params=pltpu.CompilerParams(vmem_limit_bytes=VMEM_BYTES),
        cost_estimate=pl.CostEstimate(flops=8 * 550_000_000, bytes_accessed=1024, transcendentals=0),
        name=name,
    )(where, *(parts * len(part_blocks)), *extra)


def norm_stats(values):
    inv_root = lax.rsqrt(jnp.mean(values * values, axis=-1, keepdims=True) + EPS)
    return (inv_root, values * inv_root)


def norm_back(gradient, unit_rows, inv_root, gain):
    scaled = gain * gradient
    rows_part = inv_root * (scaled - unit_rows * jnp.mean(unit_rows * scaled, axis=-1, keepdims=True))
    return (rows_part, jnp.sum(gradient * unit_rows, axis=0))


def body(
    tokens, cotangent, live_counts, routes, norm_in, w_query, w_key, w_value, norm_query, norm_key, w_out, norm_mid,
    w_router, w_gate, w_up, w_down,
):
    chips, shards = lax.axis_size("chip"), lax.axis_size("shard")
    chip, core = lax.axis_index("chip"), lax.axis_index("core")
    rows_here, width = tokens.shape
    head_size = width // HEADS
    heads = HEADS // chips
    wide = heads * head_size
    experts, top = w_gate.shape[0], routes.shape[1]
    piece = rows_here // chips
    group_rows = rows_here * shards
    shard_rows = w_query.shape[0]
    half_rows = shard_rows // 2
    shard_hidden, hidden = w_down.shape[1], w_gate.shape[2]
    own_hidden = shard_hidden // (2 * chips)
    parts = 2 * shards
    heads_spread = HEADS // shards == chips
    fast = chips == 4 and own_hidden % 16 == 0 and heads_spread
    where = jnp.stack([chip, core]).astype(jnp.int32)
    owners = ("shard", "core")

    def from_owners(part):
        return lax.all_gather(part, owners, axis=0, tiled=True)

    def to_owners(total):
        return lax.psum_scatter(total, owners, scatter_dimension=0, tiled=True)

    with jax.named_scope("rehome_tokens"):
        token_parts = rehome_chips(tokens)

    head_ids = [i * chips + chip for i in range(heads)]
    with jax.named_scope("weights_qkv"):
        qkv_piece = jnp.concatenate(
            [
                lax.dynamic_slice(w, (core * half_rows, head * head_size), (half_rows, head_size))
                for w in (w_query, w_key, w_value)
                for head in head_ids
            ],
            axis=1,
        )
        qkv_w = from_owners(qkv_piece)
    route_columns = jnp.pad(routes.astype(BF16), ((0, 0), (0, 128 - top)))
    extended = jnp.concatenate([cotangent, route_columns], axis=1)
    small = jnp.concatenate(
        [v.astype(F32)[None] for v in (norm_in, norm_query, norm_key, norm_mid)] + [w_router.astype(F32).T], axis=0
    )
    extended, token_parts = tie(extended, token_parts)
    with jax.named_scope("norm_in"):
        inputs = rehome_planes(token_parts).astype(F32)
    with jax.named_scope("small_gathers"):
        small_all = exchange(jnp.broadcast_to(small[None], (shards,) + small.shape), "shard")
        small_all = small_all.transpose(1, 0, 2).reshape(small.shape[0], width)
        gain_in, gain_query, gain_key, gain_mid = (small_all[i] for i in range(4))
        router = jnp.pad(small_all[4:], ((0, 8 - experts), (0, 0))).astype(BF16)
        counts = lax.ppermute(
            live_counts,
            ("chip", "core", "shard"),
            [
                ((i * 2 + k) * shards + j, (j * 2 + k) * shards + i)
                for i in range(chips)
                for k in range(2)
                for j in range(shards)
            ],
        )[0]
    with jax.named_scope("rehome_cotangent"):
        cotangent_parts = exchange(extended.reshape(chips, piece, extended.shape[1]), "chip")
    hidden_at = 2 * chip * own_hidden
    with jax.named_scope("weights_gate_up"):
        unit = jnp.arange(parts * own_hidden, dtype=jnp.int32)
        wanted = (unit // (2 * own_hidden)) * shard_hidden + hidden_at + unit % (2 * own_hidden)
        choose = (jnp.arange(hidden, dtype=jnp.int32)[:, None] == wanted[None, :]).astype(BF16)
        gate_up_rows = [lax.dynamic_slice_in_dim(w, core * half_rows, half_rows, 1) for w in (w_gate, w_up)]
        gate_up_piece = jnp.concatenate(
            [dot(w[expert], choose).astype(BF16) for w in gate_up_rows for expert in range(experts)], axis=1
        )
    down_piece = lax.dynamic_slice_in_dim(w_down, hidden_at + core * own_hidden, own_hidden, 1)
    down_piece = down_piece.reshape(experts * own_hidden, width)
    if heads_spread:
        out_piece = lax.dynamic_slice_in_dim(w_out, chip * head_size + core * (head_size // 2), head_size // 2, 0)
    else:
        out_piece = lax.dynamic_slice_in_dim(w_out, core * half_rows, half_rows, 0)

    starts = jnp.cumsum(counts) - counts
    chip_of = chip ^ jnp.arange(chips, dtype=jnp.int32)
    in_block = (chip_of[:, None] * piece + jnp.arange(piece, dtype=jnp.int32)[None, :]).reshape(1, rows_here)
    positions = (starts[:, None] + in_block).reshape(group_rows)
    live = (in_block < counts[:, None]).reshape(group_rows)
    live_own = live.astype(F32).reshape(shards, chips, piece)[:, 0].reshape(rows_here, 1)
    half_size = head_size // 2
    frequency = THETA ** (-jnp.arange(half_size, dtype=F32) * 2.0 / head_size)
    phases = positions.astype(F32)[:, None] * frequency[None, :]
    cosine, sine = jnp.cos(phases), jnp.sin(phases)
    angles = (
        jnp.concatenate([cosine, cosine], axis=1),
        jnp.concatenate([-sine, sine], axis=1),
        positions[:, None],
        jnp.where(live, positions, FAR)[None, :],
    )

    with jax.named_scope("norm_in"):
        inv_in, unit_in = norm_stats(inputs)
        normed_own = (unit_in * gain_in).astype(BF16)
        normed_own, cotangent_parts = tie(normed_own, cotangent_parts)
    with jax.named_scope("rehome_cotangent"):
        extended = rehome_planes(cotangent_parts)
    with jax.named_scope("gather_normed"):
        normed = gather_first(normed_own)
        normed = gather_last(normed)
        *normed, qkv_w, out_piece, extended = tie(*normed, qkv_w, out_piece, extended)
    with jax.named_scope("weights_out"):
        out_w = from_owners(out_piece)
    with jax.named_scope("gather_upstream"):
        own_routes = extended[:, width : width + top]
        upstream_own = extended[:, :width].astype(F32) * live_own
        upstream = gather_first(jnp.concatenate([upstream_own.astype(BF16), extended[:, width:]], axis=1))
    with jax.named_scope("qkv"):
        lin, squares = run_project(normed, qkv_w, wide)
        inv_qk = lax.rsqrt(sum_rows(jnp.stack([squares[0], squares[8]], axis=0)) / width + EPS).T
        *upstream, inv_qk, out_w, gate_up_piece = tie(*upstream, inv_qk, out_w, gate_up_piece)
        upstream = gather_last(upstream)
    with jax.named_scope("weights_gate_up"):
        gate_up_w = from_owners(gate_up_piece)
    pick = (jnp.arange(HEADS, dtype=jnp.int32)[None, :] == jnp.stack(head_ids)[:, None]).astype(F32)

    def head_gain(gain):
        spread = gain.reshape(1, HEADS, head_size) * pick[:, :, None]
        return jnp.sum(spread, axis=1).reshape(1, wide)

    gains = (head_gain(gain_query), head_gain(gain_key))
    attention = (chips, heads, head_size, rows_here)
    mixed, *kept = run_attend_forward(lin, inv_qk, gains, angles, *attention)
    if not heads_spread:
        out_w = jnp.concatenate([lax.dynamic_slice_in_dim(out_w, h * head_size, head_size, 0) for h in head_ids], axis=0)
    with jax.named_scope("out_proj"):
        out_split = split_matmul(mixed, out_w, False, 6)
        upstream_full = jnp.concatenate(upstream, axis=0)
        upstream_full, *out_split = tie(upstream_full, *out_split)
        residual = inputs + scatter_chips(tuple(out_split))

    with jax.named_scope("gather_middle"):
        inv_mid, unit_mid = norm_stats(residual)
        middle_own = (unit_mid * gain_mid).astype(BF16)
        middle_own, gate_up_w, down_piece = tie(middle_own, gate_up_w, down_piece)
        middle = gather_last(gather_first(middle_own))
    with jax.named_scope("weights_down"):
        down_w = from_owners(down_piece).reshape(parts, experts, own_hidden, width)
        if not fast:
            down_w = down_w.transpose(1, 0, 2, 3).reshape(1, experts, parts * own_hidden, width)
    with jax.named_scope("router"):
        logits = dot_nt(router[:experts], middle_own)
        router_expo = jnp.exp(logits - jnp.max(logits, axis=0, keepdims=True))
        router_probs = router_expo / jnp.sum(router_expo, axis=0, keepdims=True)
        expert_ids = jnp.arange(experts, dtype=F32)
        chosen = jnp.sum(
            (own_routes.astype(F32).T[None, :, :] == expert_ids[:, None, None]).astype(F32), axis=1
        )
    with jax.named_scope("experts"):
        act, lin_grad, mix_grad = run_experts(middle, upstream, gate_up_w, down_w, router, experts, top)
        middle_split = split_matmul(lin_grad, gate_up_w, True, 14)

    with jax.named_scope("middle_grad"):
        *middle_split, mix_grad, act = tie(*middle_split, mix_grad, act)
        middle_first = scatter_first(tuple(middle_split))
        mix_grad_own = mix_grad[:rows_here].T
        for step in range(1, chips):
            part = mix_grad[step * rows_here : (step + 1) * rows_here].T
            mix_grad_own = mix_grad_own + swap(part, "chip", step)
        mix_grad_own = mix_grad_own[:experts]
    with jax.named_scope("w_down_grad"):
        if fast:
            down_total = run_down_grad(act, upstream_full, width, experts, parts)
        else:
            down_total = dot_tn(act, upstream_full[:, :width]).astype(BF16)
            down_total = down_total.reshape(experts, parts, own_hidden, width).transpose(1, 0, 2, 3)
        down_total = down_total.reshape(parts * experts * own_hidden, width)
        down_part = to_owners(down_total)
    with jax.named_scope("w_gate_up_grad"):
        gate_up_total = run_weight_grad(middle, lin_grad, 14)
    with jax.named_scope("middle_grad"):
        passed = scatter_pass(middle_first)
        *passed, gate_up_total = tie(*passed, gate_up_total)
        arrived = scatter_second(tuple(passed))
        prob_grad = mix_grad_own * chosen
        logit_grad = (router_probs * (prob_grad - jnp.sum(router_probs * prob_grad, axis=0, keepdims=True))).astype(BF16)
        middle_grad = scatter_sum(middle_first, arrived) + dot_tn(logit_grad, router[:experts])
        resid_part, gain_mid_grad = norm_back(middle_grad, unit_mid, inv_mid, gain_mid)
        resid_grad = upstream_own + resid_part
        branch_own = resid_grad.astype(BF16)
    with jax.named_scope("gather_branch"):
        branch_own, down_part, gate_up_total = tie(branch_own, down_part, gate_up_total)
        gate_up_part = to_owners(gate_up_total)
        branch = gather_first(branch_own)
    with jax.named_scope("output"):
        act, branch[0] = tie(act, branch[0])
        sum_split = split_matmul(act, down_w, False, 8)
    with jax.named_scope("mixed_grad"):
        branch = gather_last(branch)
        branch, sum_split = tie_lists(branch, sum_split)
        mixed_grad = run_back(branch, out_w, min(wide, 256))
        sum_first = scatter_first(tuple(sum_split))
    query_back, key_back, value_back, gain_grads, row_sums = run_attend_backward(
        mixed_grad, lin, kept, inv_qk, gains, angles, *attention
    )

    with jax.named_scope("qk_back"):
        *sum_first, row_sums = tie(*sum_first, row_sums)
        sum_first = tuple(sum_first)
        means = (sum_rows(jnp.stack([row_sums[0], row_sums[8]], axis=0)) / width).T
    with jax.named_scope("w_out_grad"):
        out_total = run_out_grad(mixed, branch)
        if not heads_spread:
            spread = jnp.zeros((width, width), BF16)
            for i, head in enumerate(head_ids):
                spread = lax.dynamic_update_slice_in_dim(
                    spread, out_total[i * head_size : (i + 1) * head_size], head * head_size, 0
                )
            out_total = spread
    with jax.named_scope("qk_back"):
        passed = scatter_pass(sum_first)
        *passed, means, out_total, gate_up_part = tie(*passed, means, out_total, gate_up_part)
        out_part = to_owners(out_total)
        arrived = scatter_second(tuple(passed))
        qkv_grad = run_finish((query_back, key_back, value_back), lin, gains, inv_qk, means, rows_here)
    with jax.named_scope("output"):
        expert_sum = scatter_sum(sum_first, arrived)
        output_low = ((residual + expert_sum) * live_own).astype(BF16)
    with jax.named_scope("normed_grad"):
        normed_split = split_matmul(qkv_grad, qkv_w, True, 11)
        *normed_split, output_low, qkv_grad = tie(*normed_split, output_low, qkv_grad)
        normed_first = scatter_first(tuple(normed_split))
    with jax.named_scope("output"):
        output_parts = home_planes(output_low)
    with jax.named_scope("w_qkv_grad"):
        qkv_total = run_weight_grad(normed, qkv_grad, 13)
    with jax.named_scope("normed_grad"):
        passed = scatter_pass(normed_first)
        *passed, qkv_total, out_part = tie(*passed, qkv_total, out_part)
        qkv_part = to_owners(qkv_total)
        arrived = scatter_second(tuple(passed))
        normed_grad = scatter_sum(normed_first, arrived)
        input_part, gain_in_grad = norm_back(normed_grad, unit_in, inv_in, gain_in)
        input_low = (resid_grad + input_part).astype(BF16)
        output = home_chips(output_parts)
        input_low, output = tie(input_low, output)
    with jax.named_scope("input_grad"):
        input_parts = home_planes(input_low)

    if fast:
        with jax.named_scope("plane_gathers"):
            wide_first = gather_first(jnp.concatenate([gate_up_part, down_part, out_part], axis=0))
            wide_first, (input_parts,) = tie_lists(wide_first, (input_parts,))
            wide_last = gather_last(wide_first)
    with jax.named_scope("small_grads"):
        router_grad = dot(logit_grad, middle_own)

        def spread_heads(which):
            by_head = gain_grads[8 * which].reshape(heads, 1, head_size) * pick[:, :, None]
            return jnp.sum(by_head, axis=0).reshape(1, width)

        small_grads = jnp.concatenate(
            [gain_in_grad[None], spread_heads(0), spread_heads(1), gain_mid_grad[None], router_grad], axis=0
        )
        by_owner = small_grads.reshape(small_grads.shape[0], shards, shard_rows).transpose(1, 0, 2)
        small_sum = sum_chips(jnp.sum(exchange(by_owner, "shard"), axis=0))
        small_sum = small_sum + swap(small_sum, "core", 1)

    def everywhere(part):
        return lax.all_gather(part, ("chip", "core"), axis=0, tiled=False).reshape((chips, 2) + part.shape)

    def plane_parts(pieces):
        own = list(pieces)
        if len(own) != chips:
            own = own[:1] + [jnp.concatenate(own[i : i + 2], axis=0) for i in range(1, len(own), 2)]
        return own + [swap(v, "core", 1) for v in own]

    def shapes(count, *shape):
        return [jax.ShapeDtypeStruct(shape, F32)] * count

    if fast:
        with jax.named_scope("plane_gathers"):
            wide_last, (input_parts, small_sum) = tie_lists(wide_last, (input_parts, small_sum))
            qkv_first = gather_first(qkv_part)
            wide_parts = plane_parts(wide_last)
        input_grad = home_chips(input_parts)
        with jax.named_scope("w_down_grad"):
            (w_down_grad,) = place(
                functools.partial(place_rows, chips), where, wide_parts,
                (((own_hidden, width), lambda i, where: (half_rows // own_hidden + i, 0)),),
                shapes(1, experts, shard_hidden, width),
                ((1, shard_hidden, width), lambda i, where: (i, 0, 0)),
                (experts,), "place_down",
            )
        with jax.named_scope("w_out_grad"):
            out_at = half_rows + experts * own_hidden
            (w_out_grad,) = place(
                functools.partial(place_rows, chips), where, wide_parts,
                (((head_size // 2, width // 4), lambda i, where: (out_at // (head_size // 2), i)),),
                shapes(1, 1, shard_rows, width),
                ((1, shard_rows, width // 4), lambda i, where: (0, 0, i)),
                (4,), "place_out",
            )
            w_out_grad = w_out_grad.reshape(shard_rows, width)
        with jax.named_scope("w_gate_up_grad"):
            columns = jnp.concatenate([wanted + 2 * own_hidden * ((chip ^ step) - chip) for step in range(chips)])
            order = (columns[:, None] == jnp.arange(hidden, dtype=jnp.int32)[None, :]).astype(BF16)
            tile = parts * own_hidden
            w_gate_grad, w_up_grad = place(
                functools.partial(place_hidden, chips), where, wide_parts,
                (
                    ((half_rows, tile), lambda i, where: (0, i)),
                    ((half_rows, tile), lambda i, where: (0, experts + i)),
                ),
                shapes(2, experts, 2, half_rows, hidden),
                ((1, 2, half_rows, hidden), lambda i, where: (i, 0, 0, 0)),
                (experts,), "place_gate_up", (order,),
            )
            w_gate_grad = w_gate_grad.reshape(experts, shard_rows, hidden)
            w_up_grad = w_up_grad.reshape(experts, shard_rows, hidden)
        with jax.named_scope("w_qkv_grad"):
            tile = 64

            qkv_first, (w_down_grad, w_out_grad, w_gate_grad, w_up_grad) = tie_lists(
                qkv_first, (w_down_grad, w_out_grad, w_gate_grad, w_up_grad)
            )
            qkv_parts, (input_grad,) = tie_lists(plane_parts(gather_last(qkv_first)), (input_grad,))
            w_query_grad, w_key_grad, w_value_grad = (
                v.reshape(shard_rows, width)
                for v in place(
                    functools.partial(place_heads, chips, heads, head_size), where, qkv_parts,
                    (((tile, 3 * wide), lambda i, where: (i, 0)),),
                    shapes(3, 2, half_rows, width),
                    ((2, tile, width), lambda i, where: (0, i, 0)),
                    (half_rows // tile,), "place_heads",
                )
            )
    else:
        input_grad = home_chips(input_parts)
        spread = everywhere(down_part).reshape(chips, 2, experts, own_hidden, width)
        w_down_grad = spread.transpose(2, 0, 1, 3, 4).reshape(experts, shard_hidden, width).astype(F32)
        spread = everywhere(gate_up_part).reshape(chips, 2, half_rows, 2, experts, shards, 2 * own_hidden)
        spread = spread.transpose(3, 4, 1, 2, 5, 0, 6).reshape(2, experts, shard_rows, hidden).astype(F32)
        w_gate_grad, w_up_grad = spread[0], spread[1]
        if heads_spread:
            w_out_grad = everywhere(out_part).reshape(shard_rows, width).astype(F32)
        else:
            spread = lax.psum(out_part.astype(F32), "chip")
            w_out_grad = lax.all_gather(spread, "core", axis=0, tiled=True)

        def heads_back(part, count):
            spread = everywhere(part).reshape(chips, 2, half_rows, count, heads, head_size)
            return spread.transpose(3, 1, 2, 4, 0, 5).reshape(count, shard_rows, width).astype(F32)

        w_query_grad, w_key_grad, w_value_grad = heads_back(qkv_part, 3)
    return (
        output,
        input_grad,
        small_sum[0],
        w_query_grad,
        w_key_grad,
        w_value_grad,
        small_sum[1],
        small_sum[2],
        w_out_grad,
        small_sum[3],
        small_sum[4:].T,
        w_gate_grad,
        w_up_grad,
        w_down_grad,
    )


def solution(mesh):
    reps, shards = mesh.devices.shape
    split = Mesh(mesh.devices.reshape(reps // 2, 2, shards), ("chip", "core", "shard"))
    rows = P(("chip", "core", "shard"), None)
    first, second = P("shard", None), P(None, "shard", None)
    gain = P("shard")
    in_specs = (
        rows, rows, P(("chip", "core"), None), rows, gain, first, first, first, gain, gain, first, gain, first,
        second, second, second,
    )
    out_specs = (rows, rows, gain, first, first, first, gain, gain, first, gain, first, second, second, second)
    return jax.shard_map(body, mesh=split, in_specs=in_specs, out_specs=out_specs, check_vma=False)
```

```python
import functools

import jax
import jax.numpy as jnp
from jax import lax
from jax.experimental import pallas as pl
from jax.experimental.pallas import tpu as pltpu
from jax.sharding import Mesh
from jax.sharding import PartitionSpec as P

HEADS = 16
EPS = 1e-05
THETA = 10000.0
MASKED = -1e30
FAR = 1 << 30
F32 = jnp.float32
BF16 = jnp.bfloat16
VMEM_BYTES = 56 * 1024 * 1024


def dot(left, right):
    return jnp.dot(left, right, preferred_element_type=F32)


def dot_nt(left, right):
    return lax.dot_general(left, right, (((1,), (1,)), ((), ())), preferred_element_type=F32)


def dot_tn(left, right):
    return lax.dot_general(left, right, (((0,), (0,)), ((), ())), preferred_element_type=F32)


def tie(*values):
    return lax.optimization_barrier(values)


def tie_lists(*lists):
    return lax.optimization_barrier([list(values) for values in lists])


def swap(value, axis, step):
    size = lax.axis_size(axis)
    return lax.ppermute(value, axis, [(i, i ^ step) for i in range(size)])


def exchange(parts, axis):
    me = lax.axis_index(axis)
    out = parts
    for step in range(1, lax.axis_size(axis)):
        sent = lax.dynamic_index_in_dim(parts, me ^ step, 0, keepdims=True)
        out = lax.dynamic_update_slice_in_dim(out, swap(sent, axis, step), me ^ step, 0)
    return out


def gather_first(block):
    chips = lax.axis_size("chip")
    if chips != 4:
        return [block] + [swap(block, "chip", step) for step in range(1, chips)]
    half = block.shape[0] // 2
    top, low = block[:half], block[half:]
    two_top, one_low = swap(top, "chip", 2), swap(low, "chip", 1)
    one_top, two_low = swap(top, "chip", 1), swap(low, "chip", 2)
    return [block, one_top, one_low, two_top, two_low]


def gather_last(pieces):
    if lax.axis_size("chip") != 4:
        return pieces
    return pieces + [swap(pieces[3], "chip", 1), swap(pieces[2], "chip", 2)]


def scatter_first(split):
    if len(split) == 2:
        return split
    own_left, own_right, to_one, to_two, keep_left, keep_right = split
    return (own_left, own_right, swap(to_one, "chip", 1), swap(to_two, "chip", 2), keep_left, keep_right)


def scatter_pass(first):
    if len(first) == 2:
        return (first[1][0],)
    _, _, from_one, from_two, keep_left, keep_right = first
    return (
        (keep_left.astype(F32) + from_one[1].astype(F32)).astype(BF16),
        (keep_right.astype(F32) + from_two[1].astype(F32)).astype(BF16),
    )


def scatter_second(passed):
    if len(passed) == 1:
        return list(passed)
    return [swap(passed[0], "chip", 2), swap(passed[1], "chip", 1)]


def scatter_sum(first, arrived):
    if len(first) == 2:
        own, others = first
        for step, other in enumerate(tuple(arrived) + tuple(others[1:])):
            own = own + swap(other, "chip", step + 1).astype(F32)
        return own
    own_left, own_right, from_one, from_two, _, _ = first
    return jnp.concatenate(
        [
            own_left + from_one[0].astype(F32) + arrived[0].astype(F32),
            own_right + from_two[0].astype(F32) + arrived[1].astype(F32),
        ],
        axis=1,
    )


def scatter_chips(split):
    first = scatter_first(split)
    return scatter_sum(first, scatter_second(scatter_pass(first)))


def sum_chips(value):
    step = 1
    while step < lax.axis_size("chip"):
        value = value + swap(value, "chip", step)
        step *= 2
    return value


def sum_rows(values):
    chips = lax.axis_size("chip")
    total = values.reshape(values.shape[0], chips, -1)
    step = 1
    while step < chips:
        other = swap(total, "chip", step)
        total = total + jnp.concatenate([other[:, i ^ step : (i ^ step) + 1] for i in range(chips)], axis=1)
        step *= 2
    return total.reshape(values.shape)


def rehome_chips(rows):
    chips = lax.axis_size("chip")
    parts = rows.reshape(chips, rows.shape[0] // chips, rows.shape[1])
    return lax.all_to_all(parts, "chip", 0, 0, tiled=True)


def rehome_planes(parts):
    return lax.all_to_all(parts, "shard", 0, 0, tiled=True).reshape(-1, parts.shape[2])


def home_planes(rows):
    shards = lax.axis_size("shard")
    parts = rows.reshape(shards, rows.shape[0] // shards, rows.shape[1])
    return lax.all_to_all(parts, "shard", 0, 0, tiled=True)


def home_chips(parts):
    return lax.all_to_all(parts, "chip", 0, 0, tiled=True).reshape(-1, parts.shape[2])


ANYWHERE = pl.BlockSpec(memory_space=pl.ANY)


def run(kernel, name, micros, grid, in_specs, out_specs, out_shape, args, scratch=()):
    return pl.pallas_call(
        kernel,
        grid=grid,
        in_specs=in_specs,
        out_specs=out_specs,
        out_shape=out_shape,
        scratch_shapes=list(scratch),
        compiler_params=pltpu.CompilerParams(vmem_limit_bytes=VMEM_BYTES),
        cost_estimate=pl.CostEstimate(flops=micros * 550_000_000, bytes_accessed=1024, transcendentals=0),
        name=name,
    )(*args)


def load_rows(pieces, target, sems):
    copies, at = [], 0
    for i, piece in enumerate(pieces):
        copies.append(pltpu.make_async_copy(piece, target.at[pl.ds(at, piece.shape[0]), :], sems.at[i]))
        at += piece.shape[0]
    for copy in copies:
        copy.start()
    for copy in copies:
        copy.wait()


def rows_scratch(pieces):
    rows = sum(piece.shape[0] for piece in pieces)
    return [pltpu.VMEM((rows, pieces[0].shape[1]), BF16), pltpu.SemaphoreType.DMA((len(pieces),))]


def column_sums(values):
    ones = jnp.ones((8, values.shape[1]), F32)
    return lax.dot_general(
        ones, values, (((1,), (1,)), ((), ())), precision=lax.Precision.HIGHEST, preferred_element_type=F32
    )


def project_kernel(count, *refs):
    pieces, (weight, out, squares, rows, sems) = refs[:count], refs[count:]

    @pl.when(pl.program_id(0) == 0)
    def _():
        load_rows(pieces, rows, sems)

    result = dot(rows[...], weight[...])
    out[...] = result
    squares[...] = column_sums(result * result)


def run_project(pieces, weight, tile):
    depth, columns = weight.shape
    rows = sum(piece.shape[0] for piece in pieces)
    steps = columns // tile
    return run(
        functools.partial(project_kernel, len(pieces)), "project", 16, (steps,),
        [ANYWHERE] * len(pieces) + [pl.BlockSpec((depth, tile), lambda i: (0, i))],
        [pl.BlockSpec((rows, tile), lambda i: (0, i)), pl.BlockSpec((8, rows), lambda i: (i, 0))],
        [jax.ShapeDtypeStruct((rows, columns), F32), jax.ShapeDtypeStruct((8 * steps, rows), F32)],
        (*pieces, weight),
        rows_scratch(pieces),
    )


def back_kernel(count, *refs):
    pieces, (weight, out, rows, sems) = refs[:count], refs[count:]

    @pl.when(pl.program_id(0) == 0)
    def _():
        load_rows(pieces, rows, sems)

    out[...] = dot_nt(rows[...], weight[...]).astype(BF16)


def run_back(pieces, weight, tile):
    rows = sum(piece.shape[0] for piece in pieces)
    return run(
        functools.partial(back_kernel, len(pieces)), "back", 7, (weight.shape[0] // tile,),
        [ANYWHERE] * len(pieces) + [pl.BlockSpec((tile, weight.shape[1]), lambda i: (i, 0))],
        pl.BlockSpec((rows, tile), lambda i: (0, i)),
        jax.ShapeDtypeStruct((rows, weight.shape[0]), BF16),
        (*pieces, weight),
        rows_scratch(pieces),
    )


def join_experts(ref):
    parts, experts, units, columns = ref.shape
    if parts == 1:
        return ref[...].reshape(experts * units, columns)
    return jnp.concatenate([ref[:, expert].reshape(parts * units, columns) for expert in range(experts)], axis=0)


def split_kernel(block, turned, left, left_w, right_w, own_left, own_right, to_one, to_two, keep_left, keep_right):
    def product(weight):
        if turned:
            return dot_nt(left[...], weight[...])
        return dot(left[...], weight[...] if len(weight.shape) == 2 else join_experts(weight))

    result = product(left_w)
    own_left[...] = result[:block]
    to_one[0] = result[block : 2 * block].astype(BF16)
    keep_left[...] = result[2 * block : 3 * block].astype(BF16)
    to_one[1] = result[3 * block :].astype(BF16)
    result = product(right_w)
    own_right[...] = result[:block]
    keep_right[...] = result[block : 2 * block].astype(BF16)
    to_two[0] = result[2 * block : 3 * block].astype(BF16)
    to_two[1] = result[3 * block :].astype(BF16)


def split_matmul(left, weight, turned, micros):
    chips = lax.axis_size("chip")
    rows = left.shape[0]
    block = rows // chips
    width = weight.shape[0] if turned else weight.shape[-1]
    if chips != 4:
        if weight.ndim == 4:
            weight = weight.transpose(1, 0, 2, 3).reshape(-1, width)
        whole = (dot_nt if turned else dot)(left, weight)
        return (whole[:block], [whole[i * block : (i + 1) * block].astype(BF16) for i in range(1, chips)])
    half, tile = width // 2, 256
    steps = half // tile

    def weight_spec(first):
        if turned:
            return pl.BlockSpec((tile, weight.shape[1]), lambda i: (first + i, 0))
        return pl.BlockSpec((*weight.shape[:-1], tile), lambda i: (0,) * (weight.ndim - 1) + (first + i,))

    one = pl.BlockSpec((block, tile), lambda i: (0, i))
    two = pl.BlockSpec((2, block, tile), lambda i: (0, 0, i))
    wide, low = jax.ShapeDtypeStruct((block, half), F32), jax.ShapeDtypeStruct((block, half), BF16)
    pair = jax.ShapeDtypeStruct((2, block, half), BF16)
    return run(
        functools.partial(split_kernel, block, turned), "split_matmul", micros, (steps,),
        [pl.BlockSpec(left.shape, lambda i: (0, 0)), weight_spec(0), weight_spec(steps)],
        [one, one, two, two, one, one],
        [wide, wide, pair, pair, low, low],
        (left, weight, weight),
    )


def weight_grad_kernel(count, tile, *refs):
    pieces, (grad, out, rows, sems) = refs[:count], refs[count:]

    @pl.when(pl.program_id(0) == 0)
    def _():
        load_rows(pieces, rows, sems)

    columns = pl.ds(pl.multiple_of(pl.program_id(0) * tile, tile), tile)
    out[...] = dot_tn(rows[:, columns], grad[...]).astype(BF16)


def run_weight_grad(pieces, grad, micros, columns=None):
    tile = 512
    depth, columns = pieces[0].shape[1], columns or grad.shape[1]
    return run(
        functools.partial(weight_grad_kernel, len(pieces), tile), "weight_grad", micros, (depth // tile,),
        [ANYWHERE] * len(pieces) + [pl.BlockSpec((grad.shape[0], columns), lambda i: (0, 0))],
        pl.BlockSpec((tile, columns), lambda i: (i, 0)),
        jax.ShapeDtypeStruct((depth, columns), BF16),
        (*pieces, grad),
        rows_scratch(pieces),
    )


def down_grad_kernel(experts, parts, act, upstream, out):
    result = dot_tn(act[...], upstream[...]).astype(BF16)
    own = result.shape[0] // (experts * parts)
    for expert in range(experts):
        for part in range(parts):
            at = (expert * parts + part) * own
            out[part, expert * own : (expert + 1) * own, :] = result[at : at + own]


def run_down_grad(act, upstream, width, experts, parts):
    hidden, tile = act.shape[1], 512
    return run(
        functools.partial(down_grad_kernel, experts, parts), "down_grad", 9, (width // tile,),
        [pl.BlockSpec(act.shape, lambda i: (0, 0)), pl.BlockSpec((upstream.shape[0], tile), lambda i: (0, i))],
        pl.BlockSpec((parts, hidden // parts, tile), lambda i: (0, 0, i)),
        jax.ShapeDtypeStruct((parts, hidden // parts, width), BF16),
        (act, upstream),
    )


def out_grad_kernel(count, tile, *refs):
    pieces, (mixed, out, rows, sems) = refs[:count], refs[count:]

    @pl.when(pl.program_id(0) == 0)
    def _():
        load_rows(pieces, rows, sems)

    columns = pl.ds(pl.multiple_of(pl.program_id(0) * tile, tile), tile)
    out[...] = dot_tn(mixed[...], rows[:, columns]).astype(BF16)


def run_out_grad(mixed, pieces):
    tile, width = 512, pieces[0].shape[1]
    return run(
        functools.partial(out_grad_kernel, len(pieces), tile), "out_grad", 7, (width // tile,),
        [ANYWHERE] * len(pieces) + [pl.BlockSpec(mixed.shape, lambda i: (0, 0))],
        pl.BlockSpec((mixed.shape[1], tile), lambda i: (0, i)),
        jax.ShapeDtypeStruct((mixed.shape[1], width), BF16),
        (*pieces, mixed),
        rows_scratch(pieces),
    )


def lane_roll(values):
    return pltpu.roll(values, values.shape[1] // 2, 1)


def take_block(ref, block, chips, block_rows):
    piece = block_rows // chips
    at = lambda chip: chip * block_rows + block * piece
    return jnp.concatenate([ref[at(chip) : at(chip) + piece, :] for chip in range(chips)], axis=0)


def put_block(ref, block, chips, block_rows, values):
    piece = block_rows // chips
    for chip in range(chips):
        at = chip * block_rows + block * piece
        ref[at : at + piece, :] = values[chip * piece : (chip + 1) * piece]


def attend_forward(
    chips, block_rows, scale,
    query_ref, key_ref, value_ref, inv_ref, gain_q, gain_k, cos_ref, sin_ref, pos_ref, key_pos_ref,
    mixed, query_rot, key_rot, value_low, lse,
):
    blocks = inv_ref.shape[0] // block_rows
    for block in range(blocks):
        rows = pl.ds(block * block_rows, block_rows)
        cosine, sine = cos_ref[rows, :], sin_ref[rows, :]
        inv = take_block(inv_ref, block, chips, block_rows)
        query = take_block(query_ref, block, chips, block_rows) * inv[:, 0:1] * gain_q[...]
        query_rot[rows, :] = (query * cosine + lane_roll(query) * sine).astype(BF16)
        key = take_block(key_ref, block, chips, block_rows) * inv[:, 1:2] * gain_k[...]
        key_rot[rows, :] = (key * cosine + lane_roll(key) * sine).astype(BF16)
        value_low[rows, :] = take_block(value_ref, block, chips, block_rows).astype(BF16)
    for block in range(blocks):
        rows = pl.ds(block * block_rows, block_rows)
        seen = pl.ds(0, (block + 1) * block_rows)
        scores = dot_nt(query_rot[rows, :], key_rot[seen, :]) * scale
        scores = jnp.where(key_pos_ref[:, seen] <= pos_ref[rows, :], scores, MASKED)
        peak = jnp.max(scores, axis=-1, keepdims=True)
        expo = jnp.exp(scores - peak)
        total = jnp.sum(expo, axis=-1, keepdims=True)
        probs_low = (expo * (1.0 / total)).astype(BF16)
        put_block(mixed, block, chips, block_rows, dot(probs_low, value_low[seen, :]).astype(BF16))
        lse[rows, :] = jnp.broadcast_to(peak + jnp.log(total), (block_rows, lse.shape[1]))


def attend_backward(
    chips, block_rows, scale,
    grad_ref, query_ref, key_ref, query_rot, key_rot, value_low, lse, gain_q, gain_k,
    inv_ref, cos_ref, sin_ref, pos_ref, key_pos_ref,
    query_back, key_back, value_back, gains, sums_ref,
    key_sum, value_sum,
):
    blocks = inv_ref.shape[0] // block_rows

    @pl.when(pl.program_id(0) == 0)
    def _():
        sums_ref[...] = jnp.zeros_like(sums_ref)

    key_sum[...] = jnp.zeros_like(key_sum)
    value_sum[...] = jnp.zeros_like(value_sum)
    for block in range(blocks):
        rows = pl.ds(block * block_rows, block_rows)
        seen = pl.ds(0, (block + 1) * block_rows)
        query = query_rot[rows, :]
        grad = take_block(grad_ref, block, chips, block_rows)
        scores = dot_nt(query, key_rot[seen, :]) * scale
        scores = jnp.where(key_pos_ref[:, seen] <= pos_ref[rows, :], scores, MASKED)
        probs = jnp.exp(scores - lse[rows, 0:1])
        probs_grad = dot_nt(grad, value_low[seen, :])
        weighted = jnp.sum(probs * probs_grad, axis=-1, keepdims=True)
        score_grad = (probs * (probs_grad - weighted)).astype(BF16)
        query_grad = dot(score_grad, key_rot[seen, :]) * scale
        turned = query_grad * cos_ref[rows, :] - lane_roll(query_grad) * sin_ref[rows, :]
        put_block(query_back, block, chips, block_rows, turned)
        key_sum[seen, :] += dot_tn(score_grad, query)
        value_sum[seen, :] += dot_tn(probs.astype(BF16), grad)
    for block in range(blocks):
        rows = pl.ds(block * block_rows, block_rows)
        key_grad = key_sum[rows, :] * scale
        turned = key_grad * cos_ref[rows, :] - lane_roll(key_grad) * sin_ref[rows, :]
        put_block(key_back, block, chips, block_rows, turned)
        put_block(value_back, block, chips, block_rows, value_sum[rows, :].astype(BF16))
    for which, (lin, back, gain) in enumerate(((query_ref, query_back, gain_q), (key_ref, key_back, gain_k))):
        product = back[...] * lin[...] * inv_ref[:, which : which + 1]
        sums_ref[pl.ds(8 * which, 8), :] += column_sums(product * gain[...])
        gains[pl.ds(8 * which, 8), :] = jnp.broadcast_to(jnp.sum(product, axis=0, keepdims=True), (8, product.shape[1]))


def attention_specs(rows, head_size, heads):
    column = pl.BlockSpec((rows, head_size), lambda h: (0, h))
    whole = lambda shape: pl.BlockSpec(shape, lambda h: (0, 0))
    part = [pl.BlockSpec((rows, head_size), lambda h, which=which: (0, which * heads + h)) for which in range(3)]
    gain = pl.BlockSpec((1, head_size), lambda h: (0, h))
    return column, whole, part, gain


def run_attend_forward(lin, inv, gains, angles, chips, heads, head_size, block_rows):
    rows, wide = lin.shape[0], heads * head_size
    column, whole, part, gain = attention_specs(rows, head_size, heads)
    low = jax.ShapeDtypeStruct((rows, wide), BF16)
    return run(
        functools.partial(attend_forward, chips, block_rows, head_size**-0.5), "attend_forward", 17, (heads,),
        part + [whole(inv.shape), gain, gain] + [whole(v.shape) for v in angles],
        [column] * 5,
        [low, low, low, low, jax.ShapeDtypeStruct((rows, wide), F32)],
        (lin, lin, lin, inv, *gains, *angles),
    )


def run_attend_backward(mixed_grad, lin, kept, inv, gains, angles, chips, heads, head_size, block_rows):
    rows, wide = mixed_grad.shape
    column, whole, part, gain = attention_specs(rows, head_size, heads)
    full = jax.ShapeDtypeStruct((rows, wide), F32)
    return run(
        functools.partial(attend_backward, chips, block_rows, head_size**-0.5), "attend_backward", 20, (heads,),
        [column, part[0], part[1]] + [column] * 4 + [gain, gain, whole(inv.shape)] + [whole(v.shape) for v in angles],
        [column] * 3 + [pl.BlockSpec((16, head_size), lambda h: (0, h)), whole((16, rows))],
        [full, full, jax.ShapeDtypeStruct((rows, wide), BF16), jax.ShapeDtypeStruct((16, wide), F32),
         jax.ShapeDtypeStruct((16, rows), F32)],
        (mixed_grad, lin, lin, *kept, *gains, inv, *angles),
        [pltpu.VMEM((rows, head_size), F32)] * 2,
    )


def finish_kernel(wide, query_back, key_back, value_back, lin, gain_q, gain_k, inv_ref, mean_ref, out):
    for which, (back, gain) in enumerate(((query_back, gain_q), (key_back, gain_k))):
        inv = inv_ref[:, which : which + 1]
        columns = slice(which * wide, (which + 1) * wide)
        unit = lin[:, columns] * inv
        out[:, columns] = (inv * (gain[...] * back[...] - unit * mean_ref[:, which : which + 1])).astype(BF16)
    out[:, 2 * wide :] = value_back[...]


def run_finish(backs, lin, gains, inv, means, tile):
    rows, wide = backs[0].shape
    spec = lambda columns: pl.BlockSpec((tile, columns), lambda i: (i, 0))
    gain = pl.BlockSpec((1, wide), lambda i: (0, 0))
    return run(
        functools.partial(finish_kernel, wide), "finish", 7, (rows // tile,),
        [spec(wide)] * 3 + [spec(3 * wide), gain, gain, spec(2), spec(2)],
        spec(3 * wide),
        jax.ShapeDtypeStruct((rows, 3 * wide), BF16),
        (*backs, lin, *gains, inv, means),
    )


def experts_kernel(count, experts, top, *refs):
    middles, upstreams, refs = refs[:count], refs[count : 2 * count], refs[2 * count :]
    gate_w, up_w, down_w, router_w, act_out, grad_out, mix_grad, middle, upstream, mix, middle_sems, upstream_sems = refs
    step, tile = pl.program_id(0), gate_w.shape[1]
    rows, depth = middle.shape
    lane = lax.broadcasted_iota(jnp.int32, (1, mix.shape[1]), 1)

    @pl.when(step == 0)
    def _():
        load_rows(middles, middle, middle_sems)
        load_rows(upstreams, upstream, upstream_sems)
        mix_grad[...] = jnp.zeros_like(mix_grad)
        logits = jnp.where(lane < experts, dot_nt(middle[...], router_w[...]), MASKED)
        expo = jnp.exp(logits - jnp.max(logits, axis=-1, keepdims=True))
        chosen = jnp.zeros_like(expo)
        for i in range(top):
            route = upstream[:, depth + i : depth + i + 1].astype(F32)
            chosen = chosen + jnp.where(route == lane.astype(F32), 1.0, 0.0)
        mix[...] = expo / jnp.sum(expo, axis=-1, keepdims=True) * chosen

    mine = lane == step
    mix_column = jnp.sum(jnp.where(mine, mix[...], 0.0), axis=-1, keepdims=True)
    gate = dot(middle[...], gate_w[...])
    up = dot(middle[...], up_w[...])
    back = dot_nt(upstream[:, :depth], down_w[...].reshape(tile, depth))
    sigma = 1.0 / (1.0 + jnp.exp(-gate))
    silu = gate * sigma
    act = silu * up
    mix_grad[...] += jnp.where(mine, jnp.sum(act * back, axis=-1, keepdims=True), 0.0)
    back = back * mix_column
    act_out[...] = (act * mix_column).astype(BF16)
    columns = pl.ds(pl.multiple_of(step * tile, tile), tile)
    up_columns = pl.ds(pl.multiple_of((experts + step) * tile, tile), tile)
    grad_out[:, columns] = (back * up * sigma * (1.0 + gate * (1.0 - sigma))).astype(BF16)
    grad_out[:, up_columns] = (back * silu).astype(BF16)


def run_experts(middles, upstreams, gate_up, down, router, experts, top):
    rows, depth = sum(piece.shape[0] for piece in middles), middles[0].shape[1]
    parts, _, units, _ = down.shape
    tile = parts * units
    whole = lambda shape: pl.BlockSpec(shape, lambda i: (0, 0))
    grad_shape, mix_shape = (rows, 2 * experts * tile), (rows, router.shape[0])
    buffers, sems = zip(rows_scratch(middles), rows_scratch(upstreams))
    return run(
        functools.partial(experts_kernel, len(middles), experts, top), "experts", 26, (experts,),
        [ANYWHERE] * (2 * len(middles))
        + [
            pl.BlockSpec((depth, tile), lambda i: (0, i)),
            pl.BlockSpec((depth, tile), lambda i: (0, experts + i)),
            pl.BlockSpec((parts, 1, units, depth), lambda i: (0, i, 0, 0)),
            whole(router.shape),
        ],
        [pl.BlockSpec((rows, tile), lambda i: (0, i)), whole(grad_shape), whole(mix_shape)],
        [
            jax.ShapeDtypeStruct((rows, experts * tile), BF16),
            jax.ShapeDtypeStruct(grad_shape, BF16),
            jax.ShapeDtypeStruct(mix_shape, F32),
        ],
        (*middles, *upstreams, gate_up, gate_up, down, router),
        [*buffers, pltpu.VMEM(mix_shape, F32), *sems],
    )


def part_owners(where_ref, chips):
    return [(where_ref[0] ^ step, where_ref[1] ^ turn) for turn in range(2) for step in range(chips)]


def place_heads(chips, heads, head_size, where_ref, *refs):
    parts, outs = refs[: 2 * chips], refs[2 * chips :]
    for part, (chip, core) in zip(parts, part_owners(where_ref, chips)):
        for which, out in enumerate(outs):
            for i in range(heads):
                first = (which * heads + i) * head_size
                column = pl.multiple_of((i * chips + chip) * head_size, head_size)
                out[core, :, pl.ds(column, head_size)] = part[:, first : first + head_size].astype(F32)


def place_hidden(chips, where_ref, *refs):
    count = 2 * chips
    order, outs = refs[2 * count], refs[2 * count + 1 :]
    owners = part_owners(where_ref, chips)
    for which, out in enumerate(outs):
        parts = refs[which * count : (which + 1) * count]
        for turn in range(2):
            row = jnp.concatenate([part[...] for part in parts[turn * chips : (turn + 1) * chips]], axis=1)
            out[0, owners[turn * chips][1]] = dot(row, order[...])


def place_rows(chips, where_ref, *refs):
    parts, out = refs[: 2 * chips], refs[-1]
    height = parts[0].shape[0]
    for part, (chip, core) in zip(parts, part_owners(where_ref, chips)):
        row = pl.multiple_of((2 * chip + core) * height, height)
        out[0, pl.ds(row, height), :] = part[...].astype(F32)


def place(kernel, where, parts, part_blocks, out_shapes, out_block, grid, name, extra=()):
    return pl.pallas_call(
        kernel,
        grid_spec=pltpu.PrefetchScalarGridSpec(
            num_scalar_prefetch=1,
            grid=grid,
            in_specs=[pl.BlockSpec(*block) for block in part_blocks for _ in parts]
            + [pl.BlockSpec(v.shape, lambda i, where: (0, 0)) for v in extra],
            out_specs=[pl.BlockSpec(*out_block)] * len(out_shapes),
        ),
        out_shape=out_shapes,
        compiler_params=pltpu.CompilerParams(vmem_limit_bytes=VMEM_BYTES),
        cost_estimate=pl.CostEstimate(flops=8 * 550_000_000, bytes_accessed=1024, transcendentals=0),
        name=name,
    )(where, *(parts * len(part_blocks)), *extra)


def norm_stats(values):
    inv_root = lax.rsqrt(jnp.mean(values * values, axis=-1, keepdims=True) + EPS)
    return (inv_root, values * inv_root)


def norm_back(gradient, unit_rows, inv_root, gain):
    scaled = gain * gradient
    rows_part = inv_root * (scaled - unit_rows * jnp.mean(unit_rows * scaled, axis=-1, keepdims=True))
    return (rows_part, jnp.sum(gradient * unit_rows, axis=0))


def body(
    tokens, cotangent, live_counts, routes, norm_in, w_query, w_key, w_value, norm_query, norm_key, w_out, norm_mid,
    w_router, w_gate, w_up, w_down,
):
    chips, shards = lax.axis_size("chip"), lax.axis_size("shard")
    chip, core = lax.axis_index("chip"), lax.axis_index("core")
    rows_here, width = tokens.shape
    head_size = width // HEADS
    heads = HEADS // chips
    wide = heads * head_size
    experts, top = w_gate.shape[0], routes.shape[1]
    piece = rows_here // chips
    group_rows = rows_here * shards
    shard_rows = w_query.shape[0]
    half_rows = shard_rows // 2
    shard_hidden, hidden = w_down.shape[1], w_gate.shape[2]
    own_hidden = shard_hidden // (2 * chips)
    parts = 2 * shards
    heads_spread = HEADS // shards == chips
    fast = chips == 4 and own_hidden % 16 == 0 and heads_spread
    where = jnp.stack([chip, core]).astype(jnp.int32)
    owners = ("shard", "core")

    def from_owners(part):
        return lax.all_gather(part, owners, axis=0, tiled=True)

    def to_owners(total):
        return lax.psum_scatter(total, owners, scatter_dimension=0, tiled=True)

    with jax.named_scope("rehome_tokens"):
        token_parts = rehome_chips(tokens)

    head_ids = [i * chips + chip for i in range(heads)]
    with jax.named_scope("weights_qkv"):
        qkv_piece = jnp.concatenate(
            [
                lax.dynamic_slice(w, (core * half_rows, head * head_size), (half_rows, head_size))
                for w in (w_query, w_key, w_value)
                for head in head_ids
            ],
            axis=1,
        )
        qkv_w = from_owners(qkv_piece)
    route_columns = jnp.pad(routes.astype(BF16), ((0, 0), (0, 128 - top)))
    extended = jnp.concatenate([cotangent, route_columns], axis=1)
    small = jnp.concatenate(
        [v.astype(F32)[None] for v in (norm_in, norm_query, norm_key, norm_mid)] + [w_router.astype(F32).T], axis=0
    )
    extended, token_parts = tie(extended, token_parts)
    with jax.named_scope("norm_in"):
        inputs = rehome_planes(token_parts).astype(F32)
    with jax.named_scope("small_gathers"):
        small_all = exchange(jnp.broadcast_to(small[None], (shards,) + small.shape), "shard")
        small_all = small_all.transpose(1, 0, 2).reshape(small.shape[0], width)
        gain_in, gain_query, gain_key, gain_mid = (small_all[i] for i in range(4))
        router = jnp.pad(small_all[4:], ((0, 8 - experts), (0, 0))).astype(BF16)
        counts = lax.ppermute(
            live_counts,
            ("chip", "core", "shard"),
            [
                ((i * 2 + k) * shards + j, (j * 2 + k) * shards + i)
                for i in range(chips)
                for k in range(2)
                for j in range(shards)
            ],
        )[0]
    with jax.named_scope("rehome_cotangent"):
        cotangent_parts = exchange(extended.reshape(chips, piece, extended.shape[1]), "chip")
    hidden_at = 2 * chip * own_hidden
    with jax.named_scope("weights_gate_up"):
        unit = jnp.arange(parts * own_hidden, dtype=jnp.int32)
        wanted = (unit // (2 * own_hidden)) * shard_hidden + hidden_at + unit % (2 * own_hidden)
        choose = (jnp.arange(hidden, dtype=jnp.int32)[:, None] == wanted[None, :]).astype(BF16)
        gate_up_rows = [lax.dynamic_slice_in_dim(w, core * half_rows, half_rows, 1) for w in (w_gate, w_up)]
        gate_up_piece = jnp.concatenate(
            [dot(w[expert], choose).astype(BF16) for w in gate_up_rows for expert in range(experts)], axis=1
        )
    down_piece = lax.dynamic_slice_in_dim(w_down, hidden_at + core * own_hidden, own_hidden, 1)
    down_piece = down_piece.reshape(experts * own_hidden, width)
    if heads_spread:
        out_piece = lax.dynamic_slice_in_dim(w_out, chip * head_size + core * (head_size // 2), head_size // 2, 0)
    else:
        out_piece = lax.dynamic_slice_in_dim(w_out, core * half_rows, half_rows, 0)

    starts = jnp.cumsum(counts) - counts
    chip_of = chip ^ jnp.arange(chips, dtype=jnp.int32)
    in_block = (chip_of[:, None] * piece + jnp.arange(piece, dtype=jnp.int32)[None, :]).reshape(1, rows_here)
    positions = (starts[:, None] + in_block).reshape(group_rows)
    live = (in_block < counts[:, None]).reshape(group_rows)
    live_own = live.astype(F32).reshape(shards, chips, piece)[:, 0].reshape(rows_here, 1)
    half_size = head_size // 2
    frequency = THETA ** (-jnp.arange(half_size, dtype=F32) * 2.0 / head_size)
    phases = positions.astype(F32)[:, None] * frequency[None, :]
    cosine, sine = jnp.cos(phases), jnp.sin(phases)
    angles = (
        jnp.concatenate([cosine, cosine], axis=1),
        jnp.concatenate([-sine, sine], axis=1),
        positions[:, None],
        jnp.where(live, positions, FAR)[None, :],
    )

    with jax.named_scope("norm_in"):
        inv_in, unit_in = norm_stats(inputs)
        normed_own = (unit_in * gain_in).astype(BF16)
        normed_own, cotangent_parts = tie(normed_own, cotangent_parts)
    with jax.named_scope("rehome_cotangent"):
        extended = rehome_planes(cotangent_parts)
    with jax.named_scope("gather_normed"):
        normed = gather_first(normed_own)
        normed = gather_last(normed)
        *normed, qkv_w, out_piece, extended = tie(*normed, qkv_w, out_piece, extended)
    with jax.named_scope("weights_out"):
        out_w = from_owners(out_piece)
    with jax.named_scope("gather_upstream"):
        own_routes = extended[:, width : width + top]
        upstream_own = extended[:, :width].astype(F32) * live_own
        upstream = gather_first(jnp.concatenate([upstream_own.astype(BF16), extended[:, width:]], axis=1))
    with jax.named_scope("qkv"):
        lin, squares = run_project(normed, qkv_w, wide)
        inv_qk = lax.rsqrt(sum_rows(jnp.stack([squares[0], squares[8]], axis=0)) / width + EPS).T
        *upstream, inv_qk, out_w, gate_up_piece = tie(*upstream, inv_qk, out_w, gate_up_piece)
        upstream = gather_last(upstream)
    with jax.named_scope("weights_gate_up"):
        gate_up_w = from_owners(gate_up_piece)
    pick = (jnp.arange(HEADS, dtype=jnp.int32)[None, :] == jnp.stack(head_ids)[:, None]).astype(F32)

    def head_gain(gain):
        spread = gain.reshape(1, HEADS, head_size) * pick[:, :, None]
        return jnp.sum(spread, axis=1).reshape(1, wide)

    gains = (head_gain(gain_query), head_gain(gain_key))
    attention = (chips, heads, head_size, rows_here)
    mixed, *kept = run_attend_forward(lin, inv_qk, gains, angles, *attention)
    if not heads_spread:
        out_w = jnp.concatenate([lax.dynamic_slice_in_dim(out_w, h * head_size, head_size, 0) for h in head_ids], axis=0)
    with jax.named_scope("out_proj"):
        out_split = split_matmul(mixed, out_w, False, 6)
        upstream_full = jnp.concatenate(upstream, axis=0)
        upstream_full, *out_split = tie(upstream_full, *out_split)
        residual = inputs + scatter_chips(tuple(out_split))

    with jax.named_scope("gather_middle"):
        inv_mid, unit_mid = norm_stats(residual)
        middle_own = (unit_mid * gain_mid).astype(BF16)
        middle_own, gate_up_w, down_piece = tie(middle_own, gate_up_w, down_piece)
        middle = gather_last(gather_first(middle_own))
    with jax.named_scope("weights_down"):
        down_w = from_owners(down_piece).reshape(parts, experts, own_hidden, width)
        if not fast:
            down_w = down_w.transpose(1, 0, 2, 3).reshape(1, experts, parts * own_hidden, width)
    with jax.named_scope("router"):
        logits = dot_nt(router[:experts], middle_own)
        router_expo = jnp.exp(logits - jnp.max(logits, axis=0, keepdims=True))
        router_probs = router_expo / jnp.sum(router_expo, axis=0, keepdims=True)
        expert_ids = jnp.arange(experts, dtype=F32)
        chosen = jnp.sum(
            (own_routes.astype(F32).T[None, :, :] == expert_ids[:, None, None]).astype(F32), axis=1
        )
    with jax.named_scope("experts"):
        act, lin_grad, mix_grad = run_experts(middle, upstream, gate_up_w, down_w, router, experts, top)
        middle_split = split_matmul(lin_grad, gate_up_w, True, 14)

    with jax.named_scope("middle_grad"):
        *middle_split, mix_grad, act = tie(*middle_split, mix_grad, act)
        middle_first = scatter_first(tuple(middle_split))
        mix_grad_own = mix_grad[:rows_here].T
        for step in range(1, chips):
            part = mix_grad[step * rows_here : (step + 1) * rows_here].T
            mix_grad_own = mix_grad_own + swap(part, "chip", step)
        mix_grad_own = mix_grad_own[:experts]
    with jax.named_scope("w_down_grad"):
        if fast:
            down_total = run_down_grad(act, upstream_full, width, experts, parts)
        else:
            down_total = dot_tn(act, upstream_full[:, :width]).astype(BF16)
            down_total = down_total.reshape(experts, parts, own_hidden, width).transpose(1, 0, 2, 3)
        down_total = down_total.reshape(parts * experts * own_hidden, width)
        down_part = to_owners(down_total)
    with jax.named_scope("w_gate_up_grad"):
        gate_up_total = run_weight_grad(middle, lin_grad, 14)
    with jax.named_scope("middle_grad"):
        passed = scatter_pass(middle_first)
        *passed, gate_up_total = tie(*passed, gate_up_total)
        arrived = scatter_second(tuple(passed))
        prob_grad = mix_grad_own * chosen
        logit_grad = (router_probs * (prob_grad - jnp.sum(router_probs * prob_grad, axis=0, keepdims=True))).astype(BF16)
        middle_grad = scatter_sum(middle_first, arrived) + dot_tn(logit_grad, router[:experts])
        resid_part, gain_mid_grad = norm_back(middle_grad, unit_mid, inv_mid, gain_mid)
        resid_grad = upstream_own + resid_part
        branch_own = resid_grad.astype(BF16)
    with jax.named_scope("gather_branch"):
        branch_own, down_part, gate_up_total = tie(branch_own, down_part, gate_up_total)
        gate_up_part = to_owners(gate_up_total)
        branch = gather_first(branch_own)
    with jax.named_scope("output"):
        act, branch[0] = tie(act, branch[0])
        sum_split = split_matmul(act, down_w, False, 8)
    with jax.named_scope("mixed_grad"):
        branch = gather_last(branch)
        branch, sum_split = tie_lists(branch, sum_split)
        mixed_grad = run_back(branch, out_w, min(wide, 256))
        sum_first = scatter_first(tuple(sum_split))
    query_back, key_back, value_back, gain_grads, row_sums = run_attend_backward(
        mixed_grad, lin, kept, inv_qk, gains, angles, *attention
    )

    with jax.named_scope("qk_back"):
        *sum_first, row_sums = tie(*sum_first, row_sums)
        sum_first = tuple(sum_first)
        means = (sum_rows(jnp.stack([row_sums[0], row_sums[8]], axis=0)) / width).T
    with jax.named_scope("w_out_grad"):
        out_total = run_out_grad(mixed, branch)
        if not heads_spread:
            spread = jnp.zeros((width, width), BF16)
            for i, head in enumerate(head_ids):
                spread = lax.dynamic_update_slice_in_dim(
                    spread, out_total[i * head_size : (i + 1) * head_size], head * head_size, 0
                )
            out_total = spread
    with jax.named_scope("qk_back"):
        passed = scatter_pass(sum_first)
        *passed, means, out_total, gate_up_part = tie(*passed, means, out_total, gate_up_part)
        out_part = to_owners(out_total)
        arrived = scatter_second(tuple(passed))
        qkv_grad = run_finish((query_back, key_back, value_back), lin, gains, inv_qk, means, rows_here)
    with jax.named_scope("output"):
        expert_sum = scatter_sum(sum_first, arrived)
        output_low = ((residual + expert_sum) * live_own).astype(BF16)
    with jax.named_scope("normed_grad"):
        normed_split = split_matmul(qkv_grad, qkv_w, True, 11)
        *normed_split, output_low, qkv_grad = tie(*normed_split, output_low, qkv_grad)
        normed_first = scatter_first(tuple(normed_split))
    with jax.named_scope("w_qkv_grad"):
        qkv_total = run_weight_grad(normed, qkv_grad, 13)
    with jax.named_scope("normed_grad"):
        passed = scatter_pass(normed_first)
        *passed, qkv_total, out_part = tie(*passed, qkv_total, out_part)
        qkv_part = to_owners(qkv_total)
        arrived = scatter_second(tuple(passed))
        normed_grad = scatter_sum(normed_first, arrived)
        input_part, gain_in_grad = norm_back(normed_grad, unit_in, inv_in, gain_in)
        input_low = (resid_grad + input_part).astype(BF16)
    with jax.named_scope("input_grad"):
        input_parts = home_planes(input_low)

    if fast:
        with jax.named_scope("plane_gathers"):
            wide_first = gather_first(jnp.concatenate([gate_up_part, down_part, out_part], axis=0))
            wide_first, (input_parts, output_low) = tie_lists(wide_first, (input_parts, output_low))
            wide_last = gather_last(wide_first)
    with jax.named_scope("output"):
        output_parts = home_planes(output_low)
    with jax.named_scope("small_grads"):
        router_grad = dot(logit_grad, middle_own)

        def spread_heads(which):
            by_head = gain_grads[8 * which].reshape(heads, 1, head_size) * pick[:, :, None]
            return jnp.sum(by_head, axis=0).reshape(1, width)

        small_grads = jnp.concatenate(
            [gain_in_grad[None], spread_heads(0), spread_heads(1), gain_mid_grad[None], router_grad], axis=0
        )
        by_owner = small_grads.reshape(small_grads.shape[0], shards, shard_rows).transpose(1, 0, 2)
        small_sum = sum_chips(jnp.sum(exchange(by_owner, "shard"), axis=0))
        small_sum = small_sum + swap(small_sum, "core", 1)

    def everywhere(part):
        return lax.all_gather(part, ("chip", "core"), axis=0, tiled=False).reshape((chips, 2) + part.shape)

    def plane_parts(pieces):
        own = list(pieces)
        if len(own) != chips:
            own = own[:1] + [jnp.concatenate(own[i : i + 2], axis=0) for i in range(1, len(own), 2)]
        return own + [swap(v, "core", 1) for v in own]

    def shapes(count, *shape):
        return [jax.ShapeDtypeStruct(shape, F32)] * count

    if fast:
        with jax.named_scope("plane_gathers"):
            wide_last, (input_parts, small_sum) = tie_lists(wide_last, (input_parts, small_sum))
            qkv_first = gather_first(qkv_part)
            wide_parts = plane_parts(wide_last)
        input_grad = home_chips(input_parts)
        with jax.named_scope("w_down_grad"):
            (w_down_grad,) = place(
                functools.partial(place_rows, chips), where, wide_parts,
                (((own_hidden, width), lambda i, where: (half_rows // own_hidden + i, 0)),),
                shapes(1, experts, shard_hidden, width),
                ((1, shard_hidden, width), lambda i, where: (i, 0, 0)),
                (experts,), "place_down",
            )
        with jax.named_scope("w_out_grad"):
            out_at = half_rows + experts * own_hidden
            (w_out_grad,) = place(
                functools.partial(place_rows, chips), where, wide_parts,
                (((head_size // 2, width // 4), lambda i, where: (out_at // (head_size // 2), i)),),
                shapes(1, 1, shard_rows, width),
                ((1, shard_rows, width // 4), lambda i, where: (0, 0, i)),
                (4,), "place_out",
            )
            w_out_grad = w_out_grad.reshape(shard_rows, width)
        with jax.named_scope("w_gate_up_grad"):
            columns = jnp.concatenate([wanted + 2 * own_hidden * ((chip ^ step) - chip) for step in range(chips)])
            order = (columns[:, None] == jnp.arange(hidden, dtype=jnp.int32)[None, :]).astype(BF16)
            tile = parts * own_hidden
            w_gate_grad, w_up_grad = place(
                functools.partial(place_hidden, chips), where, wide_parts,
                (
                    ((half_rows, tile), lambda i, where: (0, i)),
                    ((half_rows, tile), lambda i, where: (0, experts + i)),
                ),
                shapes(2, experts, 2, half_rows, hidden),
                ((1, 2, half_rows, hidden), lambda i, where: (i, 0, 0, 0)),
                (experts,), "place_gate_up", (order,),
            )
            w_gate_grad = w_gate_grad.reshape(experts, shard_rows, hidden)
            w_up_grad = w_up_grad.reshape(experts, shard_rows, hidden)
        with jax.named_scope("w_qkv_grad"):
            tile = 64

            qkv_first, (w_down_grad, w_out_grad, w_gate_grad, w_up_grad) = tie_lists(
                qkv_first, (w_down_grad, w_out_grad, w_gate_grad, w_up_grad)
            )
            output = home_chips(output_parts)
            qkv_parts, (input_grad, output) = tie_lists(plane_parts(gather_last(qkv_first)), (input_grad, output))
            w_query_grad, w_key_grad, w_value_grad = (
                v.reshape(shard_rows, width)
                for v in place(
                    functools.partial(place_heads, chips, heads, head_size), where, qkv_parts,
                    (((tile, 3 * wide), lambda i, where: (i, 0)),),
                    shapes(3, 2, half_rows, width),
                    ((2, tile, width), lambda i, where: (0, i, 0)),
                    (half_rows // tile,), "place_heads",
                )
            )
    else:
        input_grad, output = home_chips(input_parts), home_chips(output_parts)
        spread = everywhere(down_part).reshape(chips, 2, experts, own_hidden, width)
        w_down_grad = spread.transpose(2, 0, 1, 3, 4).reshape(experts, shard_hidden, width).astype(F32)
        spread = everywhere(gate_up_part).reshape(chips, 2, half_rows, 2, experts, shards, 2 * own_hidden)
        spread = spread.transpose(3, 4, 1, 2, 5, 0, 6).reshape(2, experts, shard_rows, hidden).astype(F32)
        w_gate_grad, w_up_grad = spread[0], spread[1]
        if heads_spread:
            w_out_grad = everywhere(out_part).reshape(shard_rows, width).astype(F32)
        else:
            spread = lax.psum(out_part.astype(F32), "chip")
            w_out_grad = lax.all_gather(spread, "core", axis=0, tiled=True)

        def heads_back(part, count):
            spread = everywhere(part).reshape(chips, 2, half_rows, count, heads, head_size)
            return spread.transpose(3, 1, 2, 4, 0, 5).reshape(count, shard_rows, width).astype(F32)

        w_query_grad, w_key_grad, w_value_grad = heads_back(qkv_part, 3)
    return (
        output,
        input_grad,
        small_sum[0],
        w_query_grad,
        w_key_grad,
        w_value_grad,
        small_sum[1],
        small_sum[2],
        w_out_grad,
        small_sum[3],
        small_sum[4:].T,
        w_gate_grad,
        w_up_grad,
        w_down_grad,
    )


def solution(mesh):
    reps, shards = mesh.devices.shape
    split = Mesh(mesh.devices.reshape(reps // 2, 2, shards), ("chip", "core", "shard"))
    rows = P(("chip", "core", "shard"), None)
    first, second = P("shard", None), P(None, "shard", None)
    gain = P("shard")
    in_specs = (
        rows, rows, P(("chip", "core"), None), rows, gain, first, first, first, gain, gain, first, gain, first,
        second, second, second,
    )
    out_specs = (rows, rows, gain, first, first, first, gain, gain, first, gain, first, second, second, second)
    return jax.shard_map(body, mesh=split, in_specs=in_specs, out_specs=out_specs, check_vma=False)
```

```python
import functools

import jax
import jax.numpy as jnp
from jax import lax
from jax.experimental import pallas as pl
from jax.experimental.pallas import tpu as pltpu
from jax.sharding import Mesh
from jax.sharding import PartitionSpec as P

HEADS = 16
EPS = 1e-05
THETA = 10000.0
MASKED = -1e30
FAR = 1 << 30
F32 = jnp.float32
BF16 = jnp.bfloat16
VMEM_BYTES = 56 * 1024 * 1024


def dot(left, right):
    return jnp.dot(left, right, preferred_element_type=F32)


def dot_nt(left, right):
    return lax.dot_general(left, right, (((1,), (1,)), ((), ())), preferred_element_type=F32)


def dot_tn(left, right):
    return lax.dot_general(left, right, (((0,), (0,)), ((), ())), preferred_element_type=F32)


def tie(*values):
    return lax.optimization_barrier(values)


def tie_lists(*lists):
    return lax.optimization_barrier([list(values) for values in lists])


def swap(value, axis, step):
    size = lax.axis_size(axis)
    return lax.ppermute(value, axis, [(i, i ^ step) for i in range(size)])


def exchange(parts, axis):
    me = lax.axis_index(axis)
    out = parts
    for step in range(1, lax.axis_size(axis)):
        sent = lax.dynamic_index_in_dim(parts, me ^ step, 0, keepdims=True)
        out = lax.dynamic_update_slice_in_dim(out, swap(sent, axis, step), me ^ step, 0)
    return out


def gather_first(block):
    chips = lax.axis_size("chip")
    if chips != 4:
        return [block] + [swap(block, "chip", step) for step in range(1, chips)]
    half = block.shape[0] // 2
    top, low = block[:half], block[half:]
    two_top, one_low = swap(top, "chip", 2), swap(low, "chip", 1)
    one_top, two_low = swap(top, "chip", 1), swap(low, "chip", 2)
    return [block, one_top, one_low, two_top, two_low]


def gather_last(pieces):
    if lax.axis_size("chip") != 4:
        return pieces
    return pieces + [swap(pieces[3], "chip", 1), swap(pieces[2], "chip", 2)]


def scatter_first(split):
    if len(split) == 2:
        return split
    own_left, own_right, to_one, to_two, keep_left, keep_right = split
    return (own_left, own_right, swap(to_one, "chip", 1), swap(to_two, "chip", 2), keep_left, keep_right)


def scatter_pass(first):
    if len(first) == 2:
        return (first[1][0],)
    _, _, from_one, from_two, keep_left, keep_right = first
    return (
        (keep_left.astype(F32) + from_one[1].astype(F32)).astype(BF16),
        (keep_right.astype(F32) + from_two[1].astype(F32)).astype(BF16),
    )


def scatter_second(passed):
    if len(passed) == 1:
        return list(passed)
    return [swap(passed[0], "chip", 2), swap(passed[1], "chip", 1)]


def scatter_sum(first, arrived):
    if len(first) == 2:
        own, others = first
        for step, other in enumerate(tuple(arrived) + tuple(others[1:])):
            own = own + swap(other, "chip", step + 1).astype(F32)
        return own
    own_left, own_right, from_one, from_two, _, _ = first
    return jnp.concatenate(
        [
            own_left + from_one[0].astype(F32) + arrived[0].astype(F32),
            own_right + from_two[0].astype(F32) + arrived[1].astype(F32),
        ],
        axis=1,
    )


def scatter_chips(split):
    first = scatter_first(split)
    return scatter_sum(first, scatter_second(scatter_pass(first)))


def sum_chips(value):
    step = 1
    while step < lax.axis_size("chip"):
        value = value + swap(value, "chip", step)
        step *= 2
    return value


def sum_rows(values):
    chips = lax.axis_size("chip")
    total = values.reshape(values.shape[0], chips, -1)
    step = 1
    while step < chips:
        other = swap(total, "chip", step)
        total = total + jnp.concatenate([other[:, i ^ step : (i ^ step) + 1] for i in range(chips)], axis=1)
        step *= 2
    return total.reshape(values.shape)


def rehome_chips(rows):
    chips = lax.axis_size("chip")
    parts = rows.reshape(chips, rows.shape[0] // chips, rows.shape[1])
    return lax.all_to_all(parts, "chip", 0, 0, tiled=True)


def rehome_planes(parts):
    return lax.all_to_all(parts, "shard", 0, 0, tiled=True).reshape(-1, parts.shape[2])


def home_planes(rows):
    shards = lax.axis_size("shard")
    parts = rows.reshape(shards, rows.shape[0] // shards, rows.shape[1])
    return lax.all_to_all(parts, "shard", 0, 0, tiled=True)


def home_chips(parts):
    return lax.all_to_all(parts, "chip", 0, 0, tiled=True).reshape(-1, parts.shape[2])


ANYWHERE = pl.BlockSpec(memory_space=pl.ANY)


def run(kernel, name, micros, grid, in_specs, out_specs, out_shape, args, scratch=()):
    return pl.pallas_call(
        kernel,
        grid=grid,
        in_specs=in_specs,
        out_specs=out_specs,
        out_shape=out_shape,
        scratch_shapes=list(scratch),
        compiler_params=pltpu.CompilerParams(vmem_limit_bytes=VMEM_BYTES),
        cost_estimate=pl.CostEstimate(flops=micros * 550_000_000, bytes_accessed=1024, transcendentals=0),
        name=name,
    )(*args)


def load_rows(pieces, target, sems):
    copies, at = [], 0
    for i, piece in enumerate(pieces):
        copies.append(pltpu.make_async_copy(piece, target.at[pl.ds(at, piece.shape[0]), :], sems.at[i]))
        at += piece.shape[0]
    for copy in copies:
        copy.start()
    for copy in copies:
        copy.wait()


def rows_scratch(pieces):
    rows = sum(piece.shape[0] for piece in pieces)
    return [pltpu.VMEM((rows, pieces[0].shape[1]), BF16), pltpu.SemaphoreType.DMA((len(pieces),))]


def column_sums(values):
    ones = jnp.ones((8, values.shape[1]), F32)
    return lax.dot_general(
        ones, values, (((1,), (1,)), ((), ())), precision=lax.Precision.HIGHEST, preferred_element_type=F32
    )


def project_kernel(count, *refs):
    pieces, (weight, out, squares, rows, sems) = refs[:count], refs[count:]

    @pl.when(pl.program_id(0) == 0)
    def _():
        load_rows(pieces, rows, sems)

    result = dot(rows[...], weight[...])
    out[...] = result
    squares[...] = column_sums(result * result)


def run_project(pieces, weight, tile):
    depth, columns = weight.shape
    rows = sum(piece.shape[0] for piece in pieces)
    steps = columns // tile
    return run(
        functools.partial(project_kernel, len(pieces)), "project", 16, (steps,),
        [ANYWHERE] * len(pieces) + [pl.BlockSpec((depth, tile), lambda i: (0, i))],
        [pl.BlockSpec((rows, tile), lambda i: (0, i)), pl.BlockSpec((8, rows), lambda i: (i, 0))],
        [jax.ShapeDtypeStruct((rows, columns), F32), jax.ShapeDtypeStruct((8 * steps, rows), F32)],
        (*pieces, weight),
        rows_scratch(pieces),
    )


def back_kernel(count, *refs):
    pieces, (weight, out, rows, sems) = refs[:count], refs[count:]

    @pl.when(pl.program_id(0) == 0)
    def _():
        load_rows(pieces, rows, sems)

    out[...] = dot_nt(rows[...], weight[...]).astype(BF16)


def run_back(pieces, weight, tile):
    rows = sum(piece.shape[0] for piece in pieces)
    return run(
        functools.partial(back_kernel, len(pieces)), "back", 7, (weight.shape[0] // tile,),
        [ANYWHERE] * len(pieces) + [pl.BlockSpec((tile, weight.shape[1]), lambda i: (i, 0))],
        pl.BlockSpec((rows, tile), lambda i: (0, i)),
        jax.ShapeDtypeStruct((rows, weight.shape[0]), BF16),
        (*pieces, weight),
        rows_scratch(pieces),
    )


def join_experts(ref):
    parts, experts, units, columns = ref.shape
    if parts == 1:
        return ref[...].reshape(experts * units, columns)
    return jnp.concatenate([ref[:, expert].reshape(parts * units, columns) for expert in range(experts)], axis=0)


def split_kernel(block, turned, left, left_w, right_w, own_left, own_right, to_one, to_two, keep_left, keep_right):
    def product(weight):
        if turned:
            return dot_nt(left[...], weight[...])
        return dot(left[...], weight[...] if len(weight.shape) == 2 else join_experts(weight))

    result = product(left_w)
    own_left[...] = result[:block]
    to_one[0] = result[block : 2 * block].astype(BF16)
    keep_left[...] = result[2 * block : 3 * block].astype(BF16)
    to_one[1] = result[3 * block :].astype(BF16)
    result = product(right_w)
    own_right[...] = result[:block]
    keep_right[...] = result[block : 2 * block].astype(BF16)
    to_two[0] = result[2 * block : 3 * block].astype(BF16)
    to_two[1] = result[3 * block :].astype(BF16)


def split_matmul(left, weight, turned, micros):
    chips = lax.axis_size("chip")
    rows = left.shape[0]
    block = rows // chips
    width = weight.shape[0] if turned else weight.shape[-1]
    if chips != 4:
        if weight.ndim == 4:
            weight = weight.transpose(1, 0, 2, 3).reshape(-1, width)
        whole = (dot_nt if turned else dot)(left, weight)
        return (whole[:block], [whole[i * block : (i + 1) * block].astype(BF16) for i in range(1, chips)])
    half, tile = width // 2, 256
    steps = half // tile

    def weight_spec(first):
        if turned:
            return pl.BlockSpec((tile, weight.shape[1]), lambda i: (first + i, 0))
        return pl.BlockSpec((*weight.shape[:-1], tile), lambda i: (0,) * (weight.ndim - 1) + (first + i,))

    one = pl.BlockSpec((block, tile), lambda i: (0, i))
    two = pl.BlockSpec((2, block, tile), lambda i: (0, 0, i))
    wide, low = jax.ShapeDtypeStruct((block, half), F32), jax.ShapeDtypeStruct((block, half), BF16)
    pair = jax.ShapeDtypeStruct((2, block, half), BF16)
    return run(
        functools.partial(split_kernel, block, turned), "split_matmul", micros, (steps,),
        [pl.BlockSpec(left.shape, lambda i: (0, 0)), weight_spec(0), weight_spec(steps)],
        [one, one, two, two, one, one],
        [wide, wide, pair, pair, low, low],
        (left, weight, weight),
    )


def weight_grad_kernel(count, tile, *refs):
    pieces, (grad, out, rows, sems) = refs[:count], refs[count:]

    @pl.when(pl.program_id(0) == 0)
    def _():
        load_rows(pieces, rows, sems)

    columns = pl.ds(pl.multiple_of(pl.program_id(0) * tile, tile), tile)
    out[...] = dot_tn(rows[:, columns], grad[...]).astype(BF16)


def run_weight_grad(pieces, grad, micros, columns=None):
    tile = 512
    depth, columns = pieces[0].shape[1], columns or grad.shape[1]
    return run(
        functools.partial(weight_grad_kernel, len(pieces), tile), "weight_grad", micros, (depth // tile,),
        [ANYWHERE] * len(pieces) + [pl.BlockSpec((grad.shape[0], columns), lambda i: (0, 0))],
        pl.BlockSpec((tile, columns), lambda i: (i, 0)),
        jax.ShapeDtypeStruct((depth, columns), BF16),
        (*pieces, grad),
        rows_scratch(pieces),
    )


def down_grad_kernel(experts, parts, act, upstream, out):
    result = dot_tn(act[...], upstream[...]).astype(BF16)
    own = result.shape[0] // (experts * parts)
    for expert in range(experts):
        for part in range(parts):
            at = (expert * parts + part) * own
            out[part, expert * own : (expert + 1) * own, :] = result[at : at + own]


def run_down_grad(act, upstream, width, experts, parts):
    hidden, tile = act.shape[1], 512
    return run(
        functools.partial(down_grad_kernel, experts, parts), "down_grad", 3, (width // tile,),
        [pl.BlockSpec(act.shape, lambda i: (0, 0)), pl.BlockSpec((upstream.shape[0], tile), lambda i: (0, i))],
        pl.BlockSpec((parts, hidden // parts, tile), lambda i: (0, 0, i)),
        jax.ShapeDtypeStruct((parts, hidden // parts, width), BF16),
        (act, upstream),
    )


def out_grad_kernel(count, tile, *refs):
    pieces, (mixed, out, rows, sems) = refs[:count], refs[count:]

    @pl.when(pl.program_id(0) == 0)
    def _():
        load_rows(pieces, rows, sems)

    columns = pl.ds(pl.multiple_of(pl.program_id(0) * tile, tile), tile)
    out[...] = dot_tn(mixed[...], rows[:, columns]).astype(BF16)


def run_out_grad(mixed, pieces):
    tile, width = 512, pieces[0].shape[1]
    return run(
        functools.partial(out_grad_kernel, len(pieces), tile), "out_grad", 7, (width // tile,),
        [ANYWHERE] * len(pieces) + [pl.BlockSpec(mixed.shape, lambda i: (0, 0))],
        pl.BlockSpec((mixed.shape[1], tile), lambda i: (0, i)),
        jax.ShapeDtypeStruct((mixed.shape[1], width), BF16),
        (*pieces, mixed),
        rows_scratch(pieces),
    )


def lane_roll(values):
    return pltpu.roll(values, values.shape[1] // 2, 1)


def take_block(ref, block, chips, block_rows):
    piece = block_rows // chips
    at = lambda chip: chip * block_rows + block * piece
    return jnp.concatenate([ref[at(chip) : at(chip) + piece, :] for chip in range(chips)], axis=0)


def put_block(ref, block, chips, block_rows, values):
    piece = block_rows // chips
    for chip in range(chips):
        at = chip * block_rows + block * piece
        ref[at : at + piece, :] = values[chip * piece : (chip + 1) * piece]


def attend_forward(
    chips, block_rows, scale,
    query_ref, key_ref, value_ref, inv_ref, gain_q, gain_k, cos_ref, sin_ref, pos_ref, key_pos_ref,
    mixed, query_rot, key_rot, value_low, lse,
):
    blocks = inv_ref.shape[0] // block_rows
    for block in range(blocks):
        rows = pl.ds(block * block_rows, block_rows)
        cosine, sine = cos_ref[rows, :], sin_ref[rows, :]
        inv = take_block(inv_ref, block, chips, block_rows)
        query = take_block(query_ref, block, chips, block_rows) * inv[:, 0:1] * gain_q[...]
        query_rot[rows, :] = (query * cosine + lane_roll(query) * sine).astype(BF16)
        key = take_block(key_ref, block, chips, block_rows) * inv[:, 1:2] * gain_k[...]
        key_rot[rows, :] = (key * cosine + lane_roll(key) * sine).astype(BF16)
        value_low[rows, :] = take_block(value_ref, block, chips, block_rows).astype(BF16)
    for block in range(blocks):
        rows = pl.ds(block * block_rows, block_rows)
        seen = pl.ds(0, (block + 1) * block_rows)
        scores = dot_nt(query_rot[rows, :], key_rot[seen, :]) * scale
        scores = jnp.where(key_pos_ref[:, seen] <= pos_ref[rows, :], scores, MASKED)
        peak = jnp.max(scores, axis=-1, keepdims=True)
        expo = jnp.exp(scores - peak)
        total = jnp.sum(expo, axis=-1, keepdims=True)
        probs_low = (expo * (1.0 / total)).astype(BF16)
        put_block(mixed, block, chips, block_rows, dot(probs_low, value_low[seen, :]).astype(BF16))
        lse[rows, :] = jnp.broadcast_to(peak + jnp.log(total), (block_rows, lse.shape[1]))


def attend_backward(
    chips, block_rows, scale,
    grad_ref, query_ref, key_ref, query_rot, key_rot, value_low, lse, gain_q, gain_k,
    inv_ref, cos_ref, sin_ref, pos_ref, key_pos_ref,
    query_back, key_back, value_back, gains, sums_ref,
    key_sum, value_sum,
):
    blocks = inv_ref.shape[0] // block_rows

    @pl.when(pl.program_id(0) == 0)
    def _():
        sums_ref[...] = jnp.zeros_like(sums_ref)

    key_sum[...] = jnp.zeros_like(key_sum)
    value_sum[...] = jnp.zeros_like(value_sum)
    for block in range(blocks):
        rows = pl.ds(block * block_rows, block_rows)
        seen = pl.ds(0, (block + 1) * block_rows)
        query = query_rot[rows, :]
        grad = take_block(grad_ref, block, chips, block_rows)
        scores = dot_nt(query, key_rot[seen, :]) * scale
        scores = jnp.where(key_pos_ref[:, seen] <= pos_ref[rows, :], scores, MASKED)
        probs = jnp.exp(scores - lse[rows, 0:1])
        probs_grad = dot_nt(grad, value_low[seen, :])
        weighted = jnp.sum(probs * probs_grad, axis=-1, keepdims=True)
        score_grad = (probs * (probs_grad - weighted)).astype(BF16)
        query_grad = dot(score_grad, key_rot[seen, :]) * scale
        turned = query_grad * cos_ref[rows, :] - lane_roll(query_grad) * sin_ref[rows, :]
        put_block(query_back, block, chips, block_rows, turned)
        key_sum[seen, :] += dot_tn(score_grad, query)
        value_sum[seen, :] += dot_tn(probs.astype(BF16), grad)
    for block in range(blocks):
        rows = pl.ds(block * block_rows, block_rows)
        key_grad = key_sum[rows, :] * scale
        turned = key_grad * cos_ref[rows, :] - lane_roll(key_grad) * sin_ref[rows, :]
        put_block(key_back, block, chips, block_rows, turned)
        put_block(value_back, block, chips, block_rows, value_sum[rows, :].astype(BF16))
    for which, (lin, back, gain) in enumerate(((query_ref, query_back, gain_q), (key_ref, key_back, gain_k))):
        product = back[...] * lin[...] * inv_ref[:, which : which + 1]
        sums_ref[pl.ds(8 * which, 8), :] += column_sums(product * gain[...])
        gains[pl.ds(8 * which, 8), :] = jnp.broadcast_to(jnp.sum(product, axis=0, keepdims=True), (8, product.shape[1]))


def attention_specs(rows, head_size, heads):
    column = pl.BlockSpec((rows, head_size), lambda h: (0, h))
    whole = lambda shape: pl.BlockSpec(shape, lambda h: (0, 0))
    part = [pl.BlockSpec((rows, head_size), lambda h, which=which: (0, which * heads + h)) for which in range(3)]
    gain = pl.BlockSpec((1, head_size), lambda h: (0, h))
    return column, whole, part, gain


def run_attend_forward(lin, inv, gains, angles, chips, heads, head_size, block_rows):
    rows, wide = lin.shape[0], heads * head_size
    column, whole, part, gain = attention_specs(rows, head_size, heads)
    low = jax.ShapeDtypeStruct((rows, wide), BF16)
    return run(
        functools.partial(attend_forward, chips, block_rows, head_size**-0.5), "attend_forward", 17, (heads,),
        part + [whole(inv.shape), gain, gain] + [whole(v.shape) for v in angles],
        [column] * 5,
        [low, low, low, low, jax.ShapeDtypeStruct((rows, wide), F32)],
        (lin, lin, lin, inv, *gains, *angles),
    )


def run_attend_backward(mixed_grad, lin, kept, inv, gains, angles, chips, heads, head_size, block_rows):
    rows, wide = mixed_grad.shape
    column, whole, part, gain = attention_specs(rows, head_size, heads)
    full = jax.ShapeDtypeStruct((rows, wide), F32)
    return run(
        functools.partial(attend_backward, chips, block_rows, head_size**-0.5), "attend_backward", 20, (heads,),
        [column, part[0], part[1]] + [column] * 4 + [gain, gain, whole(inv.shape)] + [whole(v.shape) for v in angles],
        [column] * 3 + [pl.BlockSpec((16, head_size), lambda h: (0, h)), whole((16, rows))],
        [full, full, jax.ShapeDtypeStruct((rows, wide), BF16), jax.ShapeDtypeStruct((16, wide), F32),
         jax.ShapeDtypeStruct((16, rows), F32)],
        (mixed_grad, lin, lin, *kept, *gains, inv, *angles),
        [pltpu.VMEM((rows, head_size), F32)] * 2,
    )


def finish_kernel(wide, query_back, key_back, value_back, lin, gain_q, gain_k, inv_ref, mean_ref, out):
    for which, (back, gain) in enumerate(((query_back, gain_q), (key_back, gain_k))):
        inv = inv_ref[:, which : which + 1]
        columns = slice(which * wide, (which + 1) * wide)
        unit = lin[:, columns] * inv
        out[:, columns] = (inv * (gain[...] * back[...] - unit * mean_ref[:, which : which + 1])).astype(BF16)
    out[:, 2 * wide :] = value_back[...]


def run_finish(backs, lin, gains, inv, means, tile):
    rows, wide = backs[0].shape
    spec = lambda columns: pl.BlockSpec((tile, columns), lambda i: (i, 0))
    gain = pl.BlockSpec((1, wide), lambda i: (0, 0))
    return run(
        functools.partial(finish_kernel, wide), "finish", 7, (rows // tile,),
        [spec(wide)] * 3 + [spec(3 * wide), gain, gain, spec(2), spec(2)],
        spec(3 * wide),
        jax.ShapeDtypeStruct((rows, 3 * wide), BF16),
        (*backs, lin, *gains, inv, means),
    )


def experts_kernel(count, experts, top, *refs):
    middles, upstreams, refs = refs[:count], refs[count : 2 * count], refs[2 * count :]
    gate_w, up_w, down_w, router_w, act_out, grad_out, mix_grad, middle, upstream, mix, middle_sems, upstream_sems = refs
    step, tile = pl.program_id(0), gate_w.shape[1]
    rows, depth = middle.shape
    lane = lax.broadcasted_iota(jnp.int32, (1, mix.shape[1]), 1)

    @pl.when(step == 0)
    def _():
        load_rows(middles, middle, middle_sems)
        load_rows(upstreams, upstream, upstream_sems)
        mix_grad[...] = jnp.zeros_like(mix_grad)
        logits = jnp.where(lane < experts, dot_nt(middle[...], router_w[...]), MASKED)
        expo = jnp.exp(logits - jnp.max(logits, axis=-1, keepdims=True))
        chosen = jnp.zeros_like(expo)
        for i in range(top):
            route = upstream[:, depth + i : depth + i + 1].astype(F32)
            chosen = chosen + jnp.where(route == lane.astype(F32), 1.0, 0.0)
        mix[...] = expo / jnp.sum(expo, axis=-1, keepdims=True) * chosen

    mine = lane == step
    mix_column = jnp.sum(jnp.where(mine, mix[...], 0.0), axis=-1, keepdims=True)
    gate = dot(middle[...], gate_w[...])
    up = dot(middle[...], up_w[...])
    back = dot_nt(upstream[:, :depth], down_w[...].reshape(tile, depth))
    sigma = 1.0 / (1.0 + jnp.exp(-gate))
    silu = gate * sigma
    act = silu * up
    mix_grad[...] += jnp.where(mine, jnp.sum(act * back, axis=-1, keepdims=True), 0.0)
    back = back * mix_column
    act_out[...] = (act * mix_column).astype(BF16)
    columns = pl.ds(pl.multiple_of(step * tile, tile), tile)
    up_columns = pl.ds(pl.multiple_of((experts + step) * tile, tile), tile)
    grad_out[:, columns] = (back * up * sigma * (1.0 + gate * (1.0 - sigma))).astype(BF16)
    grad_out[:, up_columns] = (back * silu).astype(BF16)


def run_experts(middles, upstreams, gate_up, down, router, experts, top):
    rows, depth = sum(piece.shape[0] for piece in middles), middles[0].shape[1]
    parts, _, units, _ = down.shape
    tile = parts * units
    whole = lambda shape: pl.BlockSpec(shape, lambda i: (0, 0))
    grad_shape, mix_shape = (rows, 2 * experts * tile), (rows, router.shape[0])
    buffers, sems = zip(rows_scratch(middles), rows_scratch(upstreams))
    return run(
        functools.partial(experts_kernel, len(middles), experts, top), "experts", 26, (experts,),
        [ANYWHERE] * (2 * len(middles))
        + [
            pl.BlockSpec((depth, tile), lambda i: (0, i)),
            pl.BlockSpec((depth, tile), lambda i: (0, experts + i)),
            pl.BlockSpec((parts, 1, units, depth), lambda i: (0, i, 0, 0)),
            whole(router.shape),
        ],
        [pl.BlockSpec((rows, tile), lambda i: (0, i)), whole(grad_shape), whole(mix_shape)],
        [
            jax.ShapeDtypeStruct((rows, experts * tile), BF16),
            jax.ShapeDtypeStruct(grad_shape, BF16),
            jax.ShapeDtypeStruct(mix_shape, F32),
        ],
        (*middles, *upstreams, gate_up, gate_up, down, router),
        [*buffers, pltpu.VMEM(mix_shape, F32), *sems],
    )


def part_owners(where_ref, chips):
    return [(where_ref[0] ^ step, where_ref[1] ^ turn) for turn in range(2) for step in range(chips)]


def place_heads(chips, heads, head_size, where_ref, *refs):
    parts, outs = refs[: 2 * chips], refs[2 * chips :]
    for part, (chip, core) in zip(parts, part_owners(where_ref, chips)):
        for which, out in enumerate(outs):
            for i in range(heads):
                first = (which * heads + i) * head_size
                column = pl.multiple_of((i * chips + chip) * head_size, head_size)
                out[core, :, pl.ds(column, head_size)] = part[:, first : first + head_size].astype(F32)


def place_hidden(chips, where_ref, *refs):
    count = 2 * chips
    order, outs = refs[2 * count], refs[2 * count + 1 :]
    owners = part_owners(where_ref, chips)
    for which, out in enumerate(outs):
        parts = refs[which * count : (which + 1) * count]
        for turn in range(2):
            row = jnp.concatenate([part[...] for part in parts[turn * chips : (turn + 1) * chips]], axis=1)
            out[0, owners[turn * chips][1]] = dot(row, order[...])


def place_rows(chips, where_ref, *refs):
    parts, out = refs[: 2 * chips], refs[-1]
    height = parts[0].shape[0]
    for part, (chip, core) in zip(parts, part_owners(where_ref, chips)):
        row = pl.multiple_of((2 * chip + core) * height, height)
        out[0, pl.ds(row, height), :] = part[...].astype(F32)


def place(kernel, where, parts, part_blocks, out_shapes, out_block, grid, name, extra=()):
    return pl.pallas_call(
        kernel,
        grid_spec=pltpu.PrefetchScalarGridSpec(
            num_scalar_prefetch=1,
            grid=grid,
            in_specs=[pl.BlockSpec(*block) for block in part_blocks for _ in parts]
            + [pl.BlockSpec(v.shape, lambda i, where: (0, 0)) for v in extra],
            out_specs=[pl.BlockSpec(*out_block)] * len(out_shapes),
        ),
        out_shape=out_shapes,
        compiler_params=pltpu.CompilerParams(vmem_limit_bytes=VMEM_BYTES),
        cost_estimate=pl.CostEstimate(flops=8 * 550_000_000, bytes_accessed=1024, transcendentals=0),
        name=name,
    )(where, *(parts * len(part_blocks)), *extra)


def norm_stats(values):
    inv_root = lax.rsqrt(jnp.mean(values * values, axis=-1, keepdims=True) + EPS)
    return (inv_root, values * inv_root)


def norm_back(gradient, unit_rows, inv_root, gain):
    scaled = gain * gradient
    rows_part = inv_root * (scaled - unit_rows * jnp.mean(unit_rows * scaled, axis=-1, keepdims=True))
    return (rows_part, jnp.sum(gradient * unit_rows, axis=0))


def body(
    tokens, cotangent, live_counts, routes, norm_in, w_query, w_key, w_value, norm_query, norm_key, w_out, norm_mid,
    w_router, w_gate, w_up, w_down,
):
    chips, shards = lax.axis_size("chip"), lax.axis_size("shard")
    chip, core = lax.axis_index("chip"), lax.axis_index("core")
    rows_here, width = tokens.shape
    head_size = width // HEADS
    heads = HEADS // chips
    wide = heads * head_size
    experts, top = w_gate.shape[0], routes.shape[1]
    piece = rows_here // chips
    group_rows = rows_here * shards
    shard_rows = w_query.shape[0]
    half_rows = shard_rows // 2
    shard_hidden, hidden = w_down.shape[1], w_gate.shape[2]
    own_hidden = shard_hidden // (2 * chips)
    parts = 2 * shards
    heads_spread = HEADS // shards == chips
    fast = chips == 4 and own_hidden % 16 == 0 and heads_spread
    where = jnp.stack([chip, core]).astype(jnp.int32)
    owners = ("shard", "core")

    def from_owners(part):
        return lax.all_gather(part, owners, axis=0, tiled=True)

    def to_owners(total):
        return lax.psum_scatter(total, owners, scatter_dimension=0, tiled=True)

    with jax.named_scope("rehome_tokens"):
        token_parts = rehome_chips(tokens)

    head_ids = [i * chips + chip for i in range(heads)]
    with jax.named_scope("weights_qkv"):
        qkv_piece = jnp.concatenate(
            [
                lax.dynamic_slice(w, (core * half_rows, head * head_size), (half_rows, head_size))
                for w in (w_query, w_key, w_value)
                for head in head_ids
            ],
            axis=1,
        )
        qkv_w = from_owners(qkv_piece)
    route_columns = jnp.pad(routes.astype(BF16), ((0, 0), (0, 128 - top)))
    extended = jnp.concatenate([cotangent, route_columns], axis=1)
    small = jnp.concatenate(
        [v.astype(F32)[None] for v in (norm_in, norm_query, norm_key, norm_mid)] + [w_router.astype(F32).T], axis=0
    )
    extended, token_parts = tie(extended, token_parts)
    with jax.named_scope("norm_in"):
        inputs = rehome_planes(token_parts).astype(F32)
    with jax.named_scope("small_gathers"):
        small_all = exchange(jnp.broadcast_to(small[None], (shards,) + small.shape), "shard")
        small_all = small_all.transpose(1, 0, 2).reshape(small.shape[0], width)
        gain_in, gain_query, gain_key, gain_mid = (small_all[i] for i in range(4))
        router = jnp.pad(small_all[4:], ((0, 8 - experts), (0, 0))).astype(BF16)
        counts = lax.ppermute(
            live_counts,
            ("chip", "core", "shard"),
            [
                ((i * 2 + k) * shards + j, (j * 2 + k) * shards + i)
                for i in range(chips)
                for k in range(2)
                for j in range(shards)
            ],
        )[0]
    with jax.named_scope("rehome_cotangent"):
        cotangent_parts = exchange(extended.reshape(chips, piece, extended.shape[1]), "chip")
    hidden_at = 2 * chip * own_hidden
    with jax.named_scope("weights_gate_up"):
        unit = jnp.arange(parts * own_hidden, dtype=jnp.int32)
        wanted = (unit // (2 * own_hidden)) * shard_hidden + hidden_at + unit % (2 * own_hidden)
        choose = (jnp.arange(hidden, dtype=jnp.int32)[:, None] == wanted[None, :]).astype(BF16)
        gate_up_rows = [lax.dynamic_slice_in_dim(w, core * half_rows, half_rows, 1) for w in (w_gate, w_up)]
        gate_up_piece = jnp.concatenate(
            [dot(w[expert], choose).astype(BF16) for w in gate_up_rows for expert in range(experts)], axis=1
        )
    down_piece = lax.dynamic_slice_in_dim(w_down, hidden_at + core * own_hidden, own_hidden, 1)
    down_piece = down_piece.reshape(experts * own_hidden, width)
    if heads_spread:
        out_piece = lax.dynamic_slice_in_dim(w_out, chip * head_size + core * (head_size // 2), head_size // 2, 0)
    else:
        out_piece = lax.dynamic_slice_in_dim(w_out, core * half_rows, half_rows, 0)

    starts = jnp.cumsum(counts) - counts
    chip_of = chip ^ jnp.arange(chips, dtype=jnp.int32)
    in_block = (chip_of[:, None] * piece + jnp.arange(piece, dtype=jnp.int32)[None, :]).reshape(1, rows_here)
    positions = (starts[:, None] + in_block).reshape(group_rows)
    live = (in_block < counts[:, None]).reshape(group_rows)
    live_own = live.astype(F32).reshape(shards, chips, piece)[:, 0].reshape(rows_here, 1)
    half_size = head_size // 2
    frequency = THETA ** (-jnp.arange(half_size, dtype=F32) * 2.0 / head_size)
    phases = positions.astype(F32)[:, None] * frequency[None, :]
    cosine, sine = jnp.cos(phases), jnp.sin(phases)
    angles = (
        jnp.concatenate([cosine, cosine], axis=1),
        jnp.concatenate([-sine, sine], axis=1),
        positions[:, None],
        jnp.where(live, positions, FAR)[None, :],
    )

    with jax.named_scope("norm_in"):
        inv_in, unit_in = norm_stats(inputs)
        normed_own = (unit_in * gain_in).astype(BF16)
        normed_own, cotangent_parts = tie(normed_own, cotangent_parts)
    with jax.named_scope("rehome_cotangent"):
        extended = rehome_planes(cotangent_parts)
    with jax.named_scope("gather_normed"):
        normed = gather_first(normed_own)
        normed = gather_last(normed)
        *normed, qkv_w, out_piece, extended = tie(*normed, qkv_w, out_piece, extended)
    with jax.named_scope("weights_out"):
        out_w = from_owners(out_piece)
    with jax.named_scope("gather_upstream"):
        own_routes = extended[:, width : width + top]
        upstream_own = extended[:, :width].astype(F32) * live_own
        upstream = gather_first(jnp.concatenate([upstream_own.astype(BF16), extended[:, width:]], axis=1))
    with jax.named_scope("qkv"):
        lin, squares = run_project(normed, qkv_w, wide)
        inv_qk = lax.rsqrt(sum_rows(jnp.stack([squares[0], squares[8]], axis=0)) / width + EPS).T
        *upstream, inv_qk, out_w, gate_up_piece = tie(*upstream, inv_qk, out_w, gate_up_piece)
        upstream = gather_last(upstream)
    with jax.named_scope("weights_gate_up"):
        gate_up_w = from_owners(gate_up_piece)
    pick = (jnp.arange(HEADS, dtype=jnp.int32)[None, :] == jnp.stack(head_ids)[:, None]).astype(F32)

    def head_gain(gain):
        spread = gain.reshape(1, HEADS, head_size) * pick[:, :, None]
        return jnp.sum(spread, axis=1).reshape(1, wide)

    gains = (head_gain(gain_query), head_gain(gain_key))
    attention = (chips, heads, head_size, rows_here)
    mixed, *kept = run_attend_forward(lin, inv_qk, gains, angles, *attention)
    if not heads_spread:
        out_w = jnp.concatenate([lax.dynamic_slice_in_dim(out_w, h * head_size, head_size, 0) for h in head_ids], axis=0)
    with jax.named_scope("out_proj"):
        out_split = split_matmul(mixed, out_w, False, 6)
        upstream_full = jnp.concatenate(upstream, axis=0)
        upstream_full, *out_split = tie(upstream_full, *out_split)
        residual = inputs + scatter_chips(tuple(out_split))

    with jax.named_scope("gather_middle"):
        inv_mid, unit_mid = norm_stats(residual)
        middle_own = (unit_mid * gain_mid).astype(BF16)
        middle_own, gate_up_w, down_piece = tie(middle_own, gate_up_w, down_piece)
        middle = gather_last(gather_first(middle_own))
    with jax.named_scope("weights_down"):
        down_w = from_owners(down_piece).reshape(parts, experts, own_hidden, width)
        if not fast:
            down_w = down_w.transpose(1, 0, 2, 3).reshape(1, experts, parts * own_hidden, width)
    with jax.named_scope("router"):
        logits = dot_nt(router[:experts], middle_own)
        router_expo = jnp.exp(logits - jnp.max(logits, axis=0, keepdims=True))
        router_probs = router_expo / jnp.sum(router_expo, axis=0, keepdims=True)
        expert_ids = jnp.arange(experts, dtype=F32)
        chosen = jnp.sum(
            (own_routes.astype(F32).T[None, :, :] == expert_ids[:, None, None]).astype(F32), axis=1
        )
    with jax.named_scope("experts"):
        act, lin_grad, mix_grad = run_experts(middle, upstream, gate_up_w, down_w, router, experts, top)
        middle_split = split_matmul(lin_grad, gate_up_w, True, 14)

    with jax.named_scope("middle_grad"):
        *middle_split, mix_grad, act = tie(*middle_split, mix_grad, act)
        middle_first = scatter_first(tuple(middle_split))
        mix_grad_own = mix_grad[:rows_here].T
        for step in range(1, chips):
            part = mix_grad[step * rows_here : (step + 1) * rows_here].T
            mix_grad_own = mix_grad_own + swap(part, "chip", step)
        mix_grad_own = mix_grad_own[:experts]
    with jax.named_scope("w_down_grad"):
        if fast:
            down_total = run_down_grad(act, upstream_full, width, experts, parts)
        else:
            down_total = dot_tn(act, upstream_full[:, :width]).astype(BF16)
            down_total = down_total.reshape(experts, parts, own_hidden, width).transpose(1, 0, 2, 3)
        down_total = down_total.reshape(parts * experts * own_hidden, width)
        down_part = to_owners(down_total)
    with jax.named_scope("w_gate_up_grad"):
        gate_up_total = run_weight_grad(middle, lin_grad, 4)
    with jax.named_scope("middle_grad"):
        passed = scatter_pass(middle_first)
        *passed, gate_up_total = tie(*passed, gate_up_total)
        arrived = scatter_second(tuple(passed))
        prob_grad = mix_grad_own * chosen
        logit_grad = (router_probs * (prob_grad - jnp.sum(router_probs * prob_grad, axis=0, keepdims=True))).astype(BF16)
        middle_grad = scatter_sum(middle_first, arrived) + dot_tn(logit_grad, router[:experts])
        resid_part, gain_mid_grad = norm_back(middle_grad, unit_mid, inv_mid, gain_mid)
        resid_grad = upstream_own + resid_part
        branch_own = resid_grad.astype(BF16)
    with jax.named_scope("gather_branch"):
        branch_own, down_part, gate_up_total = tie(branch_own, down_part, gate_up_total)
        gate_up_part = to_owners(gate_up_total)
        branch = gather_first(branch_own)
    with jax.named_scope("output"):
        act, branch[0] = tie(act, branch[0])
        sum_split = split_matmul(act, down_w, False, 8)
    with jax.named_scope("mixed_grad"):
        branch = gather_last(branch)
        branch, sum_split = tie_lists(branch, sum_split)
        mixed_grad = run_back(branch, out_w, min(wide, 256))
        sum_first = scatter_first(tuple(sum_split))
    query_back, key_back, value_back, gain_grads, row_sums = run_attend_backward(
        mixed_grad, lin, kept, inv_qk, gains, angles, *attention
    )

    with jax.named_scope("qk_back"):
        *sum_first, row_sums = tie(*sum_first, row_sums)
        sum_first = tuple(sum_first)
        means = (sum_rows(jnp.stack([row_sums[0], row_sums[8]], axis=0)) / width).T
    with jax.named_scope("w_out_grad"):
        out_total = run_out_grad(mixed, branch)
        if not heads_spread:
            spread = jnp.zeros((width, width), BF16)
            for i, head in enumerate(head_ids):
                spread = lax.dynamic_update_slice_in_dim(
                    spread, out_total[i * head_size : (i + 1) * head_size], head * head_size, 0
                )
            out_total = spread
    with jax.named_scope("qk_back"):
        passed = scatter_pass(sum_first)
        *passed, means, out_total, gate_up_part = tie(*passed, means, out_total, gate_up_part)
        out_part = to_owners(out_total)
        arrived = scatter_second(tuple(passed))
        qkv_grad = run_finish((query_back, key_back, value_back), lin, gains, inv_qk, means, rows_here)
    with jax.named_scope("output"):
        expert_sum = scatter_sum(sum_first, arrived)
        output_low = ((residual + expert_sum) * live_own).astype(BF16)
    with jax.named_scope("normed_grad"):
        normed_split = split_matmul(qkv_grad, qkv_w, True, 11)
        *normed_split, output_low, qkv_grad = tie(*normed_split, output_low, qkv_grad)
        normed_first = scatter_first(tuple(normed_split))
    with jax.named_scope("w_qkv_grad"):
        qkv_total = run_weight_grad(normed, qkv_grad, 4)
    with jax.named_scope("normed_grad"):
        passed = scatter_pass(normed_first)
        *passed, qkv_total, out_part = tie(*passed, qkv_total, out_part)
        qkv_part = to_owners(qkv_total)
        arrived = scatter_second(tuple(passed))
        normed_grad = scatter_sum(normed_first, arrived)
        input_part, gain_in_grad = norm_back(normed_grad, unit_in, inv_in, gain_in)
        input_low = (resid_grad + input_part).astype(BF16)
    with jax.named_scope("input_grad"):
        input_parts = home_planes(input_low)

    if fast:
        with jax.named_scope("plane_gathers"):
            wide_first = gather_first(jnp.concatenate([gate_up_part, down_part, out_part], axis=0))
            wide_first, (input_parts, output_low) = tie_lists(wide_first, (input_parts, output_low))
            wide_last = gather_last(wide_first)
    with jax.named_scope("output"):
        output_parts = home_planes(output_low)
    with jax.named_scope("small_grads"):
        router_grad = dot(logit_grad, middle_own)

        def spread_heads(which):
            by_head = gain_grads[8 * which].reshape(heads, 1, head_size) * pick[:, :, None]
            return jnp.sum(by_head, axis=0).reshape(1, width)

        small_grads = jnp.concatenate(
            [gain_in_grad[None], spread_heads(0), spread_heads(1), gain_mid_grad[None], router_grad], axis=0
        )
        by_owner = small_grads.reshape(small_grads.shape[0], shards, shard_rows).transpose(1, 0, 2)
        small_sum = sum_chips(jnp.sum(exchange(by_owner, "shard"), axis=0))
        small_sum = small_sum + swap(small_sum, "core", 1)

    def everywhere(part):
        return lax.all_gather(part, ("chip", "core"), axis=0, tiled=False).reshape((chips, 2) + part.shape)

    def plane_parts(pieces):
        own = list(pieces)
        if len(own) != chips:
            own = own[:1] + [jnp.concatenate(own[i : i + 2], axis=0) for i in range(1, len(own), 2)]
        return own + [swap(v, "core", 1) for v in own]

    def shapes(count, *shape):
        return [jax.ShapeDtypeStruct(shape, F32)] * count

    if fast:
        with jax.named_scope("plane_gathers"):
            wide_last, (input_parts, small_sum) = tie_lists(wide_last, (input_parts, small_sum))
            qkv_first = gather_first(qkv_part)
            wide_parts = plane_parts(wide_last)
        input_grad = home_chips(input_parts)
        with jax.named_scope("w_down_grad"):
            (w_down_grad,) = place(
                functools.partial(place_rows, chips), where, wide_parts,
                (((own_hidden, width), lambda i, where: (half_rows // own_hidden + i, 0)),),
                shapes(1, experts, shard_hidden, width),
                ((1, shard_hidden, width), lambda i, where: (i, 0, 0)),
                (experts,), "place_down",
            )
        with jax.named_scope("w_out_grad"):
            out_at = half_rows + experts * own_hidden
            (w_out_grad,) = place(
                functools.partial(place_rows, chips), where, wide_parts,
                (((head_size // 2, width // 4), lambda i, where: (out_at // (head_size // 2), i)),),
                shapes(1, 1, shard_rows, width),
                ((1, shard_rows, width // 4), lambda i, where: (0, 0, i)),
                (4,), "place_out",
            )
            w_out_grad = w_out_grad.reshape(shard_rows, width)
        with jax.named_scope("w_gate_up_grad"):
            columns = jnp.concatenate([wanted + 2 * own_hidden * ((chip ^ step) - chip) for step in range(chips)])
            order = (columns[:, None] == jnp.arange(hidden, dtype=jnp.int32)[None, :]).astype(BF16)
            tile = parts * own_hidden
            w_gate_grad, w_up_grad = place(
                functools.partial(place_hidden, chips), where, wide_parts,
                (
                    ((half_rows, tile), lambda i, where: (0, i)),
                    ((half_rows, tile), lambda i, where: (0, experts + i)),
                ),
                shapes(2, experts, 2, half_rows, hidden),
                ((1, 2, half_rows, hidden), lambda i, where: (i, 0, 0, 0)),
                (experts,), "place_gate_up", (order,),
            )
            w_gate_grad = w_gate_grad.reshape(experts, shard_rows, hidden)
            w_up_grad = w_up_grad.reshape(experts, shard_rows, hidden)
        with jax.named_scope("w_qkv_grad"):
            tile = 64

            qkv_first, (w_down_grad, w_out_grad, w_gate_grad, w_up_grad) = tie_lists(
                qkv_first, (w_down_grad, w_out_grad, w_gate_grad, w_up_grad)
            )
            output = home_chips(output_parts)
            qkv_parts, (input_grad, output) = tie_lists(plane_parts(gather_last(qkv_first)), (input_grad, output))
            w_query_grad, w_key_grad, w_value_grad = (
                v.reshape(shard_rows, width)
                for v in place(
                    functools.partial(place_heads, chips, heads, head_size), where, qkv_parts,
                    (((tile, 3 * wide), lambda i, where: (i, 0)),),
                    shapes(3, 2, half_rows, width),
                    ((2, tile, width), lambda i, where: (0, i, 0)),
                    (half_rows // tile,), "place_heads",
                )
            )
    else:
        input_grad, output = home_chips(input_parts), home_chips(output_parts)
        spread = everywhere(down_part).reshape(chips, 2, experts, own_hidden, width)
        w_down_grad = spread.transpose(2, 0, 1, 3, 4).reshape(experts, shard_hidden, width).astype(F32)
        spread = everywhere(gate_up_part).reshape(chips, 2, half_rows, 2, experts, shards, 2 * own_hidden)
        spread = spread.transpose(3, 4, 1, 2, 5, 0, 6).reshape(2, experts, shard_rows, hidden).astype(F32)
        w_gate_grad, w_up_grad = spread[0], spread[1]
        if heads_spread:
            w_out_grad = everywhere(out_part).reshape(shard_rows, width).astype(F32)
        else:
            spread = lax.psum(out_part.astype(F32), "chip")
            w_out_grad = lax.all_gather(spread, "core", axis=0, tiled=True)

        def heads_back(part, count):
            spread = everywhere(part).reshape(chips, 2, half_rows, count, heads, head_size)
            return spread.transpose(3, 1, 2, 4, 0, 5).reshape(count, shard_rows, width).astype(F32)

        w_query_grad, w_key_grad, w_value_grad = heads_back(qkv_part, 3)
    return (
        output,
        input_grad,
        small_sum[0],
        w_query_grad,
        w_key_grad,
        w_value_grad,
        small_sum[1],
        small_sum[2],
        w_out_grad,
        small_sum[3],
        small_sum[4:].T,
        w_gate_grad,
        w_up_grad,
        w_down_grad,
    )


def solution(mesh):
    reps, shards = mesh.devices.shape
    split = Mesh(mesh.devices.reshape(reps // 2, 2, shards), ("chip", "core", "shard"))
    rows = P(("chip", "core", "shard"), None)
    first, second = P("shard", None), P(None, "shard", None)
    gain = P("shard")
    in_specs = (
        rows, rows, P(("chip", "core"), None), rows, gain, first, first, first, gain, gain, first, gain, first,
        second, second, second,
    )
    out_specs = (rows, rows, gain, first, first, first, gain, gain, first, gain, first, second, second, second)
    return jax.shard_map(body, mesh=split, in_specs=in_specs, out_specs=out_specs, check_vma=False)
```
